256 devices in a mesh: chord: 8 (over y, x_lo), span: 32 (over x_hi, z, core).
Axes of the slice: x: 4 (x_hi: 2, x_lo: 2; x = x_hi * 2 + x_lo), y: 4, z: 8, core: 2. Of those that a mesh axis runs over, the one named last changes fastest.
Arguments:
- velocity: float32 [3, 8, 256, 8192], P(None, None, 'chord', 'span'), may hold values from -6 to 6
- stress: float32 [6, 8, 256, 8192], P(None, None, 'chord', 'span'), may hold values from -6 to 6
- material: int32 [8, 256, 8192], P(None, 'chord', 'span'), may hold values from 0 to 3
- moduli: float32 [4, 10], replicated, may hold values from 0.2 to 0.8
- drive: float32 [1024, 128], P(('chord', 'span')), may hold values from -6 to 6
- owner: int32 [1024, 1], replicated, may hold values from 0 to 255; in each aligned block of 1024 rows (0 to 1023, 1024 to 2047, ...) at most 16 rows name the same one
- cells: int32 [1024, 64], replicated, may hold values from 0 to 8191, as said below
Outputs:
- velocity_out: float32 [3, 8, 256, 8192], P(None, None, 'chord', 'span')
- stress_out: float32 [6, 8, 256, 8192], P(None, None, 'chord', 'span')
- records: float32 [1024, 128], P(('chord', 'span'))
The draws below stay inside these ranges and needn't reach their ends.
Inputs may be any that keep to these rules, and one draw needn't show every extreme that they name: `owner`: every device owns at least one patch and none owns more than 16; some device owns exactly 16. The cells of one patch form a square of 8 x 8 cells inside its owner's tile; cell q lies q // 8 rows and q % 8 columns from cell 0.
All inputs are finite; a program needn't handle non-finite values.
Results may differ from the reference program's by a relative error of at most 0.0001.
Values sent between devices are 32-bit elements; how exact they have to be, the bound alone decides.
A program may use at most 64 MiB of HBM per device.

```python
import math
import jax
import jax.numpy as jnp
import numpy as np
from jax import lax

CX = 32
CY = 256
NZ = 8
STEPS = 2
MATS = 4
PSIDE = 8
PCELLS = 64
OWN_MOST = 16
NX = 256
NY = 8192
PATCHES = 1024
N_SPAN = 32
DEVICES = 256


def draw_cells(key, part):
    key = jax.random.fold_in(key, 7)
    first_key, second_key, third_key, fourth_key = jax.random.split(key, 4)
    anchor_x = jax.random.randint(first_key, (PATCHES,), 0, CX - PSIDE + 1)
    anchor_y = jax.random.randint(second_key, (PATCHES,), 0, CY - PSIDE + 1)
    far_patch = jax.random.randint(third_key, (), 0, PATCHES)
    near_patch = (far_patch + 1 + jax.random.randint(fourth_key, (), 0, PATCHES - 1)) % PATCHES
    anchor_x = anchor_x.at[far_patch].set(CX - PSIDE).at[near_patch].set(0)
    anchor_y = anchor_y.at[far_patch].set(CY - PSIDE).at[near_patch].set(0)
    offsets = jnp.arange(PSIDE * PSIDE, dtype=jnp.int32)
    local_x = anchor_x[:, None] + offsets[None, :] // PSIDE
    local_y = anchor_y[:, None] + offsets[None, :] % PSIDE
    return (local_x * CY + local_y).astype(jnp.int32)


def plant(entries, own_key, smallest, largest):
    spot = [jax.random.randint(jax.random.fold_in(own_key, axis), (), 0, length) for axis, length in enumerate(entries.shape)]
    main_axis = entries.shape.index(max(entries.shape))
    neighbour = spot[:main_axis] + [(spot[main_axis] + 1) % entries.shape[main_axis]] + spot[main_axis + 1:]
    return entries.at[tuple(spot)].set(smallest).at[tuple(neighbour)].set(largest)


def steps_of(key, dims, cuts, low, largest):
    def one(position, shards_of):
        heights = jax.random.uniform(jax.random.fold_in(jax.random.fold_in(key, 6), position), (shards_of,), jnp.float32, low / len(cuts), largest / len(cuts))
        return jnp.repeat(jnp.exp(heights), dims[position] // shards_of).reshape((-1,) + (1,) * (len(dims) - position - 1))

    level = one(*cuts[0])
    for cut in cuts[1:]:
        level = level * one(*cut)
    return level


def assign_block(stream_key, own, number, rows, count, top, most, lean):
    ranking = jax.random.permutation(stream_key, count)
    heavy_load, usual = load_shares(count, rows * top, most, lean, True), load_shares(count, rows * top, most, lean, False)
    places = jnp.arange(count)

    def named(lengths, rotation):
        used = int((lengths > 0).sum())
        fixed = max(1, used // 4)
        passed = fixed + (places - fixed + rotation * (used - fixed)) % max(1, count - fixed)
        return jnp.zeros((count,), jnp.int32).at[ranking[jnp.where(places < fixed, places, passed)]].set(jnp.asarray(lengths, jnp.int32))

    lengths = jnp.where(number % 4 == 0, named(heavy_load, number // 4), named(usual, number - number // 4 - 1))
    mixed = jax.random.permutation(jax.random.fold_in(own, 3), count)
    source_of, receiver = mixed[0:count // 2 * 2:2], mixed[1:count // 2 * 2:2]
    margin = jnp.minimum(lengths[source_of] - 1, most - lengths[receiver]) // 2
    margin = jnp.where((source_of == ranking[0]) | (receiver == ranking[0]) | (lengths[receiver] == 0), 0, jnp.maximum(margin, 0))
    passed = jax.random.randint(jax.random.fold_in(own, 4), (count // 2,), 0, 1 << 20) % (margin + 1)
    lengths = lengths.at[source_of].add(-passed).at[receiver].add(passed)
    labels = jnp.searchsorted(jnp.cumsum(lengths), jnp.arange(rows * top), side="right").astype(jnp.int32)
    grid = labels.reshape(top, rows).T
    grid = grid[jax.random.permutation(jax.random.fold_in(own, 1), rows)]
    rotation = jax.random.randint(jax.random.fold_in(own, 2), (rows, 1), 0, top)
    return jnp.take_along_axis(grid, (jnp.arange(top)[None, :] + rotation) % top, axis=1)


def load_shares(amount, total, reach, skew, full):
    weights = [(1 << 20) // math.isqrt(grade ** skew) + 1 for grade in range(1, amount + 1)]
    largest = reach if full else min(reach, max(-(-total // amount), total * weights[0] // sum(weights)))
    least = 1 if total - largest >= amount - 1 else 0
    given, rest = [largest] + [least] * (amount - 1), total - largest - least * (amount - 1)
    while rest > 0:
        free = [i for i in range(1, amount) if given[i] < largest] or [i for i in range(1, amount) if given[i] < reach]
        pool, remaining = sum([weights[i] for i in free]), rest
        for i in free:
            extra = min(reach - given[i], max(1, remaining * weights[i] // pool), rest)
            given[i] = given[i] + extra
            rest = rest - extra
    return np.array(given)


def bell_draw(own_key, extent, scale, bound, cuts=(), kind=jnp.bfloat16):
    entries = jax.random.normal(own_key, extent, jnp.float32) * scale
    if len(cuts) > 0:
        entries = steps_of(own_key, extent, cuts, -0.22, 0.18) * entries
    return jnp.clip(entries, min=-bound, max=bound).astype(kind)


def setup_inputs(seed: int = 0) -> dict:
    splits = jax.random.split(jax.random.key(seed), 8)
    velocity = bell_draw(splits[0], (3, NZ, NX, NY), 1.0, 6.0, ((2, 8), (3, 32)), jnp.float32)
    stress = bell_draw(splits[1], (6, NZ, NX, NY), 1.0, 6.0, ((2, 8), (3, 32)), jnp.float32)
    material = plant(jax.random.randint(splits[2], (NZ, NX, NY), 0, MATS), jax.random.fold_in(splits[2], 1), 0, MATS - 1).astype(jnp.int32)
    moduli = jnp.clip(jax.random.uniform(splits[3], (MATS, 10), jnp.float32, 0.2, 0.8), 0.2, 0.8)
    drive = bell_draw(splits[4], (PATCHES, STEPS * PCELLS), 1.0, 6.0, ((0, 256),), jnp.float32)
    owner_keys = jax.random.split(jax.random.fold_in(splits[5], 1), PATCHES // PATCHES)
    owner_turns = jax.random.permutation(jax.random.fold_in(splits[5], 3), PATCHES // PATCHES)
    owner = jax.vmap(lambda own, number: assign_block(jax.random.fold_in(splits[5], 2), own, number, PATCHES, DEVICES, 1, OWN_MOST, 2))(owner_keys, owner_turns).reshape((PATCHES, 1))
    cells = draw_cells(jax.random.fold_in(splits[7], 71), 0)
    return dict(velocity=velocity, stress=stress, material=material, moduli=moduli, drive=drive, owner=owner, cells=cells)


TIME_STEP = 0.5


def forward_diff(values, along):
    shifted = lax.slice_in_dim(values, 1, values.shape[along], axis=along)
    widths = [(0, 0), (0, 0), (0, 0)]
    widths[along] = (0, 1)
    return jnp.pad(shifted, widths) - values


def backward_diff(values, along):
    shifted = lax.slice_in_dim(values, 0, values.shape[along] - 1, axis=along)
    widths = [(0, 0), (0, 0), (0, 0)]
    widths[along] = (1, 0)
    return values - jnp.pad(shifted, widths)


def reference(velocity, stress, material, moduli, drive, owner, cells):
    coeffs = [moduli[:, column][material] for column in range(10)]
    owners = owner[:, 0]
    glob_x = ((owners // N_SPAN) * CX)[:, None] + cells // CY
    glob_y = ((owners % N_SPAN) * CY)[:, None] + cells % CY
    vel_x, vel_y, vel_z = velocity[0], velocity[1], velocity[2]
    sig_xx, sig_yy, sig_zz = stress[0], stress[1], stress[2]
    sig_yz, sig_xz, sig_xy = stress[3], stress[4], stress[5]
    records = []
    for step in range(STEPS):
        strain_xx = backward_diff(vel_x, 1)
        strain_yy = backward_diff(vel_y, 2)
        strain_zz = backward_diff(vel_z, 0)
        shear_yz = forward_diff(vel_y, 0) + forward_diff(vel_z, 2)
        shear_xz = forward_diff(vel_x, 0) + forward_diff(vel_z, 1)
        shear_xy = forward_diff(vel_x, 2) + forward_diff(vel_y, 1)
        sig_xx = sig_xx + TIME_STEP * (coeffs[0] * strain_xx + coeffs[1] * strain_yy + coeffs[2] * strain_zz)
        sig_yy = sig_yy + TIME_STEP * (coeffs[1] * strain_xx + coeffs[3] * strain_yy + coeffs[4] * strain_zz)
        sig_zz = sig_zz + TIME_STEP * (coeffs[2] * strain_xx + coeffs[4] * strain_yy + coeffs[5] * strain_zz)
        sig_yz = sig_yz + TIME_STEP * coeffs[6] * shear_yz
        sig_xz = sig_xz + TIME_STEP * coeffs[7] * shear_xz
        sig_xy = sig_xy + TIME_STEP * coeffs[8] * shear_xy
        plane = jnp.zeros((NX, NY), jnp.float32).at[glob_x, glob_y].add(drive[:, step * PCELLS:(step + 1) * PCELLS])
        force = jnp.zeros((NZ, NX, NY), jnp.float32).at[NZ - 1].set(plane)
        scale = TIME_STEP * coeffs[9]
        accel_x = forward_diff(sig_xx, 1) + backward_diff(sig_xy, 2) + backward_diff(sig_xz, 0)
        accel_y = backward_diff(sig_xy, 1) + forward_diff(sig_yy, 2) + backward_diff(sig_yz, 0)
        accel_z = backward_diff(sig_xz, 1) + backward_diff(sig_yz, 2) + forward_diff(sig_zz, 0) + force
        vel_x = vel_x + scale * accel_x
        vel_y = vel_y + scale * accel_y
        vel_z = vel_z + scale * accel_z
        records.append(vel_z[NZ - 1][glob_x, glob_y])
    velocity_out = jnp.stack([vel_x, vel_y, vel_z])
    stress_out = jnp.stack([sig_xx, sig_yy, sig_zz, sig_yz, sig_xz, sig_xy])
    return velocity_out, stress_out, jnp.concatenate(records, axis=1)
```

```python
import functools

import jax
import jax.numpy as jnp
from jax import lax
from jax.experimental import pallas as pl
from jax.experimental.pallas import tpu as pltpu
from jax.sharding import PartitionSpec as P

MESH = pl.DeviceIdType.MESH
F32 = jnp.float32
BF16 = jnp.bfloat16
DT = 0.5
SLOTS = 16
LANES = 128
C11, C12, C13, C22, C23, C33, C44, C55, C66, BUOY = range(10)
XX, YY, ZZ, YZ, XZ, XY = range(6)


def iota(shape, dim):
    return lax.broadcasted_iota(jnp.int32, shape, dim)


def fiota(shape, dim):
    return iota(shape, dim).astype(F32)


def split3(x):
    a = x.astype(BF16)
    rest = x - a.astype(F32)
    b = rest.astype(BF16)
    return a, b, (rest - b.astype(F32)).astype(BF16)


def dot(a, b, contract=((1,), (0,))):
    return lax.dot_general(a, b, (contract, ((), ())), preferred_element_type=F32)


def kernel(
    n_chord,
    n_span,
    vel_in,
    str_in,
    mat_in,
    moduli,
    drive,
    owner,
    cells,
    vel_out,
    str_out,
    rec_out,
    v,
    s,
    mat,
    coef,
    onehot_y,
    slot_x,
    slot_y,
    plane,
    taken,
    taken_t,
    routed1,
    rows1,
    send2,
    routed2,
    rec_send,
    rec_rows,
    rec_back,
    rec_got,
    to_dn,
    to_up,
    to_rt,
    to_lt,
    from_up,
    from_dn,
    from_lt,
    from_rt,
    corner_up,
    corner_dn,
    vto_dn,
    vto_up,
    vto_rt,
    vto_lt,
    vfrom_up,
    vfrom_dn,
    vfrom_lt,
    vfrom_rt,
    vcorner_up,
    vcorner_dn,
    tto_dn,
    tto_up,
    tto_rt,
    tto_lt,
    tfrom_up,
    tfrom_dn,
    tfrom_lt,
    tfrom_rt,
    halo_row,
    halo_col,
    hcoef_row,
    hcoef_col,
    load_sem,
    out_sem,
    group_send,
    group_recv,
    edge_send,
    edge_recv,
):
    c = lax.axis_index("chord")
    sp = lax.axis_index("span")
    depth = vel_in.shape[1]
    size_x = vel_in.shape[2]
    size_y = vel_in.shape[3]
    half = size_y - LANES
    has_up, has_dn = c > 0, c < n_chord - 1
    has_lt, has_rt = sp > 0, sp < n_span - 1
    diag_up = jnp.logical_and(has_up, has_rt)
    diag_dn = jnp.logical_and(has_dn, has_lt)

    loads = [
        pltpu.make_async_copy(vel_in, v.at[:, pl.ds(1, depth)], load_sem.at[0]),
        pltpu.make_async_copy(str_in, s.at[:, pl.ds(1, depth)], load_sem.at[1]),
        pltpu.make_async_copy(mat_in, mat, load_sem.at[2]),
    ]
    for load in loads:
        load.start()

    barrier = pltpu.get_barrier_semaphore()

    def greet(to_c, to_s):
        pl.semaphore_signal(barrier, inc=1, device_id=(to_c, to_s), device_id_type=MESH)

    def greet_span(i, _):
        greet(c, lax.rem(sp + i, n_span))
        return 0

    def greet_chord(i, _):
        greet(lax.rem(c + i, n_chord), sp)
        return 0

    lax.fori_loop(1, n_span, greet_span, 0)
    lax.fori_loop(1, n_chord, greet_chord, 0)

    @pl.when(diag_up)
    def _():
        greet(c - 1, sp + 1)

    @pl.when(diag_dn)
    def _():
        greet(c + 1, sp - 1)

    blank = jnp.zeros((size_x, size_y), F32)
    for comp in range(3):
        v[comp, 0] = blank
        v[comp, depth + 1] = blank
    for comp in (ZZ, YZ, XZ):
        s[comp, 0] = blank
        s[comp, depth + 1] = blank

    @pl.when(jnp.logical_not(has_up))
    def _():
        for ref in (from_up, vfrom_up, tfrom_up):
            ref[...] = jnp.zeros_like(ref)

    @pl.when(jnp.logical_not(has_dn))
    def _():
        for ref in (from_dn, vfrom_dn, tfrom_dn):
            ref[...] = jnp.zeros_like(ref)

    @pl.when(jnp.logical_not(has_lt))
    def _():
        for ref in (from_lt, vfrom_lt, tfrom_lt):
            ref[...] = jnp.zeros_like(ref)

    @pl.when(jnp.logical_not(has_rt))
    def _():
        for ref in (from_rt, vfrom_rt, tfrom_rt):
            ref[...] = jnp.zeros_like(ref)

    @pl.when(jnp.logical_not(diag_up))
    def _():
        for ref in (corner_up, vcorner_up):
            ref[...] = jnp.zeros_like(ref)

    @pl.when(jnp.logical_not(diag_dn))
    def _():
        for ref in (corner_dn, vcorner_dn):
            ref[...] = jnp.zeros_like(ref)

    pl.semaphore_wait(
        barrier,
        n_span + n_chord - 2 + diag_up.astype(jnp.int32) + diag_dn.astype(jnp.int32),
    )

    def to_span(i, source, target, sem):
        to_s = lax.rem(sp + i, n_span)
        return pltpu.make_async_remote_copy(
            src_ref=source(to_s),
            dst_ref=target.at[sp],
            send_sem=group_send.at[sem],
            recv_sem=group_recv.at[sem],
            device_id=(c, to_s),
            device_id_type=MESH,
        )

    def to_chord(i, source, target, sem):
        to_c = lax.rem(c + i, n_chord)
        return pltpu.make_async_remote_copy(
            src_ref=source(to_c),
            dst_ref=target.at[pl.ds(pl.multiple_of(c * SLOTS, SLOTS), SLOTS)],
            send_sem=group_send.at[sem],
            recv_sem=group_recv.at[sem],
            device_id=(to_c, sp),
            device_id_type=MESH,
        )

    def start_all(count, make):
        def body(i, _):
            make(i).start()
            return 0

        lax.fori_loop(1, count, body, 0)

    def wait_all(ref, count, sems, sem):
        part = ref.at[pl.ds(0, count)]
        pltpu.make_async_copy(part, part, sems.at[sem]).wait()

    start_all(n_span, lambda i: to_span(i, lambda to_s: drive, routed1, 0))
    routed1[sp] = drive[...]

    def edge(source, target, to, index):
        return pltpu.make_async_remote_copy(
            src_ref=source,
            dst_ref=target,
            send_sem=edge_send.at[index],
            recv_sem=edge_recv.at[index],
            device_id=to,
            device_id_type=MESH,
        )

    up, dn, lt, rt = (c - 1, sp), (c + 1, sp), (c, sp - 1), (c, sp + 1)

    def exchange(first, up_src, dn_src, lt_src, rt_src, up_dst, dn_dst, lt_dst, rt_dst, corners):
        moves = [
            (has_up, has_dn, edge(up_src, dn_dst, up, first)),
            (has_dn, has_up, edge(dn_src, up_dst, dn, first + 1)),
            (has_lt, has_rt, edge(lt_src, rt_dst, lt, first + 2)),
            (has_rt, has_lt, edge(rt_src, lt_dst, rt, first + 3)),
        ]
        if corners is not None:
            corner_from_dn, corner_from_up = corners
            moves.append(
                (
                    diag_up,
                    diag_dn,
                    edge(
                        up_src.at[pl.ds(depth, depth), pl.ds(half, LANES)],
                        corner_from_dn,
                        (c - 1, sp + 1),
                        first + 4,
                    ),
                )
            )
            moves.append(
                (
                    diag_dn,
                    diag_up,
                    edge(
                        dn_src.at[pl.ds(0, depth), pl.ds(0, LANES)],
                        corner_from_up,
                        (c + 1, sp - 1),
                        first + 5,
                    ),
                )
            )

        def start():
            for goes, _, copy in moves:
                pl.when(goes)(copy.start)

        def arrive():
            for _, comes, copy in moves:
                pl.when(comes)(copy.wait_recv)

        def leave():
            for goes, _, copy in moves:
                pl.when(goes)(copy.wait_send)

        return start, arrive, leave

    start1, arrive1, leave1 = exchange(
        0, to_up, to_dn, to_lt, to_rt, from_up, from_dn, from_lt, from_rt, (corner_dn, corner_up)
    )
    start2, arrive2, leave2 = exchange(
        6, vto_up, vto_dn, vto_lt, vto_rt, vfrom_up, vfrom_dn, vfrom_lt, vfrom_rt, (vcorner_dn, vcorner_up)
    )
    start3, arrive3, leave3 = exchange(
        12, tto_up, tto_dn, tto_lt, tto_rt, tfrom_up, tfrom_dn, tfrom_lt, tfrom_rt, None
    )

    def pack_rows(ref, row, fields):
        def body(z, _):
            for k, read in enumerate(fields):
                ref[pl.ds(k * depth + z, 1), :] = read(z, row)
            return 0

        lax.fori_loop(0, depth, body, 0)

    lane = iota((size_x, LANES), 1)
    row = iota((size_x, size_y), 0)

    def pack_cols(ref, column, fields):
        base = 0 if column == 0 else half
        at = column - base

        def body(z, acc):
            for k, read in enumerate(fields):
                tile = read(z, base)
                to = k * depth + z
                moved = pltpu.roll(tile, lax.rem(to + (LANES - at), LANES), 1)
                acc = jnp.where(lane == to, moved, acc)
            return acc

        ref[...] = lax.fori_loop(0, depth, body, jnp.zeros((size_x, LANES), F32))

    def row_of(ref, comp):
        return lambda z, r: ref[comp, z + 1, r : r + 1, :]

    def col_of(ref, comp):
        return lambda z, base: ref[comp, z + 1, :, base : base + LANES]

    def mat_row(z, r):
        return mat[z, r : r + 1, :].astype(F32)

    def mat_col(z, base):
        return mat[z, :, base : base + LANES].astype(F32)

    v_rows = [row_of(v, k) for k in range(3)]
    v_cols = [col_of(v, k) for k in range(3)]

    for load in loads:
        load.wait()
    pack_rows(to_dn, size_x - 1, v_rows + [row_of(s, XY), row_of(s, XZ), mat_row])
    pack_rows(to_up, 0, v_rows + [row_of(s, XX), mat_row])
    pack_cols(to_rt, size_y - 1, v_cols + [col_of(s, XY), col_of(s, YZ), mat_col])
    pack_cols(to_lt, 0, v_cols + [col_of(s, YY), mat_col])
    start1()

    n_block = owner.shape[0]
    earlier = (iota((LANES, LANES), 0) < iota((LANES, LANES), 1)).astype(BF16)
    wanted = iota((n_chord, LANES), 0) * n_span + sp
    before = jnp.zeros((n_chord, LANES), F32)
    here = jnp.zeros((n_chord, LANES), F32)
    for a in range(n_block):
        same = (owner[a : a + 1, :] == wanted).astype(F32)
        before = before + same * (a < c).astype(F32)
        here = here + same * (a == c).astype(F32)
    rank = jnp.sum(before, axis=1, keepdims=True) + dot(here.astype(BF16), earlier)
    rank = jnp.where(here > 0.5, rank, -1.0)
    slot_ids = fiota((SLOTS, LANES), 0)
    for k in range(n_chord):
        taken[k * SLOTS : (k + 1) * SLOTS, :] = (rank[k : k + 1, :] == slot_ids).astype(F32)
    taken_t[...] = jnp.transpose(taken[...])

    mine = (owner[...] == c * n_span + sp).astype(F32)
    my_rank = dot(mine.astype(BF16), earlier)
    total = jnp.broadcast_to(jnp.sum(mine, axis=1, keepdims=True), (n_block, LANES))
    block_ids = iota((n_block, LANES), 0)
    for a in range(n_block - 1):
        my_rank = my_rank + jnp.where(block_ids > a, total[a : a + 1, :], 0.0)
    my_rank = jnp.where(mine > 0.5, my_rank, -1.0)
    first_x = jnp.zeros((SLOTS, LANES), F32)
    first_y = jnp.zeros((SLOTS, LANES), F32)
    shift = size_y.bit_length() - 1
    for a in range(n_block):
        anchor = cells[0:1, a * LANES : (a + 1) * LANES]
        hit = my_rank[a : a + 1, :] == slot_ids
        first_x = first_x + jnp.where(hit, (anchor >> shift).astype(F32), 0.0)
        first_y = first_y + jnp.where(hit, (anchor & (size_y - 1)).astype(F32), 0.0)
    first_x = jnp.sum(first_x, axis=1, keepdims=True)
    first_y = jnp.sum(first_y, axis=1, keepdims=True)
    low = iota((8, LANES), 1) < 64
    cell_id = iota((8, LANES), 1) & 63
    slot_x[...] = jnp.where(low, first_x[0:8], first_x[8:16]) + (cell_id >> 3).astype(F32)
    slot_y[...] = jnp.where(low, first_y[0:8], first_y[8:16]) + (cell_id & 7).astype(F32)
    y_ids = fiota((size_y, LANES), 0)
    for t in range(8):
        onehot_y[:, t * LANES : (t + 1) * LANES] = (
            (slot_y[t : t + 1, :] == y_ids).astype(F32).astype(BF16)
        )
    x_ids = fiota((size_x, LANES), 0)

    def table(kind, index):
        out = jnp.full(kind.shape, DT * moduli[0, index], F32)
        for m in range(1, 4):
            out = jnp.where(kind == m, DT * moduli[m, index], out)
        return out

    def coef_layer(z, _):
        kind = mat[z]
        for k in range(10):
            coef[k, z] = table(kind, k)
        return 0

    lax.fori_loop(0, depth, coef_layer, 0)

    wait_all(routed1, n_span - 1, group_recv, 0)
    per = drive.shape[0]
    for i in range(n_span):
        rows1[i * per : (i + 1) * per, :] = routed1[i]
    pick = taken[...].astype(BF16)
    send2[...] = sum(dot(pick, part) for part in split3(rows1[...]))
    own = pl.ds(pl.multiple_of(c * SLOTS, SLOTS), SLOTS)

    def for_chord(ref):
        return lambda to_c: ref.at[pl.ds(pl.multiple_of(to_c * SLOTS, SLOTS), SLOTS)]

    start_all(n_chord, lambda i: to_chord(i, for_chord(send2), routed2, 1))
    routed2[own, :] = send2[own, :]

    def along_x(field, by, edge_row):
        if by > 0:
            return jnp.where(row == 0, edge_row, pltpu.roll(field, 1, 0))
        return jnp.where(row == size_x - 1, edge_row, pltpu.roll(field, size_x - 1, 0))

    def along_y(field, by, edge_col):
        if by > 0:
            moved = pltpu.roll(field, 1, 1)
            head = jnp.where(lane == 0, edge_col, moved[:, :LANES])
            return jnp.concatenate([head, moved[:, LANES:]], axis=1)
        moved = pltpu.roll(field, size_y - 1, 1)
        tail = jnp.where(lane == LANES - 1, edge_col, moved[:, half:])
        return jnp.concatenate([moved[:, :half], tail], axis=1)

    def first_lane(ref, field, z):
        return pltpu.roll(ref[...], lax.rem(2 * LANES - (field * depth + z), LANES), 1)

    def last_lane(ref, field, z):
        return pltpu.roll(ref[...], lax.rem(2 * LANES - 1 - (field * depth + z), LANES), 1)

    def stress_layer(z, up_ref, dn_ref, lt_ref, rt_ref):
        vx, vy, vz = v[0, z + 1], v[1, z + 1], v[2, z + 1]
        xx = vx - along_x(vx, 1, up_ref[pl.ds(z, 1), :])
        yy = vy - along_y(vy, 1, first_lane(lt_ref, 1, z))
        zz = vz - v[2, z]
        yz = (v[1, z + 2] - vy) + (along_y(vz, -1, last_lane(rt_ref, 2, z)) - vz)
        xz = (v[0, z + 2] - vx) + (along_x(vz, -1, dn_ref[pl.ds(2 * depth + z, 1), :]) - vz)
        xy = (along_y(vx, -1, last_lane(rt_ref, 0, z)) - vx) + (
            along_x(vy, -1, dn_ref[pl.ds(depth + z, 1), :]) - vy
        )
        s[XX, z + 1] += coef[C11, z] * xx + coef[C12, z] * yy + coef[C13, z] * zz
        s[YY, z + 1] += coef[C12, z] * xx + coef[C22, z] * yy + coef[C23, z] * zz
        s[ZZ, z + 1] += coef[C13, z] * xx + coef[C23, z] * yy + coef[C33, z] * zz
        s[YZ, z + 1] += coef[C44, z] * yz
        s[XZ, z + 1] += coef[C55, z] * xz
        s[XY, z + 1] += coef[C66, z] * xy

    def velocity_layer(z):
        sxx, syy, szz = s[XX, z + 1], s[YY, z + 1], s[ZZ, z + 1]
        syz, sxz, sxy = s[YZ, z + 1], s[XZ, z + 1], s[XY, z + 1]
        ax = (
            (along_x(sxx, -1, halo_row[0, pl.ds(z, 1), :]) - sxx)
            + (sxy - along_y(sxy, 1, first_lane(halo_col.at[1], 0, z)))
            + (sxz - s[XZ, z])
        )
        ay = (
            (sxy - along_x(sxy, 1, halo_row[1, pl.ds(z, 1), :]))
            + (along_y(syy, -1, last_lane(halo_col.at[0], 0, z)) - syy)
            + (syz - s[YZ, z])
        )
        az = (
            (sxz - along_x(sxz, 1, halo_row[2, pl.ds(z, 1), :]))
            + (syz - along_y(syz, 1, first_lane(halo_col.at[2], 0, z)))
            + (s[ZZ, z + 2] - szz)
        )
        b = coef[BUOY, z]
        v[0, z + 1] += b * ax
        v[1, z + 1] += b * ay
        v[2, z + 1] += b * az

    wide = (depth, size_y)
    wide_lane = iota(wide, 1)
    wide_z = iota(wide, 0)

    def below_z(f):
        return jnp.where(wide_z == 0, 0.0, pltpu.roll(f, 1, 0))

    def above_z(f):
        return jnp.where(wide_z == depth - 1, 0.0, pltpu.roll(f, depth - 1, 0))

    def lane_below_z(f):
        return jnp.where(lane == 0, 0.0, pltpu.roll(f, 1, 1))

    def lane_above_z(f):
        return jnp.where(lane == depth - 1, 0.0, pltpu.roll(f, LANES - 1, 1))

    def to_lanes(corner, at):
        col = jnp.broadcast_to(corner[:, at : at + 1], (depth, LANES))
        here = iota((depth, LANES), 0) == iota((depth, LANES), 1)
        return jnp.sum(jnp.where(here, col, 0.0), axis=0, keepdims=True)

    def lanes_of(ref, field):
        if field == 0:
            return ref[...]
        return pltpu.roll(ref[...], LANES - field * depth, 1)

    narrow_row = iota((size_x, LANES), 0)

    def halo_stress(up_ref, dn_ref, lt_ref, rt_ref, cup, cdn, my_up, my_dn, my_lt, my_rt):
        def rows(ref, k):
            return ref[k * depth : (k + 1) * depth, :]

        vx, vy, vz = rows(dn_ref, 0), rows(dn_ref, 1), rows(dn_ref, 2)
        corner = jnp.broadcast_to(cdn[:, LANES - 1 : LANES], wide)
        vy_back = jnp.where(wide_lane == 0, corner, pltpu.roll(vy, 1, 1))
        halo_row[0] += (
            hcoef_row[0] * (vx - rows(my_dn, 0))
            + hcoef_row[1] * (vy - vy_back)
            + hcoef_row[2] * (vz - below_z(vz))
        )
        vx, vy, vz = rows(up_ref, 0), rows(up_ref, 1), rows(up_ref, 2)
        corner = jnp.broadcast_to(cup[:, 0:1], wide)
        vx_next = jnp.where(wide_lane == size_y - 1, corner, pltpu.roll(vx, size_y - 1, 1))
        halo_row[1] += hcoef_row[3] * ((vx_next - vx) + (rows(my_up, 1) - vy))
        halo_row[2] += hcoef_row[4] * ((above_z(vx) - vx) + (rows(my_up, 2) - vz))
        vx, vy, vz = lanes_of(rt_ref, 0), lanes_of(rt_ref, 1), lanes_of(rt_ref, 2)
        vx_back = jnp.where(narrow_row == 0, to_lanes(cup, 0), pltpu.roll(vx, 1, 0))
        halo_col[0] += (
            hcoef_col[0] * (vx - vx_back)
            + hcoef_col[1] * (vy - lanes_of(my_rt, 1))
            + hcoef_col[2] * (vz - lane_below_z(vz))
        )
        vx, vy, vz = lanes_of(lt_ref, 0), lanes_of(lt_ref, 1), lanes_of(lt_ref, 2)
        vy_next = jnp.where(
            narrow_row == size_x - 1, to_lanes(cdn, LANES - 1), pltpu.roll(vy, size_x - 1, 0)
        )
        halo_col[1] += hcoef_col[3] * ((lanes_of(my_lt, 0) - vx) + (vy_next - vy))
        halo_col[2] += hcoef_col[4] * ((lane_above_z(vy) - vy) + (lanes_of(my_lt, 2) - vz))

    arrive1()
    kind = from_dn[4 * depth : 5 * depth, :]
    inside = has_dn.astype(F32)
    for k, index in enumerate((C11, C12, C13)):
        hcoef_row[k] = table(kind, index) * inside
    kind = from_up[5 * depth : 6 * depth, :]
    inside = has_up.astype(F32)
    for k, index in enumerate((C66, C55)):
        hcoef_row[3 + k] = table(kind, index) * inside
    kind = lanes_of(from_rt, 4)
    inside = has_rt.astype(F32)
    for k, index in enumerate((C12, C22, C23)):
        hcoef_col[k] = table(kind, index) * inside
    kind = lanes_of(from_lt, 5)
    inside = has_lt.astype(F32)
    for k, index in enumerate((C66, C44)):
        hcoef_col[3 + k] = table(kind, index) * inside
    halo_row[0] = from_dn[3 * depth : 4 * depth, :]
    halo_row[1] = from_up[3 * depth : 4 * depth, :]
    halo_row[2] = from_up[4 * depth : 5 * depth, :]
    halo_col[0] = lanes_of(from_rt, 3)
    halo_col[1] = lanes_of(from_lt, 3)
    halo_col[2] = lanes_of(from_lt, 4)

    def stress_first(z, _):
        stress_layer(z, from_up, from_dn, from_lt, from_rt)
        return 0

    def velocity_body(z, _):
        velocity_layer(z)
        return 0

    lax.fori_loop(0, depth, stress_first, 0)
    halo_stress(
        from_up, from_dn, from_lt, from_rt, corner_up, corner_dn, to_up, to_dn, to_lt, to_rt
    )
    lax.fori_loop(0, depth, velocity_body, 0)

    pack_rows(vto_dn, size_x - 1, v_rows)
    pack_rows(vto_up, 0, v_rows)
    pack_cols(vto_rt, size_y - 1, v_cols)
    pack_cols(vto_lt, 0, v_cols)
    start2()

    wait_all(routed2, (n_chord - 1) * SLOTS, group_recv, 1)
    rows = routed2[0:SLOTS, :]
    for k in range(1, n_chord):
        rows = rows + routed2[k * SLOTS : (k + 1) * SLOTS, :]
    head, tail = rows[0:8], rows[8:16]
    force = [
        jnp.where(low, head, pltpu.roll(tail, 64, 1)),
        jnp.where(low, pltpu.roll(head, 64, 1), tail),
    ]

    def in_slot(t):
        return slot_x[t : t + 1, :] == x_ids

    for step in range(2):
        wide_force = jnp.concatenate(
            [jnp.where(in_slot(t), force[step][t : t + 1, :], 0.0) for t in range(8)], axis=1
        )
        parts = jnp.concatenate(split3(wide_force), axis=0)
        got = dot(parts, onehot_y[...], ((1,), (1,)))
        plane[step] = got[:size_x] + got[size_x : 2 * size_x] + got[2 * size_x :]

    def add_force(step):
        v[2, depth] += coef[BUOY, depth - 1] * plane[step]

    def sample():
        top = v[2, depth]
        got = dot(jnp.concatenate(split3(top), axis=0), onehot_y[...])
        got = got[:size_x] + got[size_x : 2 * size_x] + got[2 * size_x :]
        out = []
        for t in range(8):
            chosen = jnp.where(in_slot(t), got[:, t * LANES : (t + 1) * LANES], 0.0)
            out.append(jnp.sum(chosen, axis=0, keepdims=True))
        return jnp.concatenate(out, axis=0)

    add_force(0)
    tto_dn[...] = jnp.broadcast_to(v[2, depth, size_x - 1 : size_x, :], (depth, size_y))
    tto_up[...] = jnp.broadcast_to(v[2, depth, 0:1, :], (depth, size_y))
    tto_rt[...] = v[2, depth, :, half:]
    tto_lt[...] = v[2, depth, :, :LANES]
    start3()
    first = sample()

    arrive2()

    def stress_second(z, _):
        stress_layer(z, vfrom_up, vfrom_dn, vfrom_lt, vfrom_rt)
        return 0

    lax.fori_loop(0, depth - 1, stress_second, 0)
    arrive3()
    leave2()
    last = depth - 1
    top_row = 2 * depth + last
    vfrom_up[top_row : top_row + 1, :] = tfrom_up[0:1, :]
    vfrom_dn[top_row : top_row + 1, :] = tfrom_dn[0:1, :]
    vfrom_rt[...] = jnp.where(
        lane == top_row, pltpu.roll(tfrom_rt[...], top_row, 1), vfrom_rt[...]
    )
    vfrom_lt[...] = jnp.where(
        lane == top_row, pltpu.roll(tfrom_lt[...], top_row + 1, 1), vfrom_lt[...]
    )
    vto_up[top_row : top_row + 1, :] = v[2, depth, 0:1, :]
    vto_lt[...] = jnp.where(
        lane == top_row, pltpu.roll(v[2, depth, :, :LANES], top_row, 1), vto_lt[...]
    )
    stress_layer(last, vfrom_up, vfrom_dn, vfrom_lt, vfrom_rt)
    halo_stress(
        vfrom_up,
        vfrom_dn,
        vfrom_lt,
        vfrom_rt,
        vcorner_up,
        vcorner_dn,
        vto_up,
        vto_dn,
        vto_lt,
        vto_rt,
    )
    velocity_layer(last)
    add_force(1)
    second = sample()

    rec_send[0:8, :] = jnp.where(low, first, pltpu.roll(second, 64, 1))
    rec_send[8:16, :] = jnp.where(low, pltpu.roll(first, 64, 1), second)
    start_all(n_chord, lambda i: to_chord(i, lambda to_c: rec_send, rec_rows, 2))
    rec_rows[own, :] = rec_send[...]

    lax.fori_loop(0, depth - 1, velocity_body, 0)
    stores = [
        pltpu.make_async_copy(v.at[:, pl.ds(1, depth)], vel_out, out_sem.at[0]),
        pltpu.make_async_copy(s.at[:, pl.ds(1, depth)], str_out, out_sem.at[1]),
    ]
    for store in stores:
        store.start()

    wait_all(rec_rows, (n_chord - 1) * SLOTS, group_recv, 2)
    pick = taken_t[...].astype(BF16)
    back = sum(dot(pick, part) for part in split3(rec_rows[...]))
    for i in range(n_span):
        rec_back[i] = back[i * per : (i + 1) * per, :]
    start_all(n_span, lambda i: to_span(i, lambda to_s: rec_back.at[to_s], rec_got, 3))
    rec_got[sp] = rec_back[sp]
    wait_all(rec_got, n_span - 1, group_recv, 3)
    out = rec_got[0]
    for i in range(1, n_span):
        out = out + rec_got[i]
    rec_out[...] = out

    leave1()
    leave3()
    wait_all(routed1, n_span - 1, group_send, 0)
    wait_all(routed2, (n_chord - 1) * SLOTS, group_send, 1)
    wait_all(rec_rows, (n_chord - 1) * SLOTS, group_send, 2)
    wait_all(rec_got, n_span - 1, group_send, 3)
    for store in stores:
        store.wait()


def solution(mesh):
    n_chord, n_span = mesh.shape["chord"], mesh.shape["span"]

    def local(velocity, stress, material, moduli, drive, owner, cells):
        _, depth, size_x, size_y = velocity.shape
        per = drive.shape[0]

        def mem(*shape):
            return pltpu.VMEM(shape, F32)

        def edges(rows_dn, rows_up):
            return [
                mem(rows_dn * depth, size_y),
                mem(rows_up * depth, size_y),
                mem(size_x, LANES),
                mem(size_x, LANES),
            ]

        layer = (size_x, size_y)
        anywhere = pl.BlockSpec(memory_space=pl.ANY)
        vmem = pl.BlockSpec(memory_space=pltpu.VMEM)
        slots = n_chord * SLOTS
        return pl.pallas_call(
            functools.partial(kernel, n_chord, n_span),
            out_shape=(
                jax.ShapeDtypeStruct(velocity.shape, F32),
                jax.ShapeDtypeStruct(stress.shape, F32),
                jax.ShapeDtypeStruct(drive.shape, F32),
            ),
            in_specs=[
                anywhere,
                anywhere,
                anywhere,
                pl.BlockSpec(memory_space=pltpu.SMEM),
                vmem,
                vmem,
                vmem,
            ],
            out_specs=(anywhere, anywhere, vmem),
            scratch_shapes=[
                mem(3, depth + 2, *layer),
                mem(6, depth + 2, *layer),
                pltpu.VMEM((depth, *layer), jnp.int32),
                mem(10, depth, *layer),
                pltpu.VMEM((size_y, 8 * LANES), BF16),
                mem(8, LANES),
                mem(8, LANES),
                mem(2, *layer),
                mem(slots, LANES),
                mem(LANES, slots),
                mem(n_span, per, LANES),
                mem(n_span * per, LANES),
                mem(slots, LANES),
                mem(slots, LANES),
                mem(SLOTS, LANES),
                mem(slots, LANES),
                mem(n_span, per, LANES),
                mem(n_span, per, LANES),
                *edges(6, 5),
                mem(6 * depth, size_y),
                mem(5 * depth, size_y),
                mem(size_x, LANES),
                mem(size_x, LANES),
                mem(depth, LANES),
                mem(depth, LANES),
                *edges(3, 3),
                *edges(3, 3),
                mem(depth, LANES),
                mem(depth, LANES),
                *edges(1, 1),
                *edges(1, 1),
                mem(3, depth, size_y),
                mem(3, size_x, LANES),
                mem(5, depth, size_y),
                mem(5, size_x, LANES),
                pltpu.SemaphoreType.DMA((3,)),
                pltpu.SemaphoreType.DMA((2,)),
                pltpu.SemaphoreType.DMA((4,)),
                pltpu.SemaphoreType.DMA((4,)),
                pltpu.SemaphoreType.DMA((16,)),
                pltpu.SemaphoreType.DMA((16,)),
            ],
            compiler_params=pltpu.CompilerParams(
                collective_id=0, has_side_effects=True, vmem_limit_bytes=48 * 1024 * 1024
            ),
        )(
            velocity,
            stress,
            material,
            moduli,
            drive,
            owner.reshape(-1, LANES),
            cells.T,
        )

    in_specs = (
        P(None, None, "chord", "span"),
        P(None, None, "chord", "span"),
        P(None, "chord", "span"),
        P(),
        P(("chord", "span"), None),
        P(),
        P(),
    )
    out_specs = (
        P(None, None, "chord", "span"),
        P(None, None, "chord", "span"),
        P(("chord", "span"), None),
    )
    return jax.shard_map(local, mesh=mesh, in_specs=in_specs, out_specs=out_specs, check_vma=False)
```

```python
import functools

import jax
import jax.numpy as jnp
from jax import lax
from jax.experimental import pallas as pl
from jax.experimental.pallas import tpu as pltpu
from jax.sharding import PartitionSpec as P

MESH = pl.DeviceIdType.MESH
F32 = jnp.float32
BF16 = jnp.bfloat16
DT = 0.5
SLOTS = 16
LANES = 128
C11, C12, C13, C22, C23, C33, C44, C55, C66, BUOY = range(10)
XX, YY, ZZ, YZ, XZ, XY = range(6)


def iota(shape, dim):
    return lax.broadcasted_iota(jnp.int32, shape, dim)


def fiota(shape, dim):
    return iota(shape, dim).astype(F32)


def split3(x):
    a = x.astype(BF16)
    rest = x - a.astype(F32)
    b = rest.astype(BF16)
    return a, b, (rest - b.astype(F32)).astype(BF16)


def dot(a, b, contract=((1,), (0,))):
    return lax.dot_general(a, b, (contract, ((), ())), preferred_element_type=F32)


def kernel(
    n_chord,
    n_span,
    vel_in,
    str_in,
    mat_in,
    moduli_in,
    drive_in,
    owner_in,
    cells_in,
    v,
    s,
    rec_out,
    mat,
    moduli,
    drive,
    owner,
    cells,
    coef,
    onehot_y,
    slot_x,
    slot_y,
    plane,
    taken,
    taken_t,
    routed1,
    rows1,
    send2,
    routed2,
    rec_send,
    rec_rows,
    rec_back,
    rec_got,
    to_dn,
    to_up,
    to_rt,
    to_lt,
    from_up,
    from_dn,
    from_lt,
    from_rt,
    corner_up,
    corner_dn,
    vto_dn,
    vto_up,
    vto_rt,
    vto_lt,
    vfrom_up,
    vfrom_dn,
    vfrom_lt,
    vfrom_rt,
    vcorner_up,
    vcorner_dn,
    tto_dn,
    tto_up,
    tto_rt,
    tto_lt,
    tfrom_up,
    tfrom_dn,
    tfrom_lt,
    tfrom_rt,
    halo_row,
    halo_col,
    hcoef_row,
    hcoef_col,
    load_sem,
    group_send,
    group_recv,
    edge_send,
    edge_recv,
):
    c = lax.axis_index("chord")
    sp = lax.axis_index("span")
    depth = vel_in.shape[1]
    size_x = vel_in.shape[2]
    size_y = vel_in.shape[3]
    half = size_y - LANES
    has_up, has_dn = c > 0, c < n_chord - 1
    has_lt, has_rt = sp > 0, sp < n_span - 1
    diag_up = jnp.logical_and(has_up, has_rt)
    diag_dn = jnp.logical_and(has_dn, has_lt)

    pairs = [
        (drive_in, drive),
        (vel_in, v),
        (str_in, s),
        (mat_in, mat),
        (owner_in, owner),
        (cells_in.at[pl.ds(0, 8)], cells),
        (moduli_in, moduli),
    ]
    loads = [pltpu.make_async_copy(a, b, load_sem.at[i]) for i, (a, b) in enumerate(pairs)]
    for load in loads:
        load.start()

    barrier = pltpu.get_barrier_semaphore()

    def greet(to_c, to_s):
        pl.semaphore_signal(barrier, inc=1, device_id=(to_c, to_s), device_id_type=MESH)

    def around(at, i, count):
        to = at + i
        return jnp.where(to >= count, to - count, to)

    for i in range(1, n_span):
        greet(c, around(sp, i, n_span))
    for i in range(1, n_chord):
        greet(around(c, i, n_chord), sp)

    @pl.when(diag_up)
    def _():
        greet(c - 1, sp + 1)

    @pl.when(diag_dn)
    def _():
        greet(c + 1, sp - 1)

    @pl.when(jnp.logical_not(has_up))
    def _():
        for ref in (from_up, vfrom_up, tfrom_up):
            ref[...] = jnp.zeros_like(ref)

    @pl.when(jnp.logical_not(has_dn))
    def _():
        for ref in (from_dn, vfrom_dn, tfrom_dn):
            ref[...] = jnp.zeros_like(ref)

    @pl.when(jnp.logical_not(has_lt))
    def _():
        for ref in (from_lt, vfrom_lt, tfrom_lt):
            ref[...] = jnp.zeros_like(ref)

    @pl.when(jnp.logical_not(has_rt))
    def _():
        for ref in (from_rt, vfrom_rt, tfrom_rt):
            ref[...] = jnp.zeros_like(ref)

    @pl.when(jnp.logical_not(diag_up))
    def _():
        for ref in (corner_up, vcorner_up):
            ref[...] = jnp.zeros_like(ref)

    @pl.when(jnp.logical_not(diag_dn))
    def _():
        for ref in (corner_dn, vcorner_dn):
            ref[...] = jnp.zeros_like(ref)

    pl.semaphore_wait(
        barrier,
        n_span + n_chord - 2 + diag_up.astype(jnp.int32) + diag_dn.astype(jnp.int32),
    )

    def to_span(i, source, target, sem):
        to_s = around(sp, i, n_span)
        return pltpu.make_async_remote_copy(
            src_ref=source(to_s),
            dst_ref=target.at[sp],
            send_sem=group_send.at[sem],
            recv_sem=group_recv.at[sem],
            device_id=(c, to_s),
            device_id_type=MESH,
        )

    def to_chord(i, source, target, sem):
        to_c = around(c, i, n_chord)
        return pltpu.make_async_remote_copy(
            src_ref=source(to_c),
            dst_ref=target.at[pl.ds(pl.multiple_of(c * SLOTS, SLOTS), SLOTS)],
            send_sem=group_send.at[sem],
            recv_sem=group_recv.at[sem],
            device_id=(to_c, sp),
            device_id_type=MESH,
        )

    def start_all(count, make):
        for i in range(1, count):
            make(i).start()

    def wait_all(ref, count, sems, sem):
        part = ref.at[pl.ds(0, count)]
        pltpu.make_async_copy(part, part, sems.at[sem]).wait()

    loads[0].wait()
    start_all(n_span, lambda i: to_span(i, lambda to_s: drive, routed1, 0))
    routed1[sp] = drive[...]

    def edge(source, target, to, index):
        return pltpu.make_async_remote_copy(
            src_ref=source,
            dst_ref=target,
            send_sem=edge_send.at[index],
            recv_sem=edge_recv.at[index],
            device_id=to,
            device_id_type=MESH,
        )

    up, dn, lt, rt = (c - 1, sp), (c + 1, sp), (c, sp - 1), (c, sp + 1)

    def exchange(first, up_src, dn_src, lt_src, rt_src, up_dst, dn_dst, lt_dst, rt_dst, corners):
        moves = [
            (has_up, has_dn, edge(up_src, dn_dst, up, first)),
            (has_dn, has_up, edge(dn_src, up_dst, dn, first + 1)),
            (has_lt, has_rt, edge(lt_src, rt_dst, lt, first + 2)),
            (has_rt, has_lt, edge(rt_src, lt_dst, rt, first + 3)),
        ]
        if corners is not None:
            corner_from_dn, corner_from_up = corners
            moves.append(
                (
                    diag_up,
                    diag_dn,
                    edge(
                        up_src.at[pl.ds(depth, depth), pl.ds(half, LANES)],
                        corner_from_dn,
                        (c - 1, sp + 1),
                        first + 4,
                    ),
                )
            )
            moves.append(
                (
                    diag_dn,
                    diag_up,
                    edge(
                        dn_src.at[pl.ds(0, depth), pl.ds(0, LANES)],
                        corner_from_up,
                        (c + 1, sp - 1),
                        first + 5,
                    ),
                )
            )

        def start():
            for goes, _, copy in moves:
                pl.when(goes)(copy.start)

        def arrive():
            for _, comes, copy in moves:
                pl.when(comes)(copy.wait_recv)

        def leave():
            for goes, _, copy in moves:
                pl.when(goes)(copy.wait_send)

        return start, arrive, leave

    start1, arrive1, leave1 = exchange(
        0, to_up, to_dn, to_lt, to_rt, from_up, from_dn, from_lt, from_rt, (corner_dn, corner_up)
    )
    start2, arrive2, leave2 = exchange(
        6, vto_up, vto_dn, vto_lt, vto_rt, vfrom_up, vfrom_dn, vfrom_lt, vfrom_rt, (vcorner_dn, vcorner_up)
    )
    start3, arrive3, leave3 = exchange(
        12, tto_up, tto_dn, tto_lt, tto_rt, tfrom_up, tfrom_dn, tfrom_lt, tfrom_rt, None
    )

    def pack_rows(ref, row, fields):
        for z in range(depth):
            for k, read in enumerate(fields):
                ref[k * depth + z : k * depth + z + 1, :] = read(z, row)

    lane = iota((size_x, LANES), 1)
    row = iota((size_x, size_y), 0)

    def pack_cols(ref, column, fields):
        base = 0 if column == 0 else half
        at = column - base

        acc = jnp.zeros((size_x, LANES), F32)
        for z in range(depth):
            for k, read in enumerate(fields):
                to = k * depth + z
                by = (to + LANES - at) % LANES
                tile = read(z, base)
                moved = pltpu.roll(tile, by, 1) if by else tile
                acc = jnp.where(lane == to, moved, acc)
        ref[...] = acc

    def row_of(ref, comp):
        return lambda z, r: ref[comp, z, r : r + 1, :]

    def col_of(ref, comp):
        return lambda z, base: ref[comp, z, :, base : base + LANES]

    def mat_row(z, r):
        return mat[z, r : r + 1, :].astype(F32)

    def mat_col(z, base):
        return mat[z, :, base : base + LANES].astype(F32)

    v_rows = [row_of(v, k) for k in range(3)]
    v_cols = [col_of(v, k) for k in range(3)]

    for load in loads[1:]:
        load.wait()
    pack_rows(to_dn, size_x - 1, v_rows + [row_of(s, XY), row_of(s, XZ), mat_row])
    pack_rows(to_up, 0, v_rows + [row_of(s, XX), mat_row])
    pack_cols(to_rt, size_y - 1, v_cols + [col_of(s, XY), col_of(s, YZ), mat_col])
    pack_cols(to_lt, 0, v_cols + [col_of(s, YY), mat_col])
    start1()

    n_block = owner.shape[0]
    earlier = (iota((LANES, LANES), 0) < iota((LANES, LANES), 1)).astype(BF16)
    wanted = iota((n_chord, LANES), 0) * n_span + sp
    before = jnp.zeros((n_chord, LANES), F32)
    here = jnp.zeros((n_chord, LANES), F32)
    for a in range(n_block):
        same = (owner[a : a + 1, :] == wanted).astype(F32)
        before = before + same * (a < c).astype(F32)
        here = here + same * (a == c).astype(F32)
    rank = jnp.sum(before, axis=1, keepdims=True) + dot(here.astype(BF16), earlier)
    rank = jnp.where(here > 0.5, rank, -1.0)
    slot_ids = fiota((SLOTS, LANES), 0)
    for k in range(n_chord):
        taken[k * SLOTS : (k + 1) * SLOTS, :] = (rank[k : k + 1, :] == slot_ids).astype(F32)
    taken_t[...] = jnp.transpose(taken[...])

    mine = (owner[...] == c * n_span + sp).astype(F32)
    my_rank = dot(mine.astype(BF16), earlier)
    total = jnp.broadcast_to(jnp.sum(mine, axis=1, keepdims=True), (n_block, LANES))
    block_ids = iota((n_block, LANES), 0)
    for a in range(n_block - 1):
        my_rank = my_rank + jnp.where(block_ids > a, total[a : a + 1, :], 0.0)
    my_rank = jnp.where(mine > 0.5, my_rank, -1.0)
    first_x = jnp.zeros((SLOTS, LANES), F32)
    first_y = jnp.zeros((SLOTS, LANES), F32)
    shift = size_y.bit_length() - 1
    for a in range(n_block):
        anchor = cells[0:1, a * LANES : (a + 1) * LANES]
        hit = my_rank[a : a + 1, :] == slot_ids
        first_x = first_x + jnp.where(hit, (anchor >> shift).astype(F32), 0.0)
        first_y = first_y + jnp.where(hit, (anchor & (size_y - 1)).astype(F32), 0.0)
    first_x = jnp.sum(first_x, axis=1, keepdims=True)
    first_y = jnp.sum(first_y, axis=1, keepdims=True)
    low = iota((8, LANES), 1) < 64
    cell_id = iota((8, LANES), 1) & 63
    slot_x[...] = jnp.where(low, first_x[0:8], first_x[8:16]) + (cell_id >> 3).astype(F32)
    slot_y[...] = jnp.where(low, first_y[0:8], first_y[8:16]) + (cell_id & 7).astype(F32)
    y_ids = fiota((size_y, LANES), 0)
    for t in range(8):
        onehot_y[:, t * LANES : (t + 1) * LANES] = (
            (slot_y[t : t + 1, :] == y_ids).astype(F32).astype(BF16)
        )
    x_ids = fiota((size_x, LANES), 0)

    def table(kind, index):
        out = jnp.full(kind.shape, DT * moduli[0, index], F32)
        for m in range(1, 4):
            out = jnp.where(kind == m, DT * moduli[m, index], out)
        return out

    def coef_layer(z, _):
        kind = mat[z]
        for k in range(10):
            coef[k, z] = table(kind, k)
        return 0

    lax.fori_loop(0, depth, coef_layer, 0)

    wait_all(routed1, n_span - 1, group_recv, 0)
    per = drive.shape[0]
    for i in range(n_span):
        rows1[i * per : (i + 1) * per, :] = routed1[i]
    pick = taken[...].astype(BF16)
    send2[...] = sum(dot(pick, part) for part in split3(rows1[...]))
    own = pl.ds(pl.multiple_of(c * SLOTS, SLOTS), SLOTS)

    def for_chord(ref):
        return lambda to_c: ref.at[pl.ds(pl.multiple_of(to_c * SLOTS, SLOTS), SLOTS)]

    start_all(n_chord, lambda i: to_chord(i, for_chord(send2), routed2, 1))
    routed2[own, :] = send2[own, :]

    def along_x(field, by, edge_row):
        if by > 0:
            return jnp.where(row == 0, edge_row, pltpu.roll(field, 1, 0))
        return jnp.where(row == size_x - 1, edge_row, pltpu.roll(field, size_x - 1, 0))

    def along_y(field, by, edge_col):
        if by > 0:
            moved = pltpu.roll(field, 1, 1)
            head = jnp.where(lane == 0, edge_col, moved[:, :LANES])
            return jnp.concatenate([head, moved[:, LANES:]], axis=1)
        moved = pltpu.roll(field, size_y - 1, 1)
        tail = jnp.where(lane == LANES - 1, edge_col, moved[:, half:])
        return jnp.concatenate([moved[:, :half], tail], axis=1)

    def first_lane(ref, field, z):
        return pltpu.roll(ref[...], lax.rem(2 * LANES - (field * depth + z), LANES), 1)

    def last_lane(ref, field, z):
        return pltpu.roll(ref[...], lax.rem(2 * LANES - 1 - (field * depth + z), LANES), 1)

    bottom, top = 0, depth - 1

    def stress_layer(z, up_ref, dn_ref, lt_ref, rt_ref):
        is_bottom, is_top = isinstance(z, int) and z == bottom, isinstance(z, int) and z == top
        vx, vy, vz = v[0, z], v[1, z], v[2, z]
        zz = vz if is_bottom else vz - v[2, z - 1]
        zy = -vy if is_top else v[1, z + 1] - vy
        zx = -vx if is_top else v[0, z + 1] - vx
        xx = vx - along_x(vx, 1, up_ref[pl.ds(z, 1), :])
        yy = vy - along_y(vy, 1, first_lane(lt_ref, 1, z))
        yz = zy + (along_y(vz, -1, last_lane(rt_ref, 2, z)) - vz)
        xz = zx + (along_x(vz, -1, dn_ref[pl.ds(2 * depth + z, 1), :]) - vz)
        xy = (along_y(vx, -1, last_lane(rt_ref, 0, z)) - vx) + (
            along_x(vy, -1, dn_ref[pl.ds(depth + z, 1), :]) - vy
        )
        s[XX, z] += coef[C11, z] * xx + coef[C12, z] * yy + coef[C13, z] * zz
        s[YY, z] += coef[C12, z] * xx + coef[C22, z] * yy + coef[C23, z] * zz
        s[ZZ, z] += coef[C13, z] * xx + coef[C23, z] * yy + coef[C33, z] * zz
        s[YZ, z] += coef[C44, z] * yz
        s[XZ, z] += coef[C55, z] * xz
        s[XY, z] += coef[C66, z] * xy

    def velocity_layer(z):
        is_bottom, is_top = isinstance(z, int) and z == bottom, isinstance(z, int) and z == top
        sxx, syy, szz = s[XX, z], s[YY, z], s[ZZ, z]
        syz, sxz, sxy = s[YZ, z], s[XZ, z], s[XY, z]
        ax = (
            (along_x(sxx, -1, halo_row[0, pl.ds(z, 1), :]) - sxx)
            + (sxy - along_y(sxy, 1, first_lane(halo_col.at[1], 0, z)))
            + (sxz if is_bottom else sxz - s[XZ, z - 1])
        )
        ay = (
            (sxy - along_x(sxy, 1, halo_row[1, pl.ds(z, 1), :]))
            + (along_y(syy, -1, last_lane(halo_col.at[0], 0, z)) - syy)
            + (syz if is_bottom else syz - s[YZ, z - 1])
        )
        az = (
            (sxz - along_x(sxz, 1, halo_row[2, pl.ds(z, 1), :]))
            + (syz - along_y(syz, 1, first_lane(halo_col.at[2], 0, z)))
            + (-szz if is_top else s[ZZ, z + 1] - szz)
        )
        b = coef[BUOY, z]
        v[0, z] += b * ax
        v[1, z] += b * ay
        v[2, z] += b * az

    wide = (depth, size_y)
    wide_lane = iota(wide, 1)
    wide_z = iota(wide, 0)

    def below_z(f):
        return jnp.where(wide_z == 0, 0.0, pltpu.roll(f, 1, 0))

    def above_z(f):
        return jnp.where(wide_z == depth - 1, 0.0, pltpu.roll(f, depth - 1, 0))

    def lane_below_z(f):
        return jnp.where(lane == 0, 0.0, pltpu.roll(f, 1, 1))

    def lane_above_z(f):
        return jnp.where(lane == depth - 1, 0.0, pltpu.roll(f, LANES - 1, 1))

    def to_lanes(corner, at):
        col = jnp.broadcast_to(corner[:, at : at + 1], (depth, LANES))
        here = iota((depth, LANES), 0) == iota((depth, LANES), 1)
        return jnp.sum(jnp.where(here, col, 0.0), axis=0, keepdims=True)

    def lanes_of(ref, field):
        if field == 0:
            return ref[...]
        return pltpu.roll(ref[...], LANES - field * depth, 1)

    narrow_row = iota((size_x, LANES), 0)

    def halo_stress(up_ref, dn_ref, lt_ref, rt_ref, cup, cdn, my_up, my_dn, my_lt, my_rt):
        def rows(ref, k):
            return ref[k * depth : (k + 1) * depth, :]

        vx, vy, vz = rows(dn_ref, 0), rows(dn_ref, 1), rows(dn_ref, 2)
        corner = jnp.broadcast_to(cdn[:, LANES - 1 : LANES], wide)
        vy_back = jnp.where(wide_lane == 0, corner, pltpu.roll(vy, 1, 1))
        halo_row[0] += (
            hcoef_row[0] * (vx - rows(my_dn, 0))
            + hcoef_row[1] * (vy - vy_back)
            + hcoef_row[2] * (vz - below_z(vz))
        )
        vx, vy, vz = rows(up_ref, 0), rows(up_ref, 1), rows(up_ref, 2)
        corner = jnp.broadcast_to(cup[:, 0:1], wide)
        vx_next = jnp.where(wide_lane == size_y - 1, corner, pltpu.roll(vx, size_y - 1, 1))
        halo_row[1] += hcoef_row[3] * ((vx_next - vx) + (rows(my_up, 1) - vy))
        halo_row[2] += hcoef_row[4] * ((above_z(vx) - vx) + (rows(my_up, 2) - vz))
        vx, vy, vz = lanes_of(rt_ref, 0), lanes_of(rt_ref, 1), lanes_of(rt_ref, 2)
        vx_back = jnp.where(narrow_row == 0, to_lanes(cup, 0), pltpu.roll(vx, 1, 0))
        halo_col[0] += (
            hcoef_col[0] * (vx - vx_back)
            + hcoef_col[1] * (vy - lanes_of(my_rt, 1))
            + hcoef_col[2] * (vz - lane_below_z(vz))
        )
        vx, vy, vz = lanes_of(lt_ref, 0), lanes_of(lt_ref, 1), lanes_of(lt_ref, 2)
        vy_next = jnp.where(
            narrow_row == size_x - 1, to_lanes(cdn, LANES - 1), pltpu.roll(vy, size_x - 1, 0)
        )
        halo_col[1] += hcoef_col[3] * ((lanes_of(my_lt, 0) - vx) + (vy_next - vy))
        halo_col[2] += hcoef_col[4] * ((lane_above_z(vy) - vy) + (lanes_of(my_lt, 2) - vz))

    arrive1()
    kind = from_dn[4 * depth : 5 * depth, :]
    inside = has_dn.astype(F32)
    for k, index in enumerate((C11, C12, C13)):
        hcoef_row[k] = table(kind, index) * inside
    kind = from_up[5 * depth : 6 * depth, :]
    inside = has_up.astype(F32)
    for k, index in enumerate((C66, C55)):
        hcoef_row[3 + k] = table(kind, index) * inside
    kind = lanes_of(from_rt, 4)
    inside = has_rt.astype(F32)
    for k, index in enumerate((C12, C22, C23)):
        hcoef_col[k] = table(kind, index) * inside
    kind = lanes_of(from_lt, 5)
    inside = has_lt.astype(F32)
    for k, index in enumerate((C66, C44)):
        hcoef_col[3 + k] = table(kind, index) * inside
    halo_row[0] = from_dn[3 * depth : 4 * depth, :]
    halo_row[1] = from_up[3 * depth : 4 * depth, :]
    halo_row[2] = from_up[4 * depth : 5 * depth, :]
    halo_col[0] = lanes_of(from_rt, 3)
    halo_col[1] = lanes_of(from_lt, 3)
    halo_col[2] = lanes_of(from_lt, 4)

    def stress_first(z, _):
        stress_layer(z, from_up, from_dn, from_lt, from_rt)
        return 0

    def velocity_body(z, _):
        velocity_layer(z)
        return 0

    stress_first(bottom, 0)
    lax.fori_loop(bottom + 1, top, stress_first, 0)
    stress_first(top, 0)
    halo_stress(
        from_up, from_dn, from_lt, from_rt, corner_up, corner_dn, to_up, to_dn, to_lt, to_rt
    )
    velocity_layer(bottom)
    lax.fori_loop(bottom + 1, top, velocity_body, 0)
    velocity_layer(top)

    pack_rows(vto_dn, size_x - 1, v_rows)
    pack_rows(vto_up, 0, v_rows)
    pack_cols(vto_rt, size_y - 1, v_cols)
    pack_cols(vto_lt, 0, v_cols)
    start2()

    wait_all(routed2, (n_chord - 1) * SLOTS, group_recv, 1)
    rows = routed2[0:SLOTS, :]
    for k in range(1, n_chord):
        rows = rows + routed2[k * SLOTS : (k + 1) * SLOTS, :]
    head, tail = rows[0:8], rows[8:16]
    force = [
        jnp.where(low, head, pltpu.roll(tail, 64, 1)),
        jnp.where(low, pltpu.roll(head, 64, 1), tail),
    ]

    def in_slot(t):
        return slot_x[t : t + 1, :] == x_ids

    for step in range(2):
        wide_force = jnp.concatenate(
            [jnp.where(in_slot(t), force[step][t : t + 1, :], 0.0) for t in range(8)], axis=1
        )
        parts = jnp.concatenate(split3(wide_force), axis=0)
        got = dot(parts, onehot_y[...], ((1,), (1,)))
        plane[step] = got[:size_x] + got[size_x : 2 * size_x] + got[2 * size_x :]

    def add_force(step):
        v[2, top] += coef[BUOY, depth - 1] * plane[step]

    def sample():
        got = dot(jnp.concatenate(split3(v[2, top]), axis=0), onehot_y[...])
        got = got[:size_x] + got[size_x : 2 * size_x] + got[2 * size_x :]
        out = []
        for t in range(8):
            chosen = jnp.where(in_slot(t), got[:, t * LANES : (t + 1) * LANES], 0.0)
            out.append(jnp.sum(chosen, axis=0, keepdims=True))
        return jnp.concatenate(out, axis=0)

    add_force(0)
    tto_dn[...] = jnp.broadcast_to(v[2, top, size_x - 1 : size_x, :], (depth, size_y))
    tto_up[...] = jnp.broadcast_to(v[2, top, 0:1, :], (depth, size_y))
    tto_rt[...] = v[2, top, :, half:]
    tto_lt[...] = v[2, top, :, :LANES]
    start3()
    first = sample()

    arrive2()

    def stress_second(z, _):
        stress_layer(z, vfrom_up, vfrom_dn, vfrom_lt, vfrom_rt)
        return 0

    stress_second(bottom, 0)
    lax.fori_loop(bottom + 1, top, stress_second, 0)
    arrive3()
    leave2()
    top_row = 2 * depth + top
    vfrom_up[top_row : top_row + 1, :] = tfrom_up[0:1, :]
    vfrom_dn[top_row : top_row + 1, :] = tfrom_dn[0:1, :]
    vfrom_rt[...] = jnp.where(
        lane == top_row, pltpu.roll(tfrom_rt[...], top_row, 1), vfrom_rt[...]
    )
    vfrom_lt[...] = jnp.where(
        lane == top_row, pltpu.roll(tfrom_lt[...], top_row + 1, 1), vfrom_lt[...]
    )
    vto_up[top_row : top_row + 1, :] = v[2, top, 0:1, :]
    vto_lt[...] = jnp.where(
        lane == top_row, pltpu.roll(v[2, top, :, :LANES], top_row, 1), vto_lt[...]
    )
    stress_layer(top, vfrom_up, vfrom_dn, vfrom_lt, vfrom_rt)
    halo_stress(
        vfrom_up,
        vfrom_dn,
        vfrom_lt,
        vfrom_rt,
        vcorner_up,
        vcorner_dn,
        vto_up,
        vto_dn,
        vto_lt,
        vto_rt,
    )
    velocity_layer(top)
    add_force(1)
    second = sample()

    rec_send[0:8, :] = jnp.where(low, first, pltpu.roll(second, 64, 1))
    rec_send[8:16, :] = jnp.where(low, pltpu.roll(first, 64, 1), second)
    start_all(n_chord, lambda i: to_chord(i, lambda to_c: rec_send, rec_rows, 2))
    rec_rows[own, :] = rec_send[...]

    velocity_layer(bottom)
    lax.fori_loop(bottom + 1, top, velocity_body, 0)

    wait_all(rec_rows, (n_chord - 1) * SLOTS, group_recv, 2)
    pick = taken_t[...].astype(BF16)
    back = sum(dot(pick, part) for part in split3(rec_rows[...]))
    for i in range(n_span):
        rec_back[i] = back[i * per : (i + 1) * per, :]
    start_all(n_span, lambda i: to_span(i, lambda to_s: rec_back.at[to_s], rec_got, 3))
    rec_got[sp] = rec_back[sp]
    wait_all(rec_got, n_span - 1, group_recv, 3)
    out = rec_got[0]
    for i in range(1, n_span):
        out = out + rec_got[i]
    rec_out[...] = out

    leave1()
    leave3()
    wait_all(routed1, n_span - 1, group_send, 0)
    wait_all(routed2, (n_chord - 1) * SLOTS, group_send, 1)
    wait_all(rec_rows, (n_chord - 1) * SLOTS, group_send, 2)
    wait_all(rec_got, n_span - 1, group_send, 3)


def hand_over(v, s, rec, vel_out, str_out, rec_out, sem):
    pairs = [(v, vel_out), (s, str_out), (rec, rec_out)]
    copies = [pltpu.make_async_copy(a, b, sem.at[i]) for i, (a, b) in enumerate(pairs)]
    for copy in copies:
        copy.start()
    for copy in copies:
        copy.wait()


def solution(mesh):
    n_chord, n_span = mesh.shape["chord"], mesh.shape["span"]

    def local(velocity, stress, material, moduli, drive, owner, cells):
        _, depth, size_x, size_y = velocity.shape
        per = drive.shape[0]

        def mem(*shape):
            return pltpu.VMEM(shape, F32)

        def edges(rows_dn, rows_up):
            return [
                mem(rows_dn * depth, size_y),
                mem(rows_up * depth, size_y),
                mem(size_x, LANES),
                mem(size_x, LANES),
            ]

        layer = (size_x, size_y)
        vmem = pl.BlockSpec(memory_space=pltpu.VMEM)
        slots = n_chord * SLOTS
        inputs = (velocity, stress, material, moduli, drive, owner.reshape(-1, LANES), cells.T)
        state = pl.pallas_call(
            functools.partial(kernel, n_chord, n_span),
            out_shape=(
                jax.ShapeDtypeStruct(velocity.shape, F32),
                jax.ShapeDtypeStruct(stress.shape, F32),
                jax.ShapeDtypeStruct(drive.shape, F32),
            ),
            in_specs=[pl.BlockSpec(memory_space=pltpu.HBM)] * 7,
            out_specs=(vmem, vmem, vmem),
            scratch_shapes=[
                pltpu.VMEM((depth, *layer), jnp.int32),
                pltpu.SMEM(moduli.shape, F32),
                mem(*drive.shape),
                pltpu.VMEM((owner.size // LANES, LANES), jnp.int32),
                pltpu.VMEM((8, owner.size), jnp.int32),
                mem(10, depth, *layer),
                pltpu.VMEM((size_y, 8 * LANES), BF16),
                mem(8, LANES),
                mem(8, LANES),
                mem(2, *layer),
                mem(slots, LANES),
                mem(LANES, slots),
                mem(n_span, per, LANES),
                mem(n_span * per, LANES),
                mem(slots, LANES),
                mem(slots, LANES),
                mem(SLOTS, LANES),
                mem(slots, LANES),
                mem(n_span, per, LANES),
                mem(n_span, per, LANES),
                *edges(6, 5),
                mem(6 * depth, size_y),
                mem(5 * depth, size_y),
                mem(size_x, LANES),
                mem(size_x, LANES),
                mem(depth, LANES),
                mem(depth, LANES),
                *edges(3, 3),
                *edges(3, 3),
                mem(depth, LANES),
                mem(depth, LANES),
                *edges(1, 1),
                *edges(1, 1),
                mem(3, depth, size_y),
                mem(3, size_x, LANES),
                mem(5, depth, size_y),
                mem(5, size_x, LANES),
                pltpu.SemaphoreType.DMA((7,)),
                pltpu.SemaphoreType.DMA((4,)),
                pltpu.SemaphoreType.DMA((4,)),
                pltpu.SemaphoreType.DMA((16,)),
                pltpu.SemaphoreType.DMA((16,)),
            ],
            compiler_params=pltpu.CompilerParams(
                collective_id=0, has_side_effects=True, vmem_limit_bytes=48 * 1024 * 1024
            ),
        )(*(pltpu.with_memory_space_constraint(x, pltpu.HBM) for x in inputs))
        hbm = pl.BlockSpec(memory_space=pltpu.HBM)
        return pl.pallas_call(
            hand_over,
            out_shape=tuple(jax.ShapeDtypeStruct(x.shape, x.dtype) for x in state),
            in_specs=[pl.BlockSpec(memory_space=pl.ANY)] * 3,
            out_specs=(hbm, hbm, hbm),
            scratch_shapes=[pltpu.SemaphoreType.DMA((3,))],
        )(*(pltpu.with_memory_space_constraint(x, pltpu.VMEM) for x in state))

    in_specs = (
        P(None, None, "chord", "span"),
        P(None, None, "chord", "span"),
        P(None, "chord", "span"),
        P(),
        P(("chord", "span"), None),
        P(),
        P(),
    )
    out_specs = (
        P(None, None, "chord", "span"),
        P(None, None, "chord", "span"),
        P(("chord", "span"), None),
    )
    return jax.shard_map(local, mesh=mesh, in_specs=in_specs, out_specs=out_specs, check_vma=False)
```

```python
import functools

import jax
import jax.numpy as jnp
from jax import lax
from jax.experimental import pallas as pl
from jax.experimental.pallas import tpu as pltpu
from jax.sharding import PartitionSpec as P

MESH = pl.DeviceIdType.MESH
F32 = jnp.float32
BF16 = jnp.bfloat16
DT = 0.5
SLOTS = 16
LANES = 128
SPLIT_X_HI, SPLIT_Z, SPLIT_CORE = 2, 8, 2
C11, C12, C13, C22, C23, C33, C44, C55, C66, BUOY = range(10)
XX, YY, ZZ, YZ, XZ, XY = range(6)


def iota(shape, dim):
    return lax.broadcasted_iota(jnp.int32, shape, dim)


def fiota(shape, dim):
    return iota(shape, dim).astype(F32)


def split3(x):
    a = x.astype(BF16)
    rest = x - a.astype(F32)
    b = rest.astype(BF16)
    return a, b, (rest - b.astype(F32)).astype(BF16)


def dot(a, b, contract=((1,), (0,))):
    return lax.dot_general(a, b, (contract, ((), ())), preferred_element_type=F32)


def kernel(
    n_chord,
    n_span,
    vel_in,
    str_in,
    mat_in,
    moduli_in,
    drive_in,
    owner_in,
    cells_in,
    v,
    s,
    rec_out,
    mat,
    moduli,
    drive,
    owner,
    cells,
    coef,
    onehot_y,
    slot_x,
    slot_y,
    plane,
    ranks,
    taken,
    taken_t,
    gathered,
    rows1,
    send2,
    routed2,
    rec_send,
    rec_rows,
    rec_back,
    rec_got,
    to_dn,
    to_up,
    to_rt,
    to_lt,
    from_up,
    from_dn,
    from_lt,
    from_rt,
    corner_up,
    corner_dn,
    vto_dn,
    vto_up,
    vto_rt,
    vto_lt,
    vfrom_up,
    vfrom_dn,
    vfrom_lt,
    vfrom_rt,
    vcorner_up,
    vcorner_dn,
    tto_dn,
    tto_up,
    tto_rt,
    tto_lt,
    tfrom_up,
    tfrom_dn,
    tfrom_lt,
    tfrom_rt,
    halo_row,
    halo_col,
    hcoef_row,
    hcoef_col,
    load_sem,
    group_send,
    group_recv,
    edge_send,
    edge_recv,
):
    c = lax.axis_index("chord")
    sp = lax.axis_index("span")
    depth = vel_in.shape[1]
    size_x = vel_in.shape[2]
    size_y = vel_in.shape[3]
    half = size_y - LANES
    n_z = SPLIT_Z
    n_p = n_chord * SPLIT_X_HI * SPLIT_CORE
    my_z = lax.rem(lax.div(sp, SPLIT_CORE), SPLIT_Z)
    x_hi = lax.div(sp, SPLIT_Z * SPLIT_CORE)
    my_p = (c * SPLIT_X_HI + x_hi) * SPLIT_CORE + lax.rem(sp, SPLIT_CORE)
    xor = jnp.bitwise_xor

    def p_partner(i):
        core, high, to_c = i % SPLIT_CORE, i // SPLIT_CORE % SPLIT_X_HI, i // SPLIT_CORE // SPLIT_X_HI
        return xor(c, to_c), xor(sp, high * SPLIT_Z * SPLIT_CORE + core)

    def z_partner(i):
        return c, xor(sp, i * SPLIT_CORE)

    has_up, has_dn = c > 0, c < n_chord - 1
    has_lt, has_rt = sp > 0, sp < n_span - 1
    diag_up = jnp.logical_and(has_up, has_rt)
    diag_dn = jnp.logical_and(has_dn, has_lt)

    pairs = [
        (drive_in, drive),
        (vel_in, v),
        (str_in, s),
        (mat_in, mat),
        (owner_in, owner),
        (cells_in.at[pl.ds(0, 8)], cells),
        (moduli_in, moduli),
    ]
    loads = [pltpu.make_async_copy(a, b, load_sem.at[i]) for i, (a, b) in enumerate(pairs)]
    for load in loads:
        load.start()

    barrier = pltpu.get_barrier_semaphore()

    def greet(to_c, to_s):
        pl.semaphore_signal(barrier, inc=1, device_id=(to_c, to_s), device_id_type=MESH)

    for i in range(1, n_p):
        greet(*p_partner(i))
    for i in range(1, n_z):
        greet(*z_partner(i))
    sides = [
        (has_up, (c - 1, sp)),
        (has_dn, (c + 1, sp)),
        (has_lt, (c, sp - 1)),
        (has_rt, (c, sp + 1)),
        (diag_up, (c - 1, sp + 1)),
        (diag_dn, (c + 1, sp - 1)),
    ]
    for there, to in sides:
        pl.when(there)(functools.partial(greet, *to))

    @pl.when(jnp.logical_not(has_up))
    def _():
        for ref in (from_up, vfrom_up, tfrom_up):
            ref[...] = jnp.zeros_like(ref)

    @pl.when(jnp.logical_not(has_dn))
    def _():
        for ref in (from_dn, vfrom_dn, tfrom_dn):
            ref[...] = jnp.zeros_like(ref)

    @pl.when(jnp.logical_not(has_lt))
    def _():
        for ref in (from_lt, vfrom_lt, tfrom_lt):
            ref[...] = jnp.zeros_like(ref)

    @pl.when(jnp.logical_not(has_rt))
    def _():
        for ref in (from_rt, vfrom_rt, tfrom_rt):
            ref[...] = jnp.zeros_like(ref)

    @pl.when(jnp.logical_not(diag_up))
    def _():
        for ref in (corner_up, vcorner_up):
            ref[...] = jnp.zeros_like(ref)

    @pl.when(jnp.logical_not(diag_dn))
    def _():
        for ref in (corner_dn, vcorner_dn):
            ref[...] = jnp.zeros_like(ref)

    pl.semaphore_wait(
        barrier,
        n_p + n_z - 2 + sum(there.astype(jnp.int32) for there, _ in sides),
    )

    def send(source, target, to, sem):
        return pltpu.make_async_remote_copy(
            src_ref=source,
            dst_ref=target,
            send_sem=group_send.at[sem],
            recv_sem=group_recv.at[sem],
            device_id=to,
            device_id_type=MESH,
        )

    def wait_all(ref, count, sems, sem):
        if count:
            part = ref.at[pl.ds(0, count)]
            pltpu.make_async_copy(part, part, sems.at[sem]).wait()

    def block(ref, index, count):
        return ref.at[pl.ds(pl.multiple_of(index * count, count), count)]

    loads[0].wait()
    for i in range(1, n_p):
        send(drive, gathered.at[my_p], p_partner(i), 0).start()
    gathered[my_p] = drive[...]

    def edge(source, target, to, index):
        return pltpu.make_async_remote_copy(
            src_ref=source,
            dst_ref=target,
            send_sem=edge_send.at[index],
            recv_sem=edge_recv.at[index],
            device_id=to,
            device_id_type=MESH,
        )

    up, dn, lt, rt = (c - 1, sp), (c + 1, sp), (c, sp - 1), (c, sp + 1)

    def exchange(first, up_src, dn_src, lt_src, rt_src, up_dst, dn_dst, lt_dst, rt_dst, corners):
        moves = [
            (has_up, has_dn, edge(up_src, dn_dst, up, first)),
            (has_dn, has_up, edge(dn_src, up_dst, dn, first + 1)),
            (has_lt, has_rt, edge(lt_src, rt_dst, lt, first + 2)),
            (has_rt, has_lt, edge(rt_src, lt_dst, rt, first + 3)),
        ]
        if corners is not None:
            corner_from_dn, corner_from_up = corners
            moves.append(
                (
                    diag_up,
                    diag_dn,
                    edge(
                        up_src.at[pl.ds(depth, depth), pl.ds(half, LANES)],
                        corner_from_dn,
                        (c - 1, sp + 1),
                        first + 4,
                    ),
                )
            )
            moves.append(
                (
                    diag_dn,
                    diag_up,
                    edge(
                        dn_src.at[pl.ds(0, depth), pl.ds(0, LANES)],
                        corner_from_up,
                        (c + 1, sp - 1),
                        first + 5,
                    ),
                )
            )

        def start():
            for goes, _, copy in moves:
                pl.when(goes)(copy.start)

        def arrive():
            for _, comes, copy in moves:
                pl.when(comes)(copy.wait_recv)

        def leave():
            for goes, _, copy in moves:
                pl.when(goes)(copy.wait_send)

        return start, arrive, leave

    start1, arrive1, leave1 = exchange(
        0, to_up, to_dn, to_lt, to_rt, from_up, from_dn, from_lt, from_rt, (corner_dn, corner_up)
    )
    start2, arrive2, leave2 = exchange(
        6, vto_up, vto_dn, vto_lt, vto_rt, vfrom_up, vfrom_dn, vfrom_lt, vfrom_rt, (vcorner_dn, vcorner_up)
    )
    start3, arrive3, leave3 = exchange(
        12, tto_up, tto_dn, tto_lt, tto_rt, tfrom_up, tfrom_dn, tfrom_lt, tfrom_rt, None
    )

    def pack_rows(ref, row, fields):
        for z in range(depth):
            for k, read in enumerate(fields):
                ref[k * depth + z : k * depth + z + 1, :] = read(z, row)

    lane = iota((size_x, LANES), 1)
    row = iota((size_x, size_y), 0)

    def pack_cols(ref, column, fields):
        base = 0 if column == 0 else half
        at = column - base

        acc = jnp.zeros((size_x, LANES), F32)
        for z in range(depth):
            for k, read in enumerate(fields):
                to = k * depth + z
                by = (to + LANES - at) % LANES
                tile = read(z, base)
                moved = pltpu.roll(tile, by, 1) if by else tile
                acc = jnp.where(lane == to, moved, acc)
        ref[...] = acc

    def row_of(ref, comp):
        return lambda z, r: ref[comp, z, r : r + 1, :]

    def col_of(ref, comp):
        return lambda z, base: ref[comp, z, :, base : base + LANES]

    def mat_row(z, r):
        return mat[z, r : r + 1, :].astype(F32)

    def mat_col(z, base):
        return mat[z, :, base : base + LANES].astype(F32)

    v_rows = [row_of(v, k) for k in range(3)]
    v_cols = [col_of(v, k) for k in range(3)]

    for load in loads[1:]:
        load.wait()
    pack_rows(to_dn, size_x - 1, v_rows + [row_of(s, XY), row_of(s, XZ), mat_row])
    pack_rows(to_up, 0, v_rows + [row_of(s, XX), mat_row])
    pack_cols(to_rt, size_y - 1, v_cols + [col_of(s, XY), col_of(s, YZ), mat_col])
    pack_cols(to_lt, 0, v_cols + [col_of(s, YY), mat_col])
    start1()

    n_block = owner.shape[0]
    earlier = (iota((LANES, LANES), 0) < iota((LANES, LANES), 1)).astype(BF16)
    ones = jnp.ones((LANES, LANES), BF16)
    wanted = c * n_span + sp + (iota((n_z, LANES), 0) - my_z) * SPLIT_CORE
    same = jnp.concatenate(
        [(owner[a : a + 1, :] == wanted).astype(F32) for a in range(n_block)], axis=0
    )
    counts = dot(same.astype(BF16), jnp.concatenate([earlier, ones], axis=1))
    before = jnp.zeros((n_z, LANES), F32)
    per = drive.shape[0]
    chunk = SPLIT_CORE * per
    rank = jnp.full((n_z, LANES), -1.0, F32)
    lane8 = iota((n_z, LANES), 1)
    for a in range(n_block):
        at = slice(a * n_z, (a + 1) * n_z)
        rank_a = jnp.where(same[at] > 0.5, before + counts[at, :LANES], -1.0)
        before = before + counts[at, LANES:]
        ranks[at, :] = rank_a
        for h in range(SPLIT_X_HI):
            to = (a * SPLIT_X_HI + h) * chunk
            by = (to - h * SPLIT_Z * chunk) % LANES + LANES - my_z * chunk
            moved = pltpu.roll(rank_a, lax.rem(by, LANES), 1)
            rank = jnp.where(jnp.logical_and(lane8 >= to, lane8 < to + chunk), moved, rank)
    slot_ids = fiota((SLOTS, LANES), 0)
    for h in range(2):
        for k in range(n_z):
            at = (h * n_z + k) * 8
            ids = slot_ids[h * 8 : (h + 1) * 8]
            taken[at : at + 8, :] = (rank[k : k + 1, :] == ids).astype(F32)
    taken_t[...] = jnp.transpose(taken[...])
    first_x = jnp.zeros((SLOTS, LANES), F32)
    first_y = jnp.zeros((SLOTS, LANES), F32)
    shift = size_y.bit_length() - 1
    for a in range(n_block):
        anchor = cells[0:1, a * LANES : (a + 1) * LANES]
        hit = ranks[pl.ds(a * n_z + my_z, 1), :] == slot_ids
        first_x = first_x + jnp.where(hit, (anchor >> shift).astype(F32), 0.0)
        first_y = first_y + jnp.where(hit, (anchor & (size_y - 1)).astype(F32), 0.0)
    first_x = jnp.sum(first_x, axis=1, keepdims=True)
    first_y = jnp.sum(first_y, axis=1, keepdims=True)
    low = iota((8, LANES), 1) < 64
    cell_id = iota((8, LANES), 1) & 63
    slot_x[...] = jnp.where(low, first_x[0:8], first_x[8:16]) + (cell_id >> 3).astype(F32)
    slot_y[...] = jnp.where(low, first_y[0:8], first_y[8:16]) + (cell_id & 7).astype(F32)
    y_ids = fiota((size_y, LANES), 0)
    for t in range(8):
        onehot_y[:, t * LANES : (t + 1) * LANES] = (
            (slot_y[t : t + 1, :] == y_ids).astype(F32).astype(BF16)
        )
    x_ids = fiota((size_x, LANES), 0)

    def table(kind, index):
        out = jnp.full(kind.shape, DT * moduli[0, index], F32)
        for m in range(1, 4):
            out = jnp.where(kind == m, DT * moduli[m, index], out)
        return out

    def coef_layer(z, _):
        kind = mat[z]
        for k in range(10):
            coef[k, z] = table(kind, k)
        return 0

    lax.fori_loop(0, depth, coef_layer, 0)

    wait_all(gathered, n_p - 1, group_recv, 0)
    for i in range(n_p):
        rows1[i * per : (i + 1) * per, :] = gathered[i]
    pick = taken[...].astype(BF16)
    routes = sum(dot(pick, part) for part in split3(rows1[...]))
    early, late = routes[: n_z * 8], routes[n_z * 8 :]
    low_all = iota((n_z * 8, LANES), 1) < 64
    own = pl.ds(pl.multiple_of(my_z * 8, 8), 8)
    for step in range(2):
        if step == 0:
            send2[0] = jnp.where(low_all, early, pltpu.roll(late, 64, 1))
        else:
            send2[1] = jnp.where(low_all, pltpu.roll(early, 64, 1), late)
        for i in range(1, n_z):
            source, target = send2.at[step], routed2.at[step]
            send(block(source, xor(my_z, i), 8), block(target, my_z, 8), z_partner(i), 1 + step).start()
        routed2[step, own, :] = send2[step, own, :]

    def along_x(field, by, edge_row):
        if by > 0:
            return jnp.where(row == 0, edge_row, pltpu.roll(field, 1, 0))
        return jnp.where(row == size_x - 1, edge_row, pltpu.roll(field, size_x - 1, 0))

    def along_y(field, by, edge_col):
        if by > 0:
            moved = pltpu.roll(field, 1, 1)
            head = jnp.where(lane == 0, edge_col, moved[:, :LANES])
            return jnp.concatenate([head, moved[:, LANES:]], axis=1)
        moved = pltpu.roll(field, size_y - 1, 1)
        tail = jnp.where(lane == LANES - 1, edge_col, moved[:, half:])
        return jnp.concatenate([moved[:, :half], tail], axis=1)

    def first_lane(ref, field, z):
        return pltpu.roll(ref[...], lax.rem(2 * LANES - (field * depth + z), LANES), 1)

    def last_lane(ref, field, z):
        return pltpu.roll(ref[...], lax.rem(2 * LANES - 1 - (field * depth + z), LANES), 1)

    bottom, top = 0, depth - 1

    def stress_layer(z, up_ref, dn_ref, lt_ref, rt_ref):
        is_bottom, is_top = isinstance(z, int) and z == bottom, isinstance(z, int) and z == top
        vx, vy, vz = v[0, z], v[1, z], v[2, z]
        zz = vz if is_bottom else vz - v[2, z - 1]
        zy = -vy if is_top else v[1, z + 1] - vy
        zx = -vx if is_top else v[0, z + 1] - vx
        xx = vx - along_x(vx, 1, up_ref[pl.ds(z, 1), :])
        yy = vy - along_y(vy, 1, first_lane(lt_ref, 1, z))
        yz = zy + (along_y(vz, -1, last_lane(rt_ref, 2, z)) - vz)
        xz = zx + (along_x(vz, -1, dn_ref[pl.ds(2 * depth + z, 1), :]) - vz)
        xy = (along_y(vx, -1, last_lane(rt_ref, 0, z)) - vx) + (
            along_x(vy, -1, dn_ref[pl.ds(depth + z, 1), :]) - vy
        )
        s[XX, z] += coef[C11, z] * xx + coef[C12, z] * yy + coef[C13, z] * zz
        s[YY, z] += coef[C12, z] * xx + coef[C22, z] * yy + coef[C23, z] * zz
        s[ZZ, z] += coef[C13, z] * xx + coef[C23, z] * yy + coef[C33, z] * zz
        s[YZ, z] += coef[C44, z] * yz
        s[XZ, z] += coef[C55, z] * xz
        s[XY, z] += coef[C66, z] * xy

    def velocity_layer(z):
        is_bottom, is_top = isinstance(z, int) and z == bottom, isinstance(z, int) and z == top
        sxx, syy, szz = s[XX, z], s[YY, z], s[ZZ, z]
        syz, sxz, sxy = s[YZ, z], s[XZ, z], s[XY, z]
        ax = (
            (along_x(sxx, -1, halo_row[0, pl.ds(z, 1), :]) - sxx)
            + (sxy - along_y(sxy, 1, first_lane(halo_col.at[1], 0, z)))
            + (sxz if is_bottom else sxz - s[XZ, z - 1])
        )
        ay = (
            (sxy - along_x(sxy, 1, halo_row[1, pl.ds(z, 1), :]))
            + (along_y(syy, -1, last_lane(halo_col.at[0], 0, z)) - syy)
            + (syz if is_bottom else syz - s[YZ, z - 1])
        )
        az = (
            (sxz - along_x(sxz, 1, halo_row[2, pl.ds(z, 1), :]))
            + (syz - along_y(syz, 1, first_lane(halo_col.at[2], 0, z)))
            + (-szz if is_top else s[ZZ, z + 1] - szz)
        )
        b = coef[BUOY, z]
        v[0, z] += b * ax
        v[1, z] += b * ay
        v[2, z] += b * az

    wide = (depth, size_y)
    wide_lane = iota(wide, 1)
    wide_z = iota(wide, 0)

    def below_z(f):
        return jnp.where(wide_z == 0, 0.0, pltpu.roll(f, 1, 0))

    def above_z(f):
        return jnp.where(wide_z == depth - 1, 0.0, pltpu.roll(f, depth - 1, 0))

    def lane_below_z(f):
        return jnp.where(lane == 0, 0.0, pltpu.roll(f, 1, 1))

    def lane_above_z(f):
        return jnp.where(lane == depth - 1, 0.0, pltpu.roll(f, LANES - 1, 1))

    def to_lanes(corner, at):
        col = jnp.broadcast_to(corner[:, at : at + 1], (depth, LANES))
        here = iota((depth, LANES), 0) == iota((depth, LANES), 1)
        return jnp.sum(jnp.where(here, col, 0.0), axis=0, keepdims=True)

    def lanes_of(ref, field):
        if field == 0:
            return ref[...]
        return pltpu.roll(ref[...], LANES - field * depth, 1)

    narrow_row = iota((size_x, LANES), 0)

    def halo_stress(up_ref, dn_ref, lt_ref, rt_ref, cup, cdn, my_up, my_dn, my_lt, my_rt):
        def rows(ref, k):
            return ref[k * depth : (k + 1) * depth, :]

        vx, vy, vz = rows(dn_ref, 0), rows(dn_ref, 1), rows(dn_ref, 2)
        corner = jnp.broadcast_to(cdn[:, LANES - 1 : LANES], wide)
        vy_back = jnp.where(wide_lane == 0, corner, pltpu.roll(vy, 1, 1))
        halo_row[0] += (
            hcoef_row[0] * (vx - rows(my_dn, 0))
            + hcoef_row[1] * (vy - vy_back)
            + hcoef_row[2] * (vz - below_z(vz))
        )
        vx, vy, vz = rows(up_ref, 0), rows(up_ref, 1), rows(up_ref, 2)
        corner = jnp.broadcast_to(cup[:, 0:1], wide)
        vx_next = jnp.where(wide_lane == size_y - 1, corner, pltpu.roll(vx, size_y - 1, 1))
        halo_row[1] += hcoef_row[3] * ((vx_next - vx) + (rows(my_up, 1) - vy))
        halo_row[2] += hcoef_row[4] * ((above_z(vx) - vx) + (rows(my_up, 2) - vz))
        vx, vy, vz = lanes_of(rt_ref, 0), lanes_of(rt_ref, 1), lanes_of(rt_ref, 2)
        vx_back = jnp.where(narrow_row == 0, to_lanes(cup, 0), pltpu.roll(vx, 1, 0))
        halo_col[0] += (
            hcoef_col[0] * (vx - vx_back)
            + hcoef_col[1] * (vy - lanes_of(my_rt, 1))
            + hcoef_col[2] * (vz - lane_below_z(vz))
        )
        vx, vy, vz = lanes_of(lt_ref, 0), lanes_of(lt_ref, 1), lanes_of(lt_ref, 2)
        vy_next = jnp.where(
            narrow_row == size_x - 1, to_lanes(cdn, LANES - 1), pltpu.roll(vy, size_x - 1, 0)
        )
        halo_col[1] += hcoef_col[3] * ((lanes_of(my_lt, 0) - vx) + (vy_next - vy))
        halo_col[2] += hcoef_col[4] * ((lane_above_z(vy) - vy) + (lanes_of(my_lt, 2) - vz))

    arrive1()
    kind = from_dn[4 * depth : 5 * depth, :]
    inside = has_dn.astype(F32)
    for k, index in enumerate((C11, C12, C13)):
        hcoef_row[k] = table(kind, index) * inside
    kind = from_up[5 * depth : 6 * depth, :]
    inside = has_up.astype(F32)
    for k, index in enumerate((C66, C55)):
        hcoef_row[3 + k] = table(kind, index) * inside
    kind = lanes_of(from_rt, 4)
    inside = has_rt.astype(F32)
    for k, index in enumerate((C12, C22, C23)):
        hcoef_col[k] = table(kind, index) * inside
    kind = lanes_of(from_lt, 5)
    inside = has_lt.astype(F32)
    for k, index in enumerate((C66, C44)):
        hcoef_col[3 + k] = table(kind, index) * inside
    halo_row[0] = from_dn[3 * depth : 4 * depth, :]
    halo_row[1] = from_up[3 * depth : 4 * depth, :]
    halo_row[2] = from_up[4 * depth : 5 * depth, :]
    halo_col[0] = lanes_of(from_rt, 3)
    halo_col[1] = lanes_of(from_lt, 3)
    halo_col[2] = lanes_of(from_lt, 4)

    def stress_first(z, _):
        stress_layer(z, from_up, from_dn, from_lt, from_rt)
        return 0

    def velocity_body(z, _):
        velocity_layer(z)
        return 0

    stress_first(bottom, 0)
    lax.fori_loop(bottom + 1, top, stress_first, 0)
    stress_first(top, 0)
    halo_stress(
        from_up, from_dn, from_lt, from_rt, corner_up, corner_dn, to_up, to_dn, to_lt, to_rt
    )
    velocity_layer(bottom)
    lax.fori_loop(bottom + 1, top, velocity_body, 0)
    velocity_layer(top)

    pack_rows(vto_dn, size_x - 1, v_rows)
    pack_rows(vto_up, 0, v_rows)
    pack_cols(vto_rt, size_y - 1, v_cols)
    pack_cols(vto_lt, 0, v_cols)
    start2()

    def take_force(step):
        wait_all(routed2.at[step], (n_z - 1) * 8, group_recv, 1 + step)
        out = routed2[step, 0:8, :]
        for k in range(1, n_z):
            out = out + routed2[step, k * 8 : (k + 1) * 8, :]
        return out

    def in_slot(t):
        return slot_x[t : t + 1, :] == x_ids

    def force_plane(step):
        force = take_force(step)
        wide_force = jnp.concatenate(
            [jnp.where(in_slot(t), force[t : t + 1, :], 0.0) for t in range(8)], axis=1
        )
        parts = jnp.concatenate(split3(wide_force), axis=0)
        got = dot(parts, onehot_y[...], ((1,), (1,)))
        return coef[BUOY, top] * (got[:size_x] + got[size_x : 2 * size_x] + got[2 * size_x :])

    def send_records(step, values):
        rec_send[step] = values
        for i in range(1, n_z):
            send(rec_send.at[step], block(rec_rows.at[step], my_z, 8), z_partner(i), 3 + step).start()
        rec_rows[step, own, :] = values

    def sample():
        got = dot(jnp.concatenate(split3(v[2, top]), axis=0), onehot_y[...])
        got = got[:size_x] + got[size_x : 2 * size_x] + got[2 * size_x :]
        out = []
        for t in range(8):
            chosen = jnp.where(in_slot(t), got[:, t * LANES : (t + 1) * LANES], 0.0)
            out.append(jnp.sum(chosen, axis=0, keepdims=True))
        return jnp.concatenate(out, axis=0)

    v[2, top] += force_plane(0)
    tto_dn[...] = jnp.broadcast_to(v[2, top, size_x - 1 : size_x, :], (depth, size_y))
    tto_up[...] = jnp.broadcast_to(v[2, top, 0:1, :], (depth, size_y))
    tto_rt[...] = v[2, top, :, half:]
    tto_lt[...] = v[2, top, :, :LANES]
    start3()
    send_records(0, sample())
    plane[...] = force_plane(1)

    arrive2()

    def stress_second(z, _):
        stress_layer(z, vfrom_up, vfrom_dn, vfrom_lt, vfrom_rt)
        return 0

    stress_second(bottom, 0)
    lax.fori_loop(bottom + 1, top, stress_second, 0)
    arrive3()
    leave2()
    top_row = 2 * depth + top
    vfrom_up[top_row : top_row + 1, :] = tfrom_up[0:1, :]
    vfrom_dn[top_row : top_row + 1, :] = tfrom_dn[0:1, :]
    vfrom_rt[...] = jnp.where(
        lane == top_row, pltpu.roll(tfrom_rt[...], top_row, 1), vfrom_rt[...]
    )
    vfrom_lt[...] = jnp.where(
        lane == top_row, pltpu.roll(tfrom_lt[...], top_row + 1, 1), vfrom_lt[...]
    )
    vto_up[top_row : top_row + 1, :] = v[2, top, 0:1, :]
    vto_lt[...] = jnp.where(
        lane == top_row, pltpu.roll(v[2, top, :, :LANES], top_row, 1), vto_lt[...]
    )
    stress_layer(top, vfrom_up, vfrom_dn, vfrom_lt, vfrom_rt)
    halo_stress(
        vfrom_up,
        vfrom_dn,
        vfrom_lt,
        vfrom_rt,
        vcorner_up,
        vcorner_dn,
        vto_up,
        vto_dn,
        vto_lt,
        vto_rt,
    )
    velocity_layer(top)
    v[2, top] += plane[...]

    send_records(1, sample())

    velocity_layer(bottom)
    lax.fori_loop(bottom + 1, top, velocity_body, 0)

    wait_all(rec_rows.at[0], (n_z - 1) * 8, group_recv, 3)
    early = rec_rows[0]
    pick = taken_t[...].astype(BF16)
    wait_all(rec_rows.at[1], (n_z - 1) * 8, group_recv, 4)
    late = rec_rows[1]
    both = jnp.concatenate(
        [
            jnp.where(low_all, early, pltpu.roll(late, 64, 1)),
            jnp.where(low_all, pltpu.roll(early, 64, 1), late),
        ],
        axis=0,
    )
    back = sum(dot(pick, part) for part in split3(both))
    for i in range(n_p):
        rec_back[i] = back[i * per : (i + 1) * per, :]
    for i in range(1, n_p):
        send(rec_back.at[xor(my_p, i)], rec_got.at[my_p], p_partner(i), 5).start()
    rec_got[my_p] = rec_back[my_p]
    wait_all(rec_got, n_p - 1, group_recv, 5)
    parts = [rec_got[i] for i in range(n_p)]
    while len(parts) > 1:
        parts = [a + b for a, b in zip(parts[::2], parts[1::2])]
    rec_out[...] = parts[0]

    leave1()
    leave3()
    wait_all(gathered, n_p - 1, group_send, 0)
    for step in range(2):
        wait_all(routed2.at[step], (n_z - 1) * 8, group_send, 1 + step)
        wait_all(rec_rows.at[step], (n_z - 1) * 8, group_send, 3 + step)
    wait_all(rec_got, n_p - 1, group_send, 5)


def hand_over(v, s, rec, vel_out, str_out, rec_out, sem):
    pairs = [(v, vel_out), (s, str_out), (rec, rec_out)]
    copies = [pltpu.make_async_copy(a, b, sem.at[i]) for i, (a, b) in enumerate(pairs)]
    for copy in copies:
        copy.start()
    for copy in copies:
        copy.wait()


def solution(mesh):
    n_chord, n_span = mesh.shape["chord"], mesh.shape["span"]

    def local(velocity, stress, material, moduli, drive, owner, cells):
        _, depth, size_x, size_y = velocity.shape
        per = drive.shape[0]

        def mem(*shape):
            return pltpu.VMEM(shape, F32)

        def edges(rows_dn, rows_up):
            return [
                mem(rows_dn * depth, size_y),
                mem(rows_up * depth, size_y),
                mem(size_x, LANES),
                mem(size_x, LANES),
            ]

        layer = (size_x, size_y)
        vmem = pl.BlockSpec(memory_space=pltpu.VMEM)
        slots = SPLIT_Z * SLOTS
        n_p = n_chord * SPLIT_X_HI * SPLIT_CORE
        inputs = (velocity, stress, material, moduli, drive, owner.reshape(-1, LANES), cells.T)
        state = pl.pallas_call(
            functools.partial(kernel, n_chord, n_span),
            out_shape=(
                jax.ShapeDtypeStruct(velocity.shape, F32),
                jax.ShapeDtypeStruct(stress.shape, F32),
                jax.ShapeDtypeStruct(drive.shape, F32),
            ),
            in_specs=[pl.BlockSpec(memory_space=pltpu.HBM)] * 7,
            out_specs=(vmem, vmem, vmem),
            scratch_shapes=[
                pltpu.VMEM((depth, *layer), jnp.int32),
                pltpu.SMEM(moduli.shape, F32),
                mem(*drive.shape),
                pltpu.VMEM((owner.size // LANES, LANES), jnp.int32),
                pltpu.VMEM((8, owner.size), jnp.int32),
                mem(10, depth, *layer),
                pltpu.VMEM((size_y, 8 * LANES), BF16),
                mem(8, LANES),
                mem(8, LANES),
                mem(*layer),
                mem(owner.size // LANES * SPLIT_Z, LANES),
                mem(slots, LANES),
                mem(LANES, slots),
                mem(n_p, per, LANES),
                mem(LANES, LANES),
                mem(2, slots // 2, LANES),
                mem(2, slots // 2, LANES),
                mem(2, 8, LANES),
                mem(2, slots // 2, LANES),
                mem(n_p, per, LANES),
                mem(n_p, per, LANES),
                *edges(6, 5),
                mem(6 * depth, size_y),
                mem(5 * depth, size_y),
                mem(size_x, LANES),
                mem(size_x, LANES),
                mem(depth, LANES),
                mem(depth, LANES),
                *edges(3, 3),
                *edges(3, 3),
                mem(depth, LANES),
                mem(depth, LANES),
                *edges(1, 1),
                *edges(1, 1),
                mem(3, depth, size_y),
                mem(3, size_x, LANES),
                mem(5, depth, size_y),
                mem(5, size_x, LANES),
                pltpu.SemaphoreType.DMA((7,)),
                pltpu.SemaphoreType.DMA((6,)),
                pltpu.SemaphoreType.DMA((6,)),
                pltpu.SemaphoreType.DMA((16,)),
                pltpu.SemaphoreType.DMA((16,)),
            ],
            compiler_params=pltpu.CompilerParams(
                collective_id=0, has_side_effects=True, vmem_limit_bytes=48 * 1024 * 1024
            ),
        )(*(pltpu.with_memory_space_constraint(x, pltpu.HBM) for x in inputs))
        hbm = pl.BlockSpec(memory_space=pltpu.HBM)
        return pl.pallas_call(
            hand_over,
            out_shape=tuple(jax.ShapeDtypeStruct(x.shape, x.dtype) for x in state),
            in_specs=[pl.BlockSpec(memory_space=pl.ANY)] * 3,
            out_specs=(hbm, hbm, hbm),
            scratch_shapes=[pltpu.SemaphoreType.DMA((3,))],
        )(*(pltpu.with_memory_space_constraint(x, pltpu.VMEM) for x in state))

    in_specs = (
        P(None, None, "chord", "span"),
        P(None, None, "chord", "span"),
        P(None, "chord", "span"),
        P(),
        P(("chord", "span"), None),
        P(),
        P(),
    )
    out_specs = (
        P(None, None, "chord", "span"),
        P(None, None, "chord", "span"),
        P(("chord", "span"), None),
    )
    return jax.shard_map(local, mesh=mesh, in_specs=in_specs, out_specs=out_specs, check_vma=False)
```

```python
import functools

import jax
import jax.numpy as jnp
from jax import lax
from jax.experimental import pallas as pl
from jax.experimental.pallas import tpu as pltpu
from jax.sharding import PartitionSpec as P

MESH = pl.DeviceIdType.MESH
F32 = jnp.float32
BF16 = jnp.bfloat16
DT = 0.5
SLOTS = 16
PATCH = 8
LANES = 128
SPLIT_X_HI, SPLIT_Z, SPLIT_CORE = 2, 8, 2
C11, C12, C13, C22, C23, C33, C44, C55, C66, BUOY = range(10)
XX, YY, ZZ, YZ, XZ, XY = range(6)


def iota(shape, dim):
    return lax.broadcasted_iota(jnp.int32, shape, dim)


def fiota(shape, dim):
    return iota(shape, dim).astype(F32)


def split3(x):
    a = x.astype(BF16)
    rest = x - a.astype(F32)
    b = rest.astype(BF16)
    return a, b, (rest - b.astype(F32)).astype(BF16)


def dot(a, b, contract=((1,), (0,))):
    return lax.dot_general(a, b, (contract, ((), ())), preferred_element_type=F32)


def kernel(
    n_chord,
    n_span,
    vel_in,
    str_in,
    mat_in,
    moduli_in,
    drive_in,
    owner_in,
    cells_in,
    v,
    s,
    rec_out,
    mat,
    moduli,
    drive,
    owner,
    cells,
    coef,
    onehot_y,
    slot_x,
    slot_y,
    plane,
    ranks,
    taken,
    taken_t,
    gathered,
    rows1,
    send2,
    routed2,
    send3,
    routed3,
    rec_send,
    rec_rows,
    rec_back,
    rec_got,
    to_dn,
    to_up,
    to_rt,
    to_lt,
    from_up,
    from_dn,
    from_lt,
    from_rt,
    corner_up,
    corner_dn,
    vto_dn,
    vto_up,
    vto_rt,
    vto_lt,
    vfrom_up,
    vfrom_dn,
    vfrom_lt,
    vfrom_rt,
    vcorner_up,
    vcorner_dn,
    aux_t,
    off_y,
    off_x,
    edge_pick,
    halo_row,
    halo_col,
    hcoef_row,
    hcoef_col,
    load_sem,
    group_send,
    group_recv,
    edge_send,
    edge_recv,
):
    c = lax.axis_index("chord")
    sp = lax.axis_index("span")
    depth = vel_in.shape[1]
    size_x = vel_in.shape[2]
    size_y = vel_in.shape[3]
    half = size_y - LANES
    n_z = SPLIT_Z
    n_p = n_chord * SPLIT_X_HI * SPLIT_CORE
    my_z = lax.rem(lax.div(sp, SPLIT_CORE), SPLIT_Z)
    x_hi = lax.div(sp, SPLIT_Z * SPLIT_CORE)
    my_p = (c * SPLIT_X_HI + x_hi) * SPLIT_CORE + lax.rem(sp, SPLIT_CORE)
    xor = jnp.bitwise_xor

    def p_partner(i):
        core, high, to_c = i % SPLIT_CORE, i // SPLIT_CORE % SPLIT_X_HI, i // SPLIT_CORE // SPLIT_X_HI
        return xor(c, to_c), xor(sp, high * SPLIT_Z * SPLIT_CORE + core)

    def z_partner(i):
        return c, xor(sp, i * SPLIT_CORE)

    has_up, has_dn = c > 0, c < n_chord - 1
    has_lt, has_rt = sp > 0, sp < n_span - 1
    diag_up = jnp.logical_and(has_up, has_rt)
    diag_dn = jnp.logical_and(has_dn, has_lt)

    pairs = [
        (drive_in, drive),
        (vel_in, v),
        (str_in, s),
        (mat_in, mat),
        (owner_in, owner),
        (cells_in.at[pl.ds(0, 8)], cells),
        (moduli_in, moduli),
    ]
    loads = [pltpu.make_async_copy(a, b, load_sem.at[i]) for i, (a, b) in enumerate(pairs)]
    for load in loads:
        load.start()

    barrier = pltpu.get_barrier_semaphore()

    def greet(to_c, to_s):
        pl.semaphore_signal(barrier, inc=1, device_id=(to_c, to_s), device_id_type=MESH)

    ring = (0, 1, 2, 1)

    def p_hops(i):
        core, high, to_c = i % SPLIT_CORE, i // SPLIT_CORE % SPLIT_X_HI, i // SPLIT_CORE // SPLIT_X_HI
        return 4 * (ring[2 * high + to_c % 2] + ring[to_c // 2 % 4]) + core

    p_order = sorted(range(1, n_p), key=p_hops, reverse=True)
    z_order = sorted(range(1, n_z), key=lambda i: (0, 1, 2, 3, 4, 3, 2, 3)[i], reverse=True)
    for i in p_order:
        greet(*p_partner(i))
    for i in z_order:
        greet(*z_partner(i))
    sides = [
        (has_up, (c - 1, sp)),
        (has_dn, (c + 1, sp)),
        (has_lt, (c, sp - 1)),
        (has_rt, (c, sp + 1)),
        (diag_up, (c - 1, sp + 1)),
        (diag_dn, (c + 1, sp - 1)),
    ]
    for there, to in sides:
        pl.when(there)(functools.partial(greet, *to))

    @pl.when(jnp.logical_not(has_up))
    def _():
        for ref in (from_up, vfrom_up):
            ref[...] = jnp.zeros_like(ref)

    @pl.when(jnp.logical_not(has_dn))
    def _():
        for ref in (from_dn, vfrom_dn):
            ref[...] = jnp.zeros_like(ref)

    @pl.when(jnp.logical_not(has_lt))
    def _():
        for ref in (from_lt, vfrom_lt):
            ref[...] = jnp.zeros_like(ref)

    @pl.when(jnp.logical_not(has_rt))
    def _():
        for ref in (from_rt, vfrom_rt):
            ref[...] = jnp.zeros_like(ref)

    @pl.when(jnp.logical_not(diag_up))
    def _():
        for ref in (corner_up, vcorner_up):
            ref[...] = jnp.zeros_like(ref)

    @pl.when(jnp.logical_not(diag_dn))
    def _():
        for ref in (corner_dn, vcorner_dn):
            ref[...] = jnp.zeros_like(ref)

    pl.semaphore_wait(
        barrier,
        n_p + n_z - 2 + sum(there.astype(jnp.int32) for there, _ in sides),
    )

    def send(source, target, to, sem):
        return pltpu.make_async_remote_copy(
            src_ref=source,
            dst_ref=target,
            send_sem=group_send.at[sem],
            recv_sem=group_recv.at[sem],
            device_id=to,
            device_id_type=MESH,
        )

    def wait_all(ref, count, sems, sem):
        if count:
            part = ref.at[pl.ds(0, count)]
            pltpu.make_async_copy(part, part, sems.at[sem]).wait()

    def block(ref, index, count):
        return ref.at[pl.ds(pl.multiple_of(index * count, count), count)]

    loads[0].wait()
    for i in p_order:
        send(drive, gathered.at[my_p], p_partner(i), 0).start()
    gathered[my_p] = drive[...]

    def edge(source, target, to, index):
        return pltpu.make_async_remote_copy(
            src_ref=source,
            dst_ref=target,
            send_sem=edge_send.at[index],
            recv_sem=edge_recv.at[index],
            device_id=to,
            device_id_type=MESH,
        )

    up, dn, lt, rt = (c - 1, sp), (c + 1, sp), (c, sp - 1), (c, sp + 1)

    def exchange(first, up_src, dn_src, lt_src, rt_src, up_dst, dn_dst, lt_dst, rt_dst, corners):
        moves = [
            (has_up, has_dn, edge(up_src, dn_dst, up, first)),
            (has_dn, has_up, edge(dn_src, up_dst, dn, first + 1)),
            (has_lt, has_rt, edge(lt_src, rt_dst, lt, first + 2)),
            (has_rt, has_lt, edge(rt_src, lt_dst, rt, first + 3)),
        ]
        corner_from_dn, corner_from_up = corners
        vy_corner = up_src.at[pl.ds(depth, depth), pl.ds(half, LANES)]
        vx_corner = dn_src.at[pl.ds(0, depth), pl.ds(0, LANES)]
        moves += [
            (diag_up, diag_dn, edge(vy_corner, corner_from_dn, (c - 1, sp + 1), first + 4)),
            (diag_dn, diag_up, edge(vx_corner, corner_from_up, (c + 1, sp - 1), first + 5)),
        ]

        def start():
            for goes, _, copy in moves:
                pl.when(goes)(copy.start)

        def arrive():
            for _, comes, copy in moves:
                pl.when(comes)(copy.wait_recv)

        def leave():
            for goes, _, copy in moves:
                pl.when(goes)(copy.wait_send)

        return start, arrive, leave

    start1, arrive1, leave1 = exchange(
        0, to_up, to_dn, to_lt, to_rt, from_up, from_dn, from_lt, from_rt, (corner_dn, corner_up)
    )
    start2, arrive2, leave2 = exchange(
        6, vto_up, vto_dn, vto_lt, vto_rt, vfrom_up, vfrom_dn, vfrom_lt, vfrom_rt, (vcorner_dn, vcorner_up)
    )

    def pack_rows(ref, row, fields):
        for z in range(depth):
            for k, read in enumerate(fields):
                ref[k * depth + z : k * depth + z + 1, :] = read(z, row)

    lane = iota((size_x, LANES), 1)
    row = iota((size_x, size_y), 0)

    def pack_cols(ref, column, fields):
        base = 0 if column == 0 else half
        at = column - base

        acc = jnp.zeros((size_x, LANES), F32)
        for z in range(depth):
            for k, read in enumerate(fields):
                to = k * depth + z
                by = (to + LANES - at) % LANES
                tile = read(z, base)
                moved = pltpu.roll(tile, by, 1) if by else tile
                acc = jnp.where(lane == to, moved, acc)
        ref[...] = acc

    def row_of(ref, comp):
        return lambda z, r: ref[comp, z, r : r + 1, :]

    def col_of(ref, comp):
        return lambda z, base: ref[comp, z, :, base : base + LANES]

    def mat_row(z, r):
        return mat[z, r : r + 1, :].astype(F32)

    def mat_col(z, base):
        return mat[z, :, base : base + LANES].astype(F32)

    v_rows = [row_of(v, k) for k in range(3)]
    v_cols = [col_of(v, k) for k in range(3)]

    for load in loads[1:]:
        load.wait()
    pack_rows(to_dn, size_x - 1, v_rows + [row_of(s, XY), row_of(s, XZ), mat_row])
    pack_rows(to_up, 0, v_rows + [row_of(s, XX), mat_row])
    pack_cols(to_rt, size_y - 1, v_cols + [col_of(s, XY), col_of(s, YZ), mat_col])
    pack_cols(to_lt, 0, v_cols + [col_of(s, YY), mat_col])
    start1()

    n_block = owner.shape[0]
    earlier = (iota((LANES, LANES), 0) < iota((LANES, LANES), 1)).astype(BF16)
    ones = jnp.ones((LANES, LANES), BF16)
    wanted = c * n_span + sp + (iota((n_z, LANES), 0) - my_z) * SPLIT_CORE
    same = jnp.concatenate(
        [(owner[a : a + 1, :] == wanted).astype(F32) for a in range(n_block)], axis=0
    )
    counts = dot(same.astype(BF16), jnp.concatenate([earlier, ones], axis=1))
    before = jnp.zeros((n_z, LANES), F32)
    per = drive.shape[0]
    chunk = SPLIT_CORE * per
    rank = jnp.full((n_z, LANES), -1.0, F32)
    lane8 = iota((n_z, LANES), 1)
    shift = size_y.bit_length() - 1
    aux = jnp.zeros((8, LANES), F32)
    aux_lane, aux_row = iota((8, LANES), 1), iota((8, LANES), 0)
    for a in range(n_block):
        at = slice(a * n_z, (a + 1) * n_z)
        rank_a = jnp.where(same[at] > 0.5, before + counts[at, :LANES], -1.0)
        before = before + counts[at, LANES:]
        ranks[at, :] = rank_a
        anchor = cells[0:1, a * LANES : (a + 1) * LANES]
        fields = (owner[a : a + 1, :], anchor >> shift, anchor & (size_y - 1))
        aux_a = jnp.zeros((8, LANES), F32)
        for k, field in enumerate(fields):
            aux_a = jnp.where(aux_row == k, field.astype(F32), aux_a)
        for h in range(SPLIT_X_HI):
            to = (a * SPLIT_X_HI + h) * chunk
            by = (to - h * SPLIT_Z * chunk) % LANES + LANES - my_z * chunk
            moved = pltpu.roll(rank_a, lax.rem(by, LANES), 1)
            rank = jnp.where(jnp.logical_and(lane8 >= to, lane8 < to + chunk), moved, rank)
            moved = pltpu.roll(aux_a, lax.rem(by, LANES), 1)
            aux = jnp.where(jnp.logical_and(aux_lane >= to, aux_lane < to + chunk), moved, aux)
    slot_ids = fiota((SLOTS, LANES), 0)
    for h in range(2):
        for k in range(n_z):
            at = (h * n_z + k) * 8
            ids = slot_ids[h * 8 : (h + 1) * 8]
            taken[at : at + 8, :] = (rank[k : k + 1, :] == ids).astype(F32)
    side_row = iota((n_z * 8, LANES), 0)
    side = side_row & 7
    to_z = side_row >> 3
    to_span = sp + (to_z - my_z) * SPLIT_CORE
    is_dn = jnp.logical_and((side & 1) == 0, side < 4)
    is_up = jnp.logical_and((side & 1) == 1, side < 4)
    is_rt = jnp.logical_and(side == 4, to_span < n_span - 1)
    is_lt = jnp.logical_and(side == 5, to_span > 0)
    whose = (c * n_span + to_span).astype(F32)
    at_owner, at_x, at_y = aux[0:1, :], aux[1:2, :], aux[2:3, :]
    reach = PATCH - 1
    edge_pick[...] = jnp.where(
        is_dn,
        jnp.logical_and(at_owner == whose + n_span, at_x == 0).astype(F32),
        jnp.where(
            is_up,
            jnp.logical_and(at_owner == whose - n_span, at_x == size_x - 1 - reach).astype(F32),
            jnp.where(
                is_rt,
                jnp.logical_and(at_owner == whose + 1, at_y == 0).astype(F32),
                jnp.where(
                    is_lt,
                    jnp.logical_and(at_owner == whose - 1, at_y == size_y - 1 - reach).astype(F32),
                    0.0,
                ),
            ),
        ),
    )
    aux_t[...] = jnp.transpose(jnp.concatenate([aux, jnp.zeros((LANES - 8, LANES), F32)], axis=0))
    off_x[...] = fiota((LANES, LANES), 1) - aux_t[:, 1:2]
    off_y[...] = fiota((LANES, size_y), 1) - aux_t[:, 2:3]

    taken_t[...] = jnp.transpose(taken[...])
    first_x = jnp.zeros((SLOTS, LANES), F32)
    first_y = jnp.zeros((SLOTS, LANES), F32)
    for a in range(n_block):
        anchor = cells[0:1, a * LANES : (a + 1) * LANES]
        hit = ranks[pl.ds(a * n_z + my_z, 1), :] == slot_ids
        first_x = first_x + jnp.where(hit, (anchor >> shift).astype(F32), 0.0)
        first_y = first_y + jnp.where(hit, (anchor & (size_y - 1)).astype(F32), 0.0)
    first_x = jnp.sum(first_x, axis=1, keepdims=True)
    first_y = jnp.sum(first_y, axis=1, keepdims=True)
    low = iota((8, LANES), 1) < 64
    cell_id = iota((8, LANES), 1) & 63
    slot_x[...] = jnp.where(low, first_x[0:8], first_x[8:16]) + (cell_id >> 3).astype(F32)
    slot_y[...] = jnp.where(low, first_y[0:8], first_y[8:16]) + (cell_id & 7).astype(F32)
    y_ids = fiota((size_y, LANES), 0)
    for t in range(8):
        onehot_y[:, t * LANES : (t + 1) * LANES] = (
            (slot_y[t : t + 1, :] == y_ids).astype(F32).astype(BF16)
        )
    x_ids = fiota((size_x, LANES), 0)

    def table(kind, index):
        out = jnp.full(kind.shape, DT * moduli[0, index], F32)
        for m in range(1, 4):
            out = jnp.where(kind == m, DT * moduli[m, index], out)
        return out

    def coef_layer(z, _):
        kind = mat[z]
        for k in range(10):
            coef[k, z] = table(kind, k)
        return 0

    lax.fori_loop(0, depth, coef_layer, 0)

    wait_all(gathered, n_p - 1, group_recv, 0)
    for i in range(n_p):
        rows1[i * per : (i + 1) * per, :] = gathered[i]
    rows = rows1[...]
    at_x0 = aux_t[:, 1:2] == 0.0
    at_y0 = aux_t[:, 2:3] == 0.0
    along_row = jnp.where(at_x0, rows, pltpu.roll(rows, LANES - PATCH * reach, 1))
    along_col = jnp.where(at_y0, rows, pltpu.roll(rows, LANES - reach, 1))
    row_line = jnp.zeros((LANES, size_y), F32)
    col_line = jnp.zeros((LANES, LANES), F32)
    for k in range(PATCH):
        row_line = jnp.where(off_y[...] == k, along_row[:, k : k + 1], row_line)
        col_line = jnp.where(off_x[...] == k, along_col[:, k * PATCH : k * PATCH + 1], col_line)
    lines = jnp.concatenate([row_line, col_line], axis=1)
    pick = edge_pick[...].astype(BF16)
    lines = sum(dot(pick, part) for part in split3(lines))
    lines = jnp.where(
        side < 2, lines[:, :LANES], jnp.where(side < 4, lines[:, LANES:size_y], lines[:, size_y:])
    )
    pick = taken[...].astype(BF16)
    routes = sum(dot(pick, part) for part in split3(rows))
    early, late = routes[: n_z * 8], routes[n_z * 8 :]
    low_all = iota((n_z * 8, LANES), 1) < 64
    own = pl.ds(pl.multiple_of(my_z * 8, 8), 8)
    force0 = jnp.where(low_all, early, pltpu.roll(late, 64, 1))
    for k in range(n_z):
        send2[k, 0:8, :] = force0[k * 8 : (k + 1) * 8]
        send2[k, 8:16, :] = lines[k * 8 : (k + 1) * 8]
    for i in z_order:
        send(send2.at[xor(my_z, i)], routed2.at[my_z], z_partner(i), 1).start()
    routed2[my_z] = send2[my_z]
    send3[...] = jnp.where(low_all, pltpu.roll(early, 64, 1), late)
    for i in z_order:
        send(block(send3, xor(my_z, i), 8), block(routed3, my_z, 8), z_partner(i), 2).start()
    routed3[own, :] = send3[own, :]

    def along_x(field, by, edge_row):
        if by > 0:
            return jnp.where(row == 0, edge_row, pltpu.roll(field, 1, 0))
        return jnp.where(row == size_x - 1, edge_row, pltpu.roll(field, size_x - 1, 0))

    def along_y(field, by, edge_col):
        if by > 0:
            moved = pltpu.roll(field, 1, 1)
            head = jnp.where(lane == 0, edge_col, moved[:, :LANES])
            return jnp.concatenate([head, moved[:, LANES:]], axis=1)
        moved = pltpu.roll(field, size_y - 1, 1)
        tail = jnp.where(lane == LANES - 1, edge_col, moved[:, half:])
        return jnp.concatenate([moved[:, :half], tail], axis=1)

    def first_lane(ref, field, z):
        return pltpu.roll(ref[...], lax.rem(2 * LANES - (field * depth + z), LANES), 1)

    def last_lane(ref, field, z):
        return pltpu.roll(ref[...], lax.rem(2 * LANES - 1 - (field * depth + z), LANES), 1)

    bottom, top = 0, depth - 1

    def stress_layer(z, up_ref, dn_ref, lt_ref, rt_ref):
        is_bottom, is_top = isinstance(z, int) and z == bottom, isinstance(z, int) and z == top
        vx, vy, vz = v[0, z], v[1, z], v[2, z]
        zz = vz if is_bottom else vz - v[2, z - 1]
        zy = -vy if is_top else v[1, z + 1] - vy
        zx = -vx if is_top else v[0, z + 1] - vx
        xx = vx - along_x(vx, 1, up_ref[pl.ds(z, 1), :])
        yy = vy - along_y(vy, 1, first_lane(lt_ref, 1, z))
        yz = zy + (along_y(vz, -1, last_lane(rt_ref, 2, z)) - vz)
        xz = zx + (along_x(vz, -1, dn_ref[pl.ds(2 * depth + z, 1), :]) - vz)
        xy = (along_y(vx, -1, last_lane(rt_ref, 0, z)) - vx) + (
            along_x(vy, -1, dn_ref[pl.ds(depth + z, 1), :]) - vy
        )
        s[XX, z] += coef[C11, z] * xx + coef[C12, z] * yy + coef[C13, z] * zz
        s[YY, z] += coef[C12, z] * xx + coef[C22, z] * yy + coef[C23, z] * zz
        s[ZZ, z] += coef[C13, z] * xx + coef[C23, z] * yy + coef[C33, z] * zz
        s[YZ, z] += coef[C44, z] * yz
        s[XZ, z] += coef[C55, z] * xz
        s[XY, z] += coef[C66, z] * xy

    def velocity_layer(z):
        is_bottom, is_top = isinstance(z, int) and z == bottom, isinstance(z, int) and z == top
        sxx, syy, szz = s[XX, z], s[YY, z], s[ZZ, z]
        syz, sxz, sxy = s[YZ, z], s[XZ, z], s[XY, z]
        ax = (
            (along_x(sxx, -1, halo_row[0, pl.ds(z, 1), :]) - sxx)
            + (sxy - along_y(sxy, 1, first_lane(halo_col.at[1], 0, z)))
            + (sxz if is_bottom else sxz - s[XZ, z - 1])
        )
        ay = (
            (sxy - along_x(sxy, 1, halo_row[1, pl.ds(z, 1), :]))
            + (along_y(syy, -1, last_lane(halo_col.at[0], 0, z)) - syy)
            + (syz if is_bottom else syz - s[YZ, z - 1])
        )
        az = (
            (sxz - along_x(sxz, 1, halo_row[2, pl.ds(z, 1), :]))
            + (syz - along_y(syz, 1, first_lane(halo_col.at[2], 0, z)))
            + (-szz if is_top else s[ZZ, z + 1] - szz)
        )
        b = coef[BUOY, z]
        v[0, z] += b * ax
        v[1, z] += b * ay
        v[2, z] += b * az

    wide = (depth, size_y)
    wide_lane = iota(wide, 1)
    wide_z = iota(wide, 0)

    def below_z(f):
        return jnp.where(wide_z == 0, 0.0, pltpu.roll(f, 1, 0))

    def above_z(f):
        return jnp.where(wide_z == depth - 1, 0.0, pltpu.roll(f, depth - 1, 0))

    def lane_below_z(f):
        return jnp.where(lane == 0, 0.0, pltpu.roll(f, 1, 1))

    def lane_above_z(f):
        return jnp.where(lane == depth - 1, 0.0, pltpu.roll(f, LANES - 1, 1))

    def to_lanes(corner, at):
        col = jnp.broadcast_to(corner[:, at : at + 1], (depth, LANES))
        here = iota((depth, LANES), 0) == iota((depth, LANES), 1)
        return jnp.sum(jnp.where(here, col, 0.0), axis=0, keepdims=True)

    def lanes_of(ref, field):
        if field == 0:
            return ref[...]
        return pltpu.roll(ref[...], LANES - field * depth, 1)

    narrow_row = iota((size_x, LANES), 0)

    def halo_stress(up_ref, dn_ref, lt_ref, rt_ref, cup, cdn, my_up, my_dn, my_lt, my_rt):
        def rows(ref, k):
            return ref[k * depth : (k + 1) * depth, :]

        vx, vy, vz = rows(dn_ref, 0), rows(dn_ref, 1), rows(dn_ref, 2)
        corner = jnp.broadcast_to(cdn[:, LANES - 1 : LANES], wide)
        vy_back = jnp.where(wide_lane == 0, corner, pltpu.roll(vy, 1, 1))
        halo_row[0] += (
            hcoef_row[0] * (vx - rows(my_dn, 0))
            + hcoef_row[1] * (vy - vy_back)
            + hcoef_row[2] * (vz - below_z(vz))
        )
        vx, vy, vz = rows(up_ref, 0), rows(up_ref, 1), rows(up_ref, 2)
        corner = jnp.broadcast_to(cup[:, 0:1], wide)
        vx_next = jnp.where(wide_lane == size_y - 1, corner, pltpu.roll(vx, size_y - 1, 1))
        halo_row[1] += hcoef_row[3] * ((vx_next - vx) + (rows(my_up, 1) - vy))
        halo_row[2] += hcoef_row[4] * ((above_z(vx) - vx) + (rows(my_up, 2) - vz))
        vx, vy, vz = lanes_of(rt_ref, 0), lanes_of(rt_ref, 1), lanes_of(rt_ref, 2)
        vx_back = jnp.where(narrow_row == 0, to_lanes(cup, 0), pltpu.roll(vx, 1, 0))
        halo_col[0] += (
            hcoef_col[0] * (vx - vx_back)
            + hcoef_col[1] * (vy - lanes_of(my_rt, 1))
            + hcoef_col[2] * (vz - lane_below_z(vz))
        )
        vx, vy, vz = lanes_of(lt_ref, 0), lanes_of(lt_ref, 1), lanes_of(lt_ref, 2)
        vy_next = jnp.where(
            narrow_row == size_x - 1, to_lanes(cdn, LANES - 1), pltpu.roll(vy, size_x - 1, 0)
        )
        halo_col[1] += hcoef_col[3] * ((lanes_of(my_lt, 0) - vx) + (vy_next - vy))
        halo_col[2] += hcoef_col[4] * ((lane_above_z(vy) - vy) + (lanes_of(my_lt, 2) - vz))

    arrive1()
    kind = from_dn[4 * depth : 5 * depth, :]
    inside = has_dn.astype(F32)
    for k, index in enumerate((C11, C12, C13)):
        hcoef_row[k] = table(kind, index) * inside
    kind = from_up[5 * depth : 6 * depth, :]
    inside = has_up.astype(F32)
    for k, index in enumerate((C66, C55)):
        hcoef_row[3 + k] = table(kind, index) * inside
    kind = lanes_of(from_rt, 4)
    inside = has_rt.astype(F32)
    for k, index in enumerate((C12, C22, C23)):
        hcoef_col[k] = table(kind, index) * inside
    kind = lanes_of(from_lt, 5)
    inside = has_lt.astype(F32)
    for k, index in enumerate((C66, C44)):
        hcoef_col[3 + k] = table(kind, index) * inside
    halo_row[0] = from_dn[3 * depth : 4 * depth, :]
    halo_row[1] = from_up[3 * depth : 4 * depth, :]
    halo_row[2] = from_up[4 * depth : 5 * depth, :]
    halo_col[0] = lanes_of(from_rt, 3)
    halo_col[1] = lanes_of(from_lt, 3)
    halo_col[2] = lanes_of(from_lt, 4)

    def stress_first(z, _):
        stress_layer(z, from_up, from_dn, from_lt, from_rt)
        return 0

    def velocity_body(z, _):
        velocity_layer(z)
        return 0

    stress_first(bottom, 0)
    lax.fori_loop(bottom + 1, top, stress_first, 0)
    stress_first(top, 0)
    halo_stress(
        from_up, from_dn, from_lt, from_rt, corner_up, corner_dn, to_up, to_dn, to_lt, to_rt
    )
    velocity_layer(bottom)
    lax.fori_loop(bottom + 1, top, velocity_body, 0)
    velocity_layer(top)

    pack_rows(vto_dn, size_x - 1, v_rows)
    pack_rows(vto_up, 0, v_rows)
    pack_cols(vto_rt, size_y - 1, v_cols)
    pack_cols(vto_lt, 0, v_cols)
    start2()

    def in_slot(t):
        return slot_x[t : t + 1, :] == x_ids

    def force_plane(force):
        wide_force = jnp.concatenate(
            [jnp.where(in_slot(t), force[t : t + 1, :], 0.0) for t in range(8)], axis=1
        )
        parts = jnp.concatenate(split3(wide_force), axis=0)
        got = dot(parts, onehot_y[...], ((1,), (1,)))
        return coef[BUOY, top] * (got[:size_x] + got[size_x : 2 * size_x] + got[2 * size_x :])

    def send_records(step, values):
        rec_send[step] = values
        for i in z_order:
            send(rec_send.at[step], block(rec_rows.at[step], my_z, 8), z_partner(i), 3 + step).start()
        rec_rows[step, own, :] = values

    def sample():
        got = dot(jnp.concatenate(split3(v[2, top]), axis=0), onehot_y[...])
        got = got[:size_x] + got[size_x : 2 * size_x] + got[2 * size_x :]
        out = []
        for t in range(8):
            chosen = jnp.where(in_slot(t), got[:, t * LANES : (t + 1) * LANES], 0.0)
            out.append(jnp.sum(chosen, axis=0, keepdims=True))
        return jnp.concatenate(out, axis=0)

    wait_all(routed2, n_z - 1, group_recv, 1)
    force = routed2[0]
    for k in range(1, n_z):
        force = force + routed2[k]
    lines = force[8:16]
    v[2, top] += force_plane(force[0:8])
    send_records(0, sample())

    wait_all(routed3, (n_z - 1) * 8, group_recv, 2)
    force = routed3[0:8, :]
    for k in range(1, n_z):
        force = force + routed3[k * 8 : (k + 1) * 8, :]
    plane[...] = force_plane(force)

    arrive2()

    def stress_second(z, _):
        stress_layer(z, vfrom_up, vfrom_dn, vfrom_lt, vfrom_rt)
        return 0

    stress_second(bottom, 0)
    lax.fori_loop(bottom + 1, top, stress_second, 0)
    leave2()
    top_row = 2 * depth + top

    def buoyancy(kind):
        return table(kind, BUOY)

    wide_line = jnp.concatenate([lines[0:2], lines[2:4]], axis=1)
    kind = from_dn[4 * depth + top : 4 * depth + top + 1, :]
    vfrom_dn[top_row : top_row + 1, :] += buoyancy(kind) * wide_line[0:1]
    kind = from_up[5 * depth + top : 5 * depth + top + 1, :]
    vfrom_up[top_row : top_row + 1, :] += buoyancy(kind) * wide_line[1:2]
    diagonal = iota((size_x, LANES), 0) == lane

    def upright(line):
        return jnp.sum(jnp.where(diagonal, line, 0.0), axis=1, keepdims=True)

    kind = pltpu.roll(from_rt[...], (top_row - 4 * depth - top) % LANES, 1)
    vfrom_rt[...] += jnp.where(lane == top_row, buoyancy(kind) * upright(lines[4:5]), 0.0)
    kind = pltpu.roll(from_lt[...], (top_row - 5 * depth - top) % LANES, 1)
    vfrom_lt[...] += jnp.where(lane == top_row, buoyancy(kind) * upright(lines[5:6]), 0.0)
    vto_up[top_row : top_row + 1, :] = v[2, top, 0:1, :]
    vto_lt[...] = jnp.where(
        lane == top_row, pltpu.roll(v[2, top, :, :LANES], top_row, 1), vto_lt[...]
    )
    stress_layer(top, vfrom_up, vfrom_dn, vfrom_lt, vfrom_rt)
    halo_stress(
        vfrom_up,
        vfrom_dn,
        vfrom_lt,
        vfrom_rt,
        vcorner_up,
        vcorner_dn,
        vto_up,
        vto_dn,
        vto_lt,
        vto_rt,
    )
    velocity_layer(top)
    v[2, top] += plane[...]

    send_records(1, sample())

    velocity_layer(bottom)
    lax.fori_loop(bottom + 1, top, velocity_body, 0)

    wait_all(rec_rows.at[0], (n_z - 1) * 8, group_recv, 3)
    early = rec_rows[0]
    pick = taken_t[...].astype(BF16)
    wait_all(rec_rows.at[1], (n_z - 1) * 8, group_recv, 4)
    late = rec_rows[1]
    both = jnp.concatenate(
        [
            jnp.where(low_all, early, pltpu.roll(late, 64, 1)),
            jnp.where(low_all, pltpu.roll(early, 64, 1), late),
        ],
        axis=0,
    )
    back = sum(dot(pick, part) for part in split3(both))
    for i in range(n_p):
        rec_back[i] = back[i * per : (i + 1) * per, :]
    for i in p_order:
        send(rec_back.at[xor(my_p, i)], rec_got.at[my_p], p_partner(i), 5).start()
    rec_got[my_p] = rec_back[my_p]
    wait_all(rec_got, n_p - 1, group_recv, 5)
    parts = [rec_got[i] for i in range(n_p)]
    while len(parts) > 1:
        parts = [a + b for a, b in zip(parts[::2], parts[1::2])]
    rec_out[...] = parts[0]

    leave1()
    wait_all(gathered, n_p - 1, group_send, 0)
    wait_all(routed2, n_z - 1, group_send, 1)
    wait_all(routed3, (n_z - 1) * 8, group_send, 2)
    for step in range(2):
        wait_all(rec_rows.at[step], (n_z - 1) * 8, group_send, 3 + step)
    wait_all(rec_got, n_p - 1, group_send, 5)


def hand_over(v, s, rec, vel_out, str_out, rec_out, sem):
    pairs = [(v, vel_out), (s, str_out), (rec, rec_out)]
    copies = [pltpu.make_async_copy(a, b, sem.at[i]) for i, (a, b) in enumerate(pairs)]
    for copy in copies:
        copy.start()
    for copy in copies:
        copy.wait()


def solution(mesh):
    n_chord, n_span = mesh.shape["chord"], mesh.shape["span"]

    def local(velocity, stress, material, moduli, drive, owner, cells):
        _, depth, size_x, size_y = velocity.shape
        per = drive.shape[0]

        def mem(*shape):
            return pltpu.VMEM(shape, F32)

        def edges(rows_dn, rows_up):
            return [
                mem(rows_dn * depth, size_y),
                mem(rows_up * depth, size_y),
                mem(size_x, LANES),
                mem(size_x, LANES),
            ]

        layer = (size_x, size_y)
        vmem = pl.BlockSpec(memory_space=pltpu.VMEM)
        slots = SPLIT_Z * SLOTS
        n_p = n_chord * SPLIT_X_HI * SPLIT_CORE
        inputs = (velocity, stress, material, moduli, drive, owner.reshape(-1, LANES), cells.T)
        state = pl.pallas_call(
            functools.partial(kernel, n_chord, n_span),
            out_shape=(
                jax.ShapeDtypeStruct(velocity.shape, F32),
                jax.ShapeDtypeStruct(stress.shape, F32),
                jax.ShapeDtypeStruct(drive.shape, F32),
            ),
            in_specs=[pl.BlockSpec(memory_space=pltpu.HBM)] * 7,
            out_specs=(vmem, vmem, vmem),
            scratch_shapes=[
                pltpu.VMEM((depth, *layer), jnp.int32),
                pltpu.SMEM(moduli.shape, F32),
                mem(*drive.shape),
                pltpu.VMEM((owner.size // LANES, LANES), jnp.int32),
                pltpu.VMEM((8, owner.size), jnp.int32),
                mem(10, depth, *layer),
                pltpu.VMEM((size_y, 8 * LANES), BF16),
                mem(8, LANES),
                mem(8, LANES),
                mem(*layer),
                mem(owner.size // LANES * SPLIT_Z, LANES),
                mem(slots, LANES),
                mem(LANES, slots),
                mem(n_p, per, LANES),
                mem(LANES, LANES),
                mem(SPLIT_Z, 16, LANES),
                mem(SPLIT_Z, 16, LANES),
                mem(slots // 2, LANES),
                mem(slots // 2, LANES),
                mem(2, 8, LANES),
                mem(2, slots // 2, LANES),
                mem(n_p, per, LANES),
                mem(n_p, per, LANES),
                *edges(6, 5),
                mem(6 * depth, size_y),
                mem(5 * depth, size_y),
                mem(size_x, LANES),
                mem(size_x, LANES),
                mem(depth, LANES),
                mem(depth, LANES),
                *edges(3, 3),
                *edges(3, 3),
                mem(depth, LANES),
                mem(depth, LANES),
                mem(LANES, LANES),
                mem(LANES, size_y),
                mem(LANES, LANES),
                mem(SPLIT_Z * 8, LANES),
                mem(3, depth, size_y),
                mem(3, size_x, LANES),
                mem(5, depth, size_y),
                mem(5, size_x, LANES),
                pltpu.SemaphoreType.DMA((7,)),
                pltpu.SemaphoreType.DMA((6,)),
                pltpu.SemaphoreType.DMA((6,)),
                pltpu.SemaphoreType.DMA((12,)),
                pltpu.SemaphoreType.DMA((12,)),
            ],
            compiler_params=pltpu.CompilerParams(
                collective_id=0, has_side_effects=True, vmem_limit_bytes=48 * 1024 * 1024
            ),
        )(*(pltpu.with_memory_space_constraint(x, pltpu.HBM) for x in inputs))
        hbm = pl.BlockSpec(memory_space=pltpu.HBM)
        return pl.pallas_call(
            hand_over,
            out_shape=tuple(jax.ShapeDtypeStruct(x.shape, x.dtype) for x in state),
            in_specs=[pl.BlockSpec(memory_space=pl.ANY)] * 3,
            out_specs=(hbm, hbm, hbm),
            scratch_shapes=[pltpu.SemaphoreType.DMA((3,))],
        )(*(pltpu.with_memory_space_constraint(x, pltpu.VMEM) for x in state))

    in_specs = (
        P(None, None, "chord", "span"),
        P(None, None, "chord", "span"),
        P(None, "chord", "span"),
        P(),
        P(("chord", "span"), None),
        P(),
        P(),
    )
    out_specs = (
        P(None, None, "chord", "span"),
        P(None, None, "chord", "span"),
        P(("chord", "span"), None),
    )
    return jax.shard_map(local, mesh=mesh, in_specs=in_specs, out_specs=out_specs, check_vma=False)
```

```python
import functools

import jax
import jax.numpy as jnp
from jax import lax
from jax.experimental import pallas as pl
from jax.experimental.pallas import tpu as pltpu
from jax.sharding import PartitionSpec as P

MESH = pl.DeviceIdType.MESH
F32 = jnp.float32
BF16 = jnp.bfloat16
DT = 0.5
SLOTS = 16
PATCH = 8
LANES = 128
SPLIT_X_HI, SPLIT_Z, SPLIT_CORE = 2, 8, 2
C11, C12, C13, C22, C23, C33, C44, C55, C66, BUOY = range(10)
XX, YY, ZZ, YZ, XZ, XY = range(6)


def iota(shape, dim):
    return lax.broadcasted_iota(jnp.int32, shape, dim)


def fiota(shape, dim):
    return iota(shape, dim).astype(F32)


def split(x):
    a = x.astype(BF16)
    return a, (x - a.astype(F32)).astype(BF16)


def dot(a, b, contract=((1,), (0,))):
    return lax.dot_general(a, b, (contract, ((), ())), preferred_element_type=F32)


def kernel(
    n_chord,
    n_span,
    vel_in,
    str_in,
    mat_in,
    moduli_in,
    drive_in,
    owner_in,
    cells_in,
    v,
    s,
    rec_out,
    mat,
    moduli,
    drive,
    owner,
    cells,
    coef,
    onehot_y,
    slot_x,
    slot_y,
    plane,
    ranks,
    taken,
    taken_t,
    gathered,
    send2,
    routed2,
    send3,
    routed3,
    rec_send,
    rec_rows,
    rec_back,
    rec_got,
    to_dn,
    to_up,
    to_rt,
    to_lt,
    from_up,
    from_dn,
    from_lt,
    from_rt,
    corner_up,
    corner_dn,
    vto_dn,
    vto_up,
    vto_rt,
    vto_lt,
    vfrom_up,
    vfrom_dn,
    vfrom_lt,
    vfrom_rt,
    vcorner_up,
    vcorner_dn,
    aux_t,
    off_y,
    off_x,
    edge_pick,
    halo_row,
    halo_col,
    hcoef_row,
    hcoef_col,
    load_sem,
    group_send,
    group_recv,
    edge_send,
    edge_recv,
):
    c = lax.axis_index("chord")
    sp = lax.axis_index("span")
    depth = vel_in.shape[1]
    size_x = vel_in.shape[2]
    size_y = vel_in.shape[3]
    half = size_y - LANES
    n_z = SPLIT_Z
    n_p = n_chord * SPLIT_X_HI * SPLIT_CORE
    my_z = lax.rem(lax.div(sp, SPLIT_CORE), SPLIT_Z)
    x_hi = lax.div(sp, SPLIT_Z * SPLIT_CORE)
    my_p = (c * SPLIT_X_HI + x_hi) * SPLIT_CORE + lax.rem(sp, SPLIT_CORE)
    xor = jnp.bitwise_xor

    def p_partner(i):
        core, high, to_c = i % SPLIT_CORE, i // SPLIT_CORE % SPLIT_X_HI, i // SPLIT_CORE // SPLIT_X_HI
        return xor(c, to_c), xor(sp, high * SPLIT_Z * SPLIT_CORE + core)

    def z_partner(i):
        return c, xor(sp, i * SPLIT_CORE)

    has_up, has_dn = c > 0, c < n_chord - 1
    has_lt, has_rt = sp > 0, sp < n_span - 1
    diag_up = jnp.logical_and(has_up, has_rt)
    diag_dn = jnp.logical_and(has_dn, has_lt)

    pairs = [
        (drive_in, drive),
        (vel_in, v),
        (str_in, s),
        (mat_in, mat),
        (owner_in, owner),
        (cells_in.at[pl.ds(0, 8)], cells),
        (moduli_in, moduli),
    ]
    loads = [pltpu.make_async_copy(a, b, load_sem.at[i]) for i, (a, b) in enumerate(pairs)]
    loads[0].start()

    barrier = pltpu.get_barrier_semaphore()

    def greet(to_c, to_s):
        pl.semaphore_signal(barrier, inc=1, device_id=(to_c, to_s), device_id_type=MESH)

    ring = (0, 1, 2, 1)

    def p_hops(i):
        core, high, to_c = i % SPLIT_CORE, i // SPLIT_CORE % SPLIT_X_HI, i // SPLIT_CORE // SPLIT_X_HI
        return 4 * (ring[2 * high + to_c % 2] + ring[to_c // 2 % 4]) + core

    p_order = sorted(range(1, n_p), key=p_hops, reverse=True)
    z_order = sorted(range(1, n_z), key=lambda i: (0, 1, 2, 3, 4, 3, 2, 3)[i], reverse=True)
    for i in p_order:
        greet(*p_partner(i))
    for i in z_order:
        greet(*z_partner(i))
    sides = [
        (has_up, (c - 1, sp)),
        (has_dn, (c + 1, sp)),
        (has_lt, (c, sp - 1)),
        (has_rt, (c, sp + 1)),
        (diag_up, (c - 1, sp + 1)),
        (diag_dn, (c + 1, sp - 1)),
    ]
    for there, to in sides:
        pl.when(there)(functools.partial(greet, *to))
    for load in loads[1:]:
        load.start()

    @pl.when(jnp.logical_not(has_up))
    def _():
        for ref in (from_up, vfrom_up):
            ref[...] = jnp.zeros_like(ref)

    @pl.when(jnp.logical_not(has_dn))
    def _():
        for ref in (from_dn, vfrom_dn):
            ref[...] = jnp.zeros_like(ref)

    @pl.when(jnp.logical_not(has_lt))
    def _():
        for ref in (from_lt, vfrom_lt):
            ref[...] = jnp.zeros_like(ref)

    @pl.when(jnp.logical_not(has_rt))
    def _():
        for ref in (from_rt, vfrom_rt):
            ref[...] = jnp.zeros_like(ref)

    @pl.when(jnp.logical_not(diag_up))
    def _():
        for ref in (corner_up, vcorner_up):
            ref[...] = jnp.zeros_like(ref)

    @pl.when(jnp.logical_not(diag_dn))
    def _():
        for ref in (corner_dn, vcorner_dn):
            ref[...] = jnp.zeros_like(ref)

    pl.semaphore_wait(
        barrier,
        n_p + n_z - 2 + sum(there.astype(jnp.int32) for there, _ in sides),
    )

    def send(source, target, to, sem):
        return pltpu.make_async_remote_copy(
            src_ref=source,
            dst_ref=target,
            send_sem=group_send.at[sem],
            recv_sem=group_recv.at[sem],
            device_id=to,
            device_id_type=MESH,
        )

    def wait_all(ref, count, sems, sem):
        if count:
            part = ref.at[pl.ds(0, count)]
            pltpu.make_async_copy(part, part, sems.at[sem]).wait()

    def block(ref, index, count):
        return ref.at[pl.ds(pl.multiple_of(index * count, count), count)]

    per = drive.shape[0]
    loads[0].wait()
    for i in p_order:
        send(drive, block(gathered, my_p, per), p_partner(i), 0).start()
    gathered[pl.ds(pl.multiple_of(my_p * per, per), per), :] = drive[...]

    def edge(source, target, to, index):
        return pltpu.make_async_remote_copy(
            src_ref=source,
            dst_ref=target,
            send_sem=edge_send.at[index],
            recv_sem=edge_recv.at[index],
            device_id=to,
            device_id_type=MESH,
        )

    up, dn, lt, rt = (c - 1, sp), (c + 1, sp), (c, sp - 1), (c, sp + 1)

    def exchange(first, up_src, dn_src, lt_src, rt_src, up_dst, dn_dst, lt_dst, rt_dst, corners):
        moves = [
            (has_up, has_dn, edge(up_src, dn_dst, up, first)),
            (has_dn, has_up, edge(dn_src, up_dst, dn, first + 1)),
            (has_lt, has_rt, edge(lt_src, rt_dst, lt, first + 2)),
            (has_rt, has_lt, edge(rt_src, lt_dst, rt, first + 3)),
        ]
        corner_from_dn, corner_from_up = corners
        vy_corner = up_src.at[pl.ds(depth, depth), pl.ds(half, LANES)]
        vx_corner = dn_src.at[pl.ds(0, depth), pl.ds(0, LANES)]
        moves += [
            (diag_up, diag_dn, edge(vy_corner, corner_from_dn, (c - 1, sp + 1), first + 4)),
            (diag_dn, diag_up, edge(vx_corner, corner_from_up, (c + 1, sp - 1), first + 5)),
        ]

        def start():
            for goes, _, copy in moves:
                pl.when(goes)(copy.start)

        def arrive():
            for _, comes, copy in moves:
                pl.when(comes)(copy.wait_recv)

        def leave():
            for goes, _, copy in moves:
                pl.when(goes)(copy.wait_send)

        return start, arrive, leave

    start1, arrive1, leave1 = exchange(
        0, to_up, to_dn, to_lt, to_rt, from_up, from_dn, from_lt, from_rt, (corner_dn, corner_up)
    )
    start2, arrive2, leave2 = exchange(
        6, vto_up, vto_dn, vto_lt, vto_rt, vfrom_up, vfrom_dn, vfrom_lt, vfrom_rt, (vcorner_dn, vcorner_up)
    )

    def pack_rows(ref, row, fields):
        for z in range(depth):
            for k, read in enumerate(fields):
                ref[k * depth + z : k * depth + z + 1, :] = read(z, row)

    lane = iota((size_x, LANES), 1)
    row = iota((size_x, size_y), 0)

    def pack_cols(ref, column, fields):
        base = 0 if column == 0 else half
        at = column - base

        acc = jnp.zeros((size_x, LANES), F32)
        for z in range(depth):
            for k, read in enumerate(fields):
                to = k * depth + z
                by = (to + LANES - at) % LANES
                tile = read(z, base)
                moved = pltpu.roll(tile, by, 1) if by else tile
                acc = jnp.where(lane == to, moved, acc)
        ref[...] = acc

    def row_of(ref, comp):
        return lambda z, r: ref[comp, z, r : r + 1, :]

    def col_of(ref, comp):
        return lambda z, base: ref[comp, z, :, base : base + LANES]

    def mat_row(z, r):
        return mat[z, r : r + 1, :].astype(F32)

    def mat_col(z, base):
        return mat[z, :, base : base + LANES].astype(F32)

    v_rows = [row_of(v, k) for k in range(3)]
    v_cols = [col_of(v, k) for k in range(3)]

    for load in loads[1:]:
        load.wait()
    pack_rows(to_dn, size_x - 1, v_rows + [row_of(s, XY), row_of(s, XZ), mat_row])
    pack_rows(to_up, 0, v_rows + [row_of(s, XX), mat_row])
    pack_cols(to_rt, size_y - 1, v_cols + [col_of(s, XY), col_of(s, YZ), mat_col])
    pack_cols(to_lt, 0, v_cols + [col_of(s, YY), mat_col])
    start1()

    n_block = owner.shape[0]
    earlier = (iota((LANES, LANES), 0) < iota((LANES, LANES), 1)).astype(BF16)
    ones = jnp.ones((LANES, LANES), BF16)
    wanted = c * n_span + sp + (iota((n_z, LANES), 0) - my_z) * SPLIT_CORE
    same = jnp.concatenate(
        [(owner[a : a + 1, :] == wanted).astype(F32) for a in range(n_block)], axis=0
    )
    counts = dot(same.astype(BF16), jnp.concatenate([earlier, ones], axis=1))
    before = jnp.zeros((n_z, LANES), F32)
    chunk = SPLIT_CORE * per
    rank = jnp.full((n_z, LANES), -1.0, F32)
    lane8 = iota((n_z, LANES), 1)
    shift = size_y.bit_length() - 1
    aux = jnp.zeros((8, LANES), F32)
    aux_lane, aux_row = iota((8, LANES), 1), iota((8, LANES), 0)
    for a in range(n_block):
        at = slice(a * n_z, (a + 1) * n_z)
        rank_a = jnp.where(same[at] > 0.5, before + counts[at, :LANES], -1.0)
        before = before + counts[at, LANES:]
        ranks[at, :] = rank_a
        anchor = cells[0:1, a * LANES : (a + 1) * LANES]
        fields = (owner[a : a + 1, :], anchor >> shift, anchor & (size_y - 1))
        aux_a = jnp.zeros((8, LANES), F32)
        for k, field in enumerate(fields):
            aux_a = jnp.where(aux_row == k, field.astype(F32), aux_a)
        for h in range(SPLIT_X_HI):
            to = (a * SPLIT_X_HI + h) * chunk
            by = (to - h * SPLIT_Z * chunk) % LANES + LANES - my_z * chunk
            moved = pltpu.roll(rank_a, lax.rem(by, LANES), 1)
            rank = jnp.where(jnp.logical_and(lane8 >= to, lane8 < to + chunk), moved, rank)
            moved = pltpu.roll(aux_a, lax.rem(by, LANES), 1)
            aux = jnp.where(jnp.logical_and(aux_lane >= to, aux_lane < to + chunk), moved, aux)
    slot_ids = fiota((SLOTS, LANES), 0)
    for h in range(2):
        for k in range(n_z):
            at = (h * n_z + k) * 8
            ids = slot_ids[h * 8 : (h + 1) * 8]
            taken[at : at + 8, :] = (rank[k : k + 1, :] == ids).astype(F32)
    side_row = iota((n_z * 8, LANES), 0)
    side = side_row & 7
    to_z = side_row >> 3
    to_span = sp + (to_z - my_z) * SPLIT_CORE
    is_dn = jnp.logical_and((side & 1) == 0, side < 4)
    is_up = jnp.logical_and((side & 1) == 1, side < 4)
    is_rt = jnp.logical_and(side == 4, to_span < n_span - 1)
    is_lt = jnp.logical_and(side == 5, to_span > 0)
    whose = (c * n_span + to_span).astype(F32)
    at_owner, at_x, at_y = aux[0:1, :], aux[1:2, :], aux[2:3, :]
    reach = PATCH - 1
    edge_pick[...] = jnp.where(
        is_dn,
        jnp.logical_and(at_owner == whose + n_span, at_x == 0).astype(F32),
        jnp.where(
            is_up,
            jnp.logical_and(at_owner == whose - n_span, at_x == size_x - 1 - reach).astype(F32),
            jnp.where(
                is_rt,
                jnp.logical_and(at_owner == whose + 1, at_y == 0).astype(F32),
                jnp.where(
                    is_lt,
                    jnp.logical_and(at_owner == whose - 1, at_y == size_y - 1 - reach).astype(F32),
                    0.0,
                ),
            ),
        ),
    )
    aux_t[...] = jnp.transpose(jnp.concatenate([aux, jnp.zeros((LANES - 8, LANES), F32)], axis=0))
    off_x[...] = fiota((LANES, LANES), 1) - aux_t[:, 1:2]
    off_y[...] = fiota((LANES, size_y), 1) - aux_t[:, 2:3]

    taken_t[...] = jnp.transpose(taken[...])
    first_x = jnp.zeros((SLOTS, LANES), F32)
    first_y = jnp.zeros((SLOTS, LANES), F32)
    for a in range(n_block):
        anchor = cells[0:1, a * LANES : (a + 1) * LANES]
        hit = ranks[pl.ds(a * n_z + my_z, 1), :] == slot_ids
        first_x = first_x + jnp.where(hit, (anchor >> shift).astype(F32), 0.0)
        first_y = first_y + jnp.where(hit, (anchor & (size_y - 1)).astype(F32), 0.0)
    first_x = jnp.sum(first_x, axis=1, keepdims=True)
    first_y = jnp.sum(first_y, axis=1, keepdims=True)
    low = iota((8, LANES), 1) < 64
    cell_id = iota((8, LANES), 1) & 63
    slot_x[...] = jnp.where(low, first_x[0:8], first_x[8:16]) + (cell_id >> 3).astype(F32)
    slot_y[...] = jnp.where(low, first_y[0:8], first_y[8:16]) + (cell_id & 7).astype(F32)
    y_ids = fiota((size_y, LANES), 0)
    for t in range(8):
        onehot_y[:, t * LANES : (t + 1) * LANES] = (
            (slot_y[t : t + 1, :] == y_ids).astype(F32).astype(BF16)
        )
    x_ids = fiota((size_x, LANES), 0)

    def table(kind, index):
        out = jnp.full(kind.shape, DT * moduli[0, index], F32)
        for m in range(1, 4):
            out = jnp.where(kind == m, DT * moduli[m, index], out)
        return out

    def coef_layer(z, _):
        kind = mat[z]
        for k in range(10):
            coef[k, z] = table(kind, k)
        return 0

    lax.fori_loop(0, depth, coef_layer, 0)

    wait_all(gathered, (n_p - 1) * per, group_recv, 0)
    rows = gathered[...]
    pick = taken[...].astype(BF16)
    routes = sum(dot(pick, part) for part in split(rows))
    early, late = routes[: n_z * 8], routes[n_z * 8 :]
    low_all = iota((n_z * 8, LANES), 1) < 64
    force0 = jnp.where(low_all, early, pltpu.roll(late, 64, 1))
    force1 = jnp.where(low_all, pltpu.roll(early, 64, 1), late)
    for k in range(n_z):
        send2[k, 0:8, :] = force0[k * 8 : (k + 1) * 8]
        send2[k, 8:16, :] = force1[k * 8 : (k + 1) * 8]
    for i in z_order:
        send(send2.at[xor(my_z, i)], routed2.at[my_z], z_partner(i), 1).start()
    routed2[my_z] = send2[my_z]

    at_x0 = aux_t[:, 1:2] == 0.0
    at_y0 = aux_t[:, 2:3] == 0.0
    along_row = jnp.where(at_x0, rows, pltpu.roll(rows, LANES - PATCH * reach, 1))
    along_col = jnp.where(at_y0, rows, pltpu.roll(rows, LANES - reach, 1))
    row_line = jnp.zeros((LANES, size_y), F32)
    col_line = jnp.zeros((LANES, LANES), F32)
    for k in range(PATCH):
        row_line = jnp.where(off_y[...] == k, along_row[:, k : k + 1], row_line)
        col_line = jnp.where(off_x[...] == k, along_col[:, k * PATCH : k * PATCH + 1], col_line)
    lines = jnp.concatenate([row_line, col_line], axis=1)
    pick = edge_pick[...].astype(BF16)
    lines = sum(dot(pick, part) for part in split(lines))
    send3[...] = jnp.where(
        side < 2, lines[:, :LANES], jnp.where(side < 4, lines[:, LANES:size_y], lines[:, size_y:])
    )
    for i in z_order:
        send(block(send3, xor(my_z, i), 8), block(routed3, my_z, 8), z_partner(i), 2).start()
    own = pl.ds(pl.multiple_of(my_z * 8, 8), 8)
    routed3[own, :] = send3[own, :]

    def along_x(field, by, edge_row):
        if by > 0:
            return jnp.where(row == 0, edge_row, pltpu.roll(field, 1, 0))
        return jnp.where(row == size_x - 1, edge_row, pltpu.roll(field, size_x - 1, 0))

    def along_y(field, by, edge_col):
        if by > 0:
            moved = pltpu.roll(field, 1, 1)
            head = jnp.where(lane == 0, edge_col, moved[:, :LANES])
            return jnp.concatenate([head, moved[:, LANES:]], axis=1)
        moved = pltpu.roll(field, size_y - 1, 1)
        tail = jnp.where(lane == LANES - 1, edge_col, moved[:, half:])
        return jnp.concatenate([moved[:, :half], tail], axis=1)

    def first_lane(ref, field, z):
        return pltpu.roll(ref[...], lax.rem(2 * LANES - (field * depth + z), LANES), 1)

    def last_lane(ref, field, z):
        return pltpu.roll(ref[...], lax.rem(2 * LANES - 1 - (field * depth + z), LANES), 1)

    bottom, top = 0, depth - 1

    def stress_layer(z, up_ref, dn_ref, lt_ref, rt_ref):
        is_bottom, is_top = isinstance(z, int) and z == bottom, isinstance(z, int) and z == top
        vx, vy, vz = v[0, z], v[1, z], v[2, z]
        zz = vz if is_bottom else vz - v[2, z - 1]
        zy = -vy if is_top else v[1, z + 1] - vy
        zx = -vx if is_top else v[0, z + 1] - vx
        xx = vx - along_x(vx, 1, up_ref[pl.ds(z, 1), :])
        yy = vy - along_y(vy, 1, first_lane(lt_ref, 1, z))
        yz = zy + (along_y(vz, -1, last_lane(rt_ref, 2, z)) - vz)
        xz = zx + (along_x(vz, -1, dn_ref[pl.ds(2 * depth + z, 1), :]) - vz)
        xy = (along_y(vx, -1, last_lane(rt_ref, 0, z)) - vx) + (
            along_x(vy, -1, dn_ref[pl.ds(depth + z, 1), :]) - vy
        )
        s[XX, z] += coef[C11, z] * xx + coef[C12, z] * yy + coef[C13, z] * zz
        s[YY, z] += coef[C12, z] * xx + coef[C22, z] * yy + coef[C23, z] * zz
        s[ZZ, z] += coef[C13, z] * xx + coef[C23, z] * yy + coef[C33, z] * zz
        s[YZ, z] += coef[C44, z] * yz
        s[XZ, z] += coef[C55, z] * xz
        s[XY, z] += coef[C66, z] * xy

    def velocity_layer(z, comps=(0, 1, 2)):
        is_bottom, is_top = isinstance(z, int) and z == bottom, isinstance(z, int) and z == top
        sxx, syy, szz = s[XX, z], s[YY, z], s[ZZ, z]
        syz, sxz, sxy = s[YZ, z], s[XZ, z], s[XY, z]
        b = coef[BUOY, z]
        if 0 in comps:
            v[0, z] += b * (
                (along_x(sxx, -1, halo_row[0, pl.ds(z, 1), :]) - sxx)
                + (sxy - along_y(sxy, 1, first_lane(halo_col.at[1], 0, z)))
                + (sxz if is_bottom else sxz - s[XZ, z - 1])
            )
        if 1 in comps:
            v[1, z] += b * (
                (sxy - along_x(sxy, 1, halo_row[1, pl.ds(z, 1), :]))
                + (along_y(syy, -1, last_lane(halo_col.at[0], 0, z)) - syy)
                + (syz if is_bottom else syz - s[YZ, z - 1])
            )
        if 2 in comps:
            v[2, z] += b * (
                (sxz - along_x(sxz, 1, halo_row[2, pl.ds(z, 1), :]))
                + (syz - along_y(syz, 1, first_lane(halo_col.at[2], 0, z)))
                + (-szz if is_top else s[ZZ, z + 1] - szz)
            )

    wide = (depth, size_y)
    wide_lane = iota(wide, 1)
    wide_z = iota(wide, 0)

    def below_z(f):
        return jnp.where(wide_z == 0, 0.0, pltpu.roll(f, 1, 0))

    def above_z(f):
        return jnp.where(wide_z == depth - 1, 0.0, pltpu.roll(f, depth - 1, 0))

    def lane_below_z(f):
        return jnp.where(lane == 0, 0.0, pltpu.roll(f, 1, 1))

    def lane_above_z(f):
        return jnp.where(lane == depth - 1, 0.0, pltpu.roll(f, LANES - 1, 1))

    def to_lanes(corner, at):
        col = jnp.broadcast_to(corner[:, at : at + 1], (depth, LANES))
        here = iota((depth, LANES), 0) == iota((depth, LANES), 1)
        return jnp.sum(jnp.where(here, col, 0.0), axis=0, keepdims=True)

    def lanes_of(ref, field):
        if field == 0:
            return ref[...]
        return pltpu.roll(ref[...], LANES - field * depth, 1)

    narrow_row = iota((size_x, LANES), 0)

    def halo_stress(up_ref, dn_ref, lt_ref, rt_ref, cup, cdn, my_up, my_dn, my_lt, my_rt):
        def rows(ref, k):
            return ref[k * depth : (k + 1) * depth, :]

        vx, vy, vz = rows(dn_ref, 0), rows(dn_ref, 1), rows(dn_ref, 2)
        corner = jnp.broadcast_to(cdn[:, LANES - 1 : LANES], wide)
        vy_back = jnp.where(wide_lane == 0, corner, pltpu.roll(vy, 1, 1))
        halo_row[0] += (
            hcoef_row[0] * (vx - rows(my_dn, 0))
            + hcoef_row[1] * (vy - vy_back)
            + hcoef_row[2] * (vz - below_z(vz))
        )
        vx, vy, vz = rows(up_ref, 0), rows(up_ref, 1), rows(up_ref, 2)
        corner = jnp.broadcast_to(cup[:, 0:1], wide)
        vx_next = jnp.where(wide_lane == size_y - 1, corner, pltpu.roll(vx, size_y - 1, 1))
        halo_row[1] += hcoef_row[3] * ((vx_next - vx) + (rows(my_up, 1) - vy))
        halo_row[2] += hcoef_row[4] * ((above_z(vx) - vx) + (rows(my_up, 2) - vz))
        vx, vy, vz = lanes_of(rt_ref, 0), lanes_of(rt_ref, 1), lanes_of(rt_ref, 2)
        vx_back = jnp.where(narrow_row == 0, to_lanes(cup, 0), pltpu.roll(vx, 1, 0))
        halo_col[0] += (
            hcoef_col[0] * (vx - vx_back)
            + hcoef_col[1] * (vy - lanes_of(my_rt, 1))
            + hcoef_col[2] * (vz - lane_below_z(vz))
        )
        vx, vy, vz = lanes_of(lt_ref, 0), lanes_of(lt_ref, 1), lanes_of(lt_ref, 2)
        vy_next = jnp.where(
            narrow_row == size_x - 1, to_lanes(cdn, LANES - 1), pltpu.roll(vy, size_x - 1, 0)
        )
        halo_col[1] += hcoef_col[3] * ((lanes_of(my_lt, 0) - vx) + (vy_next - vy))
        halo_col[2] += hcoef_col[4] * ((lane_above_z(vy) - vy) + (lanes_of(my_lt, 2) - vz))

    arrive1()
    kind = from_dn[4 * depth : 5 * depth, :]
    inside = has_dn.astype(F32)
    for k, index in enumerate((C11, C12, C13)):
        hcoef_row[k] = table(kind, index) * inside
    kind = from_up[5 * depth : 6 * depth, :]
    inside = has_up.astype(F32)
    for k, index in enumerate((C66, C55)):
        hcoef_row[3 + k] = table(kind, index) * inside
    kind = lanes_of(from_rt, 4)
    inside = has_rt.astype(F32)
    for k, index in enumerate((C12, C22, C23)):
        hcoef_col[k] = table(kind, index) * inside
    kind = lanes_of(from_lt, 5)
    inside = has_lt.astype(F32)
    for k, index in enumerate((C66, C44)):
        hcoef_col[3 + k] = table(kind, index) * inside
    halo_row[0] = from_dn[3 * depth : 4 * depth, :]
    halo_row[1] = from_up[3 * depth : 4 * depth, :]
    halo_row[2] = from_up[4 * depth : 5 * depth, :]
    halo_col[0] = lanes_of(from_rt, 3)
    halo_col[1] = lanes_of(from_lt, 3)
    halo_col[2] = lanes_of(from_lt, 4)

    def stress_first(z, _):
        stress_layer(z, from_up, from_dn, from_lt, from_rt)
        return 0

    def velocity_body(z, _):
        velocity_layer(z)
        return 0

    stress_first(bottom, 0)
    lax.fori_loop(bottom + 1, top, stress_first, 0)
    stress_first(top, 0)
    halo_stress(
        from_up, from_dn, from_lt, from_rt, corner_up, corner_dn, to_up, to_dn, to_lt, to_rt
    )
    velocity_layer(bottom)
    lax.fori_loop(bottom + 1, top, velocity_body, 0)
    velocity_layer(top)

    pack_rows(vto_dn, size_x - 1, v_rows)
    pack_rows(vto_up, 0, v_rows)
    pack_cols(vto_rt, size_y - 1, v_cols)
    pack_cols(vto_lt, 0, v_cols)
    start2()

    def in_slot(t):
        return slot_x[t : t + 1, :] == x_ids

    wait_all(routed2, n_z - 1, group_recv, 1)
    force = routed2[0]
    for k in range(1, n_z):
        force = force + routed2[k]
    wide_force = jnp.concatenate(
        [
            jnp.concatenate(
                [jnp.where(in_slot(t), f[t : t + 1, :], 0.0) for t in range(8)], axis=1
            )
            for f in (force[0:8], force[8:16])
        ],
        axis=0,
    )
    got = dot(jnp.concatenate(split(wide_force), axis=0), onehot_y[...], ((1,), (1,)))
    got = got[: 2 * size_x] + got[2 * size_x :]
    plane[...] = coef[BUOY, top] * got[size_x:]
    top0 = v[2, top] + coef[BUOY, top] * got[:size_x]
    v[2, top] = top0

    def sample(values, step):
        got = dot(jnp.concatenate(split(values), axis=0), onehot_y[...])
        got = got[:size_x] + got[size_x:]
        for t in range(8):
            chosen = jnp.where(in_slot(t), got[:, t * LANES : (t + 1) * LANES], 0.0)
            at = step * 8 + t
            rec_send[at : at + 1, :] = jnp.sum(chosen, axis=0, keepdims=True)

    sample(top0, 0)
    wait_all(routed3, (n_z - 1) * 8, group_recv, 2)
    lines = routed3[0:8, :]
    for k in range(1, n_z):
        lines = lines + routed3[k * 8 : (k + 1) * 8, :]
    top_row = 2 * depth + top
    arrive2()
    leave2()

    def buoyancy(kind):
        return table(kind, BUOY)

    wide_line = jnp.concatenate([lines[0:2], lines[2:4]], axis=1)
    kind = from_dn[4 * depth + top : 4 * depth + top + 1, :]
    vfrom_dn[top_row : top_row + 1, :] += buoyancy(kind) * wide_line[0:1]
    kind = from_up[5 * depth + top : 5 * depth + top + 1, :]
    vfrom_up[top_row : top_row + 1, :] += buoyancy(kind) * wide_line[1:2]
    diagonal = iota((size_x, LANES), 0) == lane

    def upright(line):
        return jnp.sum(jnp.where(diagonal, line, 0.0), axis=1, keepdims=True)

    kind = pltpu.roll(from_rt[...], (top_row - 4 * depth - top) % LANES, 1)
    vfrom_rt[...] += jnp.where(lane == top_row, buoyancy(kind) * upright(lines[4:5]), 0.0)
    kind = pltpu.roll(from_lt[...], (top_row - 5 * depth - top) % LANES, 1)
    vfrom_lt[...] += jnp.where(lane == top_row, buoyancy(kind) * upright(lines[5:6]), 0.0)
    vto_up[top_row : top_row + 1, :] = v[2, top, 0:1, :]
    vto_lt[...] = jnp.where(
        lane == top_row, pltpu.roll(v[2, top, :, :LANES], top_row, 1), vto_lt[...]
    )
    stress_layer(top, vfrom_up, vfrom_dn, vfrom_lt, vfrom_rt)
    halo_stress(
        vfrom_up,
        vfrom_dn,
        vfrom_lt,
        vfrom_rt,
        vcorner_up,
        vcorner_dn,
        vto_up,
        vto_dn,
        vto_lt,
        vto_rt,
    )
    velocity_layer(top, (2,))
    top1 = v[2, top] + plane[...]
    v[2, top] = top1

    sample(top1, 1)
    for i in z_order:
        send(rec_send, rec_rows.at[my_z], z_partner(i), 3).start()
    rec_rows[my_z] = rec_send[...]

    pick = taken_t[...].astype(BF16)
    wait_all(rec_rows, n_z - 1, group_recv, 3)
    early = rec_rows[:, 0:8, :].reshape(n_z * 8, LANES)
    late = rec_rows[:, 8:16, :].reshape(n_z * 8, LANES)
    both = jnp.concatenate(
        [
            jnp.where(low_all, early, pltpu.roll(late, 64, 1)),
            jnp.where(low_all, pltpu.roll(early, 64, 1), late),
        ],
        axis=0,
    )
    back = sum(dot(pick, part) for part in split(both))
    rec_back[...] = back
    for i in p_order:
        send(block(rec_back, xor(my_p, i), per), block(rec_got, my_p, per), p_partner(i), 4).start()
    mine = pl.ds(pl.multiple_of(my_p * per, per), per)
    rec_got[mine, :] = rec_back[mine, :]
    def stress_second(z, _):
        stress_layer(z, vfrom_up, vfrom_dn, vfrom_lt, vfrom_rt)
        return 0

    stress_second(bottom, 0)
    lax.fori_loop(bottom + 1, top, stress_second, 0)
    velocity_layer(bottom)
    lax.fori_loop(bottom + 1, top, velocity_body, 0)
    velocity_layer(top, (0, 1))

    leave1()
    wait_all(gathered, (n_p - 1) * per, group_send, 0)
    wait_all(routed2, n_z - 1, group_send, 1)
    wait_all(routed3, (n_z - 1) * 8, group_send, 2)
    wait_all(rec_rows, n_z - 1, group_send, 3)
    wait_all(rec_got, (n_p - 1) * per, group_recv, 4)
    tile = max(per, 8)
    parts = [rec_got[i * tile : (i + 1) * tile, :] for i in range(n_p * per // tile)]
    while len(parts) > 1:
        parts = [a + b for a, b in zip(parts[::2], parts[1::2])]
    out = parts[0][:per]
    for i in range(1, tile // per):
        out = out + parts[0][i * per : (i + 1) * per]
    rec_out[...] = out

    wait_all(rec_got, (n_p - 1) * per, group_send, 4)


def hand_over(v, s, rec, vel_out, str_out, rec_out, sem):
    pairs = [(v, vel_out), (s, str_out), (rec, rec_out)]
    copies = [pltpu.make_async_copy(a, b, sem.at[i]) for i, (a, b) in enumerate(pairs)]
    for copy in copies:
        copy.start()
    for copy in copies:
        copy.wait()


def solution(mesh):
    n_chord, n_span = mesh.shape["chord"], mesh.shape["span"]

    def local(velocity, stress, material, moduli, drive, owner, cells):
        _, depth, size_x, size_y = velocity.shape
        per = drive.shape[0]

        def mem(*shape):
            return pltpu.VMEM(shape, F32)

        def edges(rows_dn, rows_up):
            return [
                mem(rows_dn * depth, size_y),
                mem(rows_up * depth, size_y),
                mem(size_x, LANES),
                mem(size_x, LANES),
            ]

        layer = (size_x, size_y)
        vmem = pl.BlockSpec(memory_space=pltpu.VMEM)
        slots = SPLIT_Z * SLOTS
        n_p = n_chord * SPLIT_X_HI * SPLIT_CORE
        inputs = (velocity, stress, material, moduli, drive, owner.reshape(-1, LANES), cells.T)
        state = pl.pallas_call(
            functools.partial(kernel, n_chord, n_span),
            out_shape=(
                jax.ShapeDtypeStruct(velocity.shape, F32),
                jax.ShapeDtypeStruct(stress.shape, F32),
                jax.ShapeDtypeStruct(drive.shape, F32),
            ),
            in_specs=[pl.BlockSpec(memory_space=pltpu.HBM)] * 7,
            out_specs=(vmem, vmem, vmem),
            scratch_shapes=[
                pltpu.VMEM((depth, *layer), jnp.int32),
                pltpu.SMEM(moduli.shape, F32),
                mem(*drive.shape),
                pltpu.VMEM((owner.size // LANES, LANES), jnp.int32),
                pltpu.VMEM((8, owner.size), jnp.int32),
                mem(10, depth, *layer),
                pltpu.VMEM((size_y, 8 * LANES), BF16),
                mem(8, LANES),
                mem(8, LANES),
                mem(*layer),
                mem(owner.size // LANES * SPLIT_Z, LANES),
                mem(slots, LANES),
                mem(LANES, slots),
                mem(n_p * per, LANES),
                mem(SPLIT_Z, 16, LANES),
                mem(SPLIT_Z, 16, LANES),
                mem(slots // 2, LANES),
                mem(slots // 2, LANES),
                mem(SLOTS, LANES),
                mem(SPLIT_Z, SLOTS, LANES),
                mem(n_p * per, LANES),
                mem(n_p * per, LANES),
                *edges(6, 5),
                mem(6 * depth, size_y),
                mem(5 * depth, size_y),
                mem(size_x, LANES),
                mem(size_x, LANES),
                mem(depth, LANES),
                mem(depth, LANES),
                *edges(3, 3),
                *edges(3, 3),
                mem(depth, LANES),
                mem(depth, LANES),
                mem(LANES, LANES),
                mem(LANES, size_y),
                mem(LANES, LANES),
                mem(SPLIT_Z * 8, LANES),
                mem(3, depth, size_y),
                mem(3, size_x, LANES),
                mem(5, depth, size_y),
                mem(5, size_x, LANES),
                pltpu.SemaphoreType.DMA((7,)),
                pltpu.SemaphoreType.DMA((5,)),
                pltpu.SemaphoreType.DMA((5,)),
                pltpu.SemaphoreType.DMA((12,)),
                pltpu.SemaphoreType.DMA((12,)),
            ],
            compiler_params=pltpu.CompilerParams(
                collective_id=0, has_side_effects=True, vmem_limit_bytes=48 * 1024 * 1024
            ),
        )(*(pltpu.with_memory_space_constraint(x, pltpu.HBM) for x in inputs))
        hbm = pl.BlockSpec(memory_space=pltpu.HBM)
        return pl.pallas_call(
            hand_over,
            out_shape=tuple(jax.ShapeDtypeStruct(x.shape, x.dtype) for x in state),
            in_specs=[pl.BlockSpec(memory_space=pl.ANY)] * 3,
            out_specs=(hbm, hbm, hbm),
            scratch_shapes=[pltpu.SemaphoreType.DMA((3,))],
        )(*(pltpu.with_memory_space_constraint(x, pltpu.VMEM) for x in state))

    in_specs = (
        P(None, None, "chord", "span"),
        P(None, None, "chord", "span"),
        P(None, "chord", "span"),
        P(),
        P(("chord", "span"), None),
        P(),
        P(),
    )
    out_specs = (
        P(None, None, "chord", "span"),
        P(None, None, "chord", "span"),
        P(("chord", "span"), None),
    )
    return jax.shard_map(local, mesh=mesh, in_specs=in_specs, out_specs=out_specs, check_vma=False)
```

```python
import functools

import jax
import jax.numpy as jnp
from jax import lax
from jax.experimental import pallas as pl
from jax.experimental.pallas import tpu as pltpu
from jax.sharding import PartitionSpec as P

MESH = pl.DeviceIdType.MESH
F32 = jnp.float32
BF16 = jnp.bfloat16
DT = 0.5
SLOTS = 16
PATCH = 8
LANES = 128
SPLIT_X_HI, SPLIT_Z, SPLIT_CORE = 2, 8, 2
C11, C12, C13, C22, C23, C33, C44, C55, C66, BUOY = range(10)
XX, YY, ZZ, YZ, XZ, XY = range(6)


def iota(shape, dim):
    return lax.broadcasted_iota(jnp.int32, shape, dim)


def fiota(shape, dim):
    return iota(shape, dim).astype(F32)


def split(x):
    a = x.astype(BF16)
    return a, (x - a.astype(F32)).astype(BF16)


def dot(a, b, contract=((1,), (0,))):
    return lax.dot_general(a, b, (contract, ((), ())), preferred_element_type=F32)


def kernel(
    n_chord,
    n_span,
    vel_in,
    str_in,
    mat_in,
    moduli_in,
    drive_in,
    owner_in,
    cells_in,
    v,
    s,
    rec_out,
    mat,
    moduli,
    drive,
    owner,
    cells,
    coef,
    onehot_y,
    slot_x,
    slot_y,
    plane,
    ranks,
    taken,
    taken_t,
    gathered,
    send2,
    routed2,
    send3,
    routed3,
    rec_send,
    rec_rows,
    rec_back,
    rec_got,
    to_dn,
    to_up,
    to_rt,
    to_lt,
    from_up,
    from_dn,
    from_lt,
    from_rt,
    corner_up,
    corner_dn,
    vto_dn,
    vto_up,
    vto_rt,
    vto_lt,
    vfrom_up,
    vfrom_dn,
    vfrom_lt,
    vfrom_rt,
    vcorner_up,
    vcorner_dn,
    aux_t,
    off_y,
    off_x,
    edge_pick,
    halo_row,
    halo_col,
    hcoef_row,
    hcoef_col,
    load_sem,
    group_send,
    group_recv,
    edge_send,
    edge_recv,
):
    c = lax.axis_index("chord")
    sp = lax.axis_index("span")
    depth = vel_in.shape[1]
    size_x = vel_in.shape[2]
    size_y = vel_in.shape[3]
    half = size_y - LANES
    n_z = SPLIT_Z
    n_p = n_chord * SPLIT_X_HI * SPLIT_CORE
    my_z = lax.rem(lax.div(sp, SPLIT_CORE), SPLIT_Z)
    x_hi = lax.div(sp, SPLIT_Z * SPLIT_CORE)
    my_p = (c * SPLIT_X_HI + x_hi) * SPLIT_CORE + lax.rem(sp, SPLIT_CORE)
    xor = jnp.bitwise_xor

    def p_partner(i):
        core, high, to_c = i % SPLIT_CORE, i // SPLIT_CORE % SPLIT_X_HI, i // SPLIT_CORE // SPLIT_X_HI
        return xor(c, to_c), xor(sp, high * SPLIT_Z * SPLIT_CORE + core)

    def z_partner(i):
        return c, xor(sp, i * SPLIT_CORE)

    has_up, has_dn = c > 0, c < n_chord - 1
    has_lt, has_rt = sp > 0, sp < n_span - 1
    diag_up = jnp.logical_and(has_up, has_rt)
    diag_dn = jnp.logical_and(has_dn, has_lt)

    pairs = [
        (drive_in, drive),
        (vel_in, v),
        (str_in, s),
        (mat_in, mat),
        (owner_in, owner),
        (cells_in.at[pl.ds(0, 8)], cells),
        (moduli_in, moduli),
    ]
    loads = [pltpu.make_async_copy(a, b, load_sem.at[i]) for i, (a, b) in enumerate(pairs)]
    loads[0].start()

    barrier = pltpu.get_barrier_semaphore()

    def greet(to_c, to_s):
        pl.semaphore_signal(barrier, inc=1, device_id=(to_c, to_s), device_id_type=MESH)

    ring = (0, 1, 2, 1)

    def p_hops(i):
        core, high, to_c = i % SPLIT_CORE, i // SPLIT_CORE % SPLIT_X_HI, i // SPLIT_CORE // SPLIT_X_HI
        return 4 * (ring[2 * high + to_c % 2] + ring[to_c // 2 % 4]) + core

    p_order = sorted(range(1, n_p), key=p_hops, reverse=True)
    z_order = sorted(range(1, n_z), key=lambda i: (0, 1, 2, 3, 4, 3, 2, 3)[i], reverse=True)
    for i in p_order:
        greet(*p_partner(i))
    for i in z_order:
        greet(*z_partner(i))
    sides = [
        (has_up, (c - 1, sp)),
        (has_dn, (c + 1, sp)),
        (has_lt, (c, sp - 1)),
        (has_rt, (c, sp + 1)),
        (diag_up, (c - 1, sp + 1)),
        (diag_dn, (c + 1, sp - 1)),
    ]
    for there, to in sides:
        pl.when(there)(functools.partial(greet, *to))
    for load in loads[1:]:
        load.start()

    @pl.when(jnp.logical_not(has_up))
    def _():
        for ref in (from_up, vfrom_up):
            ref[...] = jnp.zeros_like(ref)

    @pl.when(jnp.logical_not(has_dn))
    def _():
        for ref in (from_dn, vfrom_dn):
            ref[...] = jnp.zeros_like(ref)

    @pl.when(jnp.logical_not(has_lt))
    def _():
        for ref in (from_lt, vfrom_lt):
            ref[...] = jnp.zeros_like(ref)

    @pl.when(jnp.logical_not(has_rt))
    def _():
        for ref in (from_rt, vfrom_rt):
            ref[...] = jnp.zeros_like(ref)

    @pl.when(jnp.logical_not(diag_up))
    def _():
        for ref in (corner_up, vcorner_up):
            ref[...] = jnp.zeros_like(ref)

    @pl.when(jnp.logical_not(diag_dn))
    def _():
        for ref in (corner_dn, vcorner_dn):
            ref[...] = jnp.zeros_like(ref)

    pl.semaphore_wait(
        barrier,
        n_p + n_z - 2 + sum(there.astype(jnp.int32) for there, _ in sides),
    )

    def send(source, target, to, sem):
        return pltpu.make_async_remote_copy(
            src_ref=source,
            dst_ref=target,
            send_sem=group_send.at[sem],
            recv_sem=group_recv.at[sem],
            device_id=to,
            device_id_type=MESH,
        )

    def wait_all(ref, count, sems, sem):
        if count:
            part = ref.at[pl.ds(0, count)]
            pltpu.make_async_copy(part, part, sems.at[sem]).wait()

    def block(ref, index, count):
        return ref.at[pl.ds(pl.multiple_of(index * count, count), count)]

    per = drive.shape[0]
    loads[0].wait()
    for i in p_order:
        send(drive, block(gathered, my_p, per), p_partner(i), 0).start()
    gathered[pl.ds(pl.multiple_of(my_p * per, per), per), :] = drive[...]

    def edge(source, target, to, index):
        return pltpu.make_async_remote_copy(
            src_ref=source,
            dst_ref=target,
            send_sem=edge_send.at[index],
            recv_sem=edge_recv.at[index],
            device_id=to,
            device_id_type=MESH,
        )

    up, dn, lt, rt = (c - 1, sp), (c + 1, sp), (c, sp - 1), (c, sp + 1)

    def exchange(first, up_src, dn_src, lt_src, rt_src, up_dst, dn_dst, lt_dst, rt_dst, corners):
        moves = [
            (has_up, has_dn, edge(up_src, dn_dst, up, first)),
            (has_dn, has_up, edge(dn_src, up_dst, dn, first + 1)),
            (has_lt, has_rt, edge(lt_src, rt_dst, lt, first + 2)),
            (has_rt, has_lt, edge(rt_src, lt_dst, rt, first + 3)),
        ]
        corner_from_dn, corner_from_up = corners
        vy_corner = up_src.at[pl.ds(depth, depth), pl.ds(half, LANES)]
        vx_corner = dn_src.at[pl.ds(0, depth), pl.ds(0, LANES)]
        moves += [
            (diag_up, diag_dn, edge(vy_corner, corner_from_dn, (c - 1, sp + 1), first + 4)),
            (diag_dn, diag_up, edge(vx_corner, corner_from_up, (c + 1, sp - 1), first + 5)),
        ]

        def start():
            for goes, _, copy in moves:
                pl.when(goes)(copy.start)

        def arrive():
            for _, comes, copy in moves:
                pl.when(comes)(copy.wait_recv)

        def leave():
            for goes, _, copy in moves:
                pl.when(goes)(copy.wait_send)

        return start, arrive, leave

    start1, arrive1, leave1 = exchange(
        0, to_up, to_dn, to_lt, to_rt, from_up, from_dn, from_lt, from_rt, (corner_dn, corner_up)
    )
    start2, arrive2, leave2 = exchange(
        6, vto_up, vto_dn, vto_lt, vto_rt, vfrom_up, vfrom_dn, vfrom_lt, vfrom_rt, (vcorner_dn, vcorner_up)
    )

    def pack_rows(ref, row, fields):
        for z in range(depth):
            for k, read in enumerate(fields):
                ref[k * depth + z : k * depth + z + 1, :] = read(z, row)

    lane = iota((size_x, LANES), 1)
    row = iota((size_x, size_y), 0)

    def pack_cols(ref, column, fields):
        base = 0 if column == 0 else half
        at = column - base

        acc = jnp.zeros((size_x, LANES), F32)
        for z in range(depth):
            for k, read in enumerate(fields):
                to = k * depth + z
                by = (to + LANES - at) % LANES
                tile = read(z, base)
                moved = pltpu.roll(tile, by, 1) if by else tile
                acc = jnp.where(lane == to, moved, acc)
        ref[...] = acc

    def row_of(ref, comp):
        return lambda z, r: ref[comp, z, r : r + 1, :]

    def col_of(ref, comp):
        return lambda z, base: ref[comp, z, :, base : base + LANES]

    def mat_row(z, r):
        return mat[z, r : r + 1, :].astype(F32)

    def mat_col(z, base):
        return mat[z, :, base : base + LANES].astype(F32)

    v_rows = [row_of(v, k) for k in range(3)]
    v_cols = [col_of(v, k) for k in range(3)]

    for load in loads[1:]:
        load.wait()
    pack_rows(to_dn, size_x - 1, v_rows + [row_of(s, XY), row_of(s, XZ), mat_row])
    pack_rows(to_up, 0, v_rows + [row_of(s, XX), mat_row])
    pack_cols(to_rt, size_y - 1, v_cols + [col_of(s, XY), col_of(s, YZ), mat_col])
    pack_cols(to_lt, 0, v_cols + [col_of(s, YY), mat_col])
    start1()

    n_block = owner.shape[0]
    earlier = (iota((LANES, LANES), 0) < iota((LANES, LANES), 1)).astype(BF16)
    ones = jnp.ones((LANES, LANES), BF16)
    wanted = c * n_span + sp + (iota((n_z, LANES), 0) - my_z) * SPLIT_CORE
    same = jnp.concatenate(
        [(owner[a : a + 1, :] == wanted).astype(F32) for a in range(n_block)], axis=0
    )
    counts = dot(same.astype(BF16), jnp.concatenate([earlier, ones], axis=1))
    before = jnp.zeros((n_z, LANES), F32)
    chunk = SPLIT_CORE * per
    rank = jnp.full((n_z, LANES), -1.0, F32)
    lane8 = iota((n_z, LANES), 1)
    shift = size_y.bit_length() - 1
    aux = jnp.zeros((8, LANES), F32)
    aux_lane, aux_row = iota((8, LANES), 1), iota((8, LANES), 0)
    for a in range(n_block):
        at = slice(a * n_z, (a + 1) * n_z)
        rank_a = jnp.where(same[at] > 0.5, before + counts[at, :LANES], -1.0)
        before = before + counts[at, LANES:]
        ranks[at, :] = rank_a
        anchor = cells[0:1, a * LANES : (a + 1) * LANES]
        fields = (owner[a : a + 1, :], anchor >> shift, anchor & (size_y - 1))
        aux_a = jnp.zeros((8, LANES), F32)
        for k, field in enumerate(fields):
            aux_a = jnp.where(aux_row == k, field.astype(F32), aux_a)
        for h in range(SPLIT_X_HI):
            to = (a * SPLIT_X_HI + h) * chunk
            by = (to - h * SPLIT_Z * chunk) % LANES + LANES - my_z * chunk
            moved = pltpu.roll(rank_a, lax.rem(by, LANES), 1)
            rank = jnp.where(jnp.logical_and(lane8 >= to, lane8 < to + chunk), moved, rank)
            moved = pltpu.roll(aux_a, lax.rem(by, LANES), 1)
            aux = jnp.where(jnp.logical_and(aux_lane >= to, aux_lane < to + chunk), moved, aux)
    slot_ids = fiota((SLOTS, LANES), 0)
    for h in range(2):
        for k in range(n_z):
            at = (h * n_z + k) * 8
            ids = slot_ids[h * 8 : (h + 1) * 8]
            taken[at : at + 8, :] = (rank[k : k + 1, :] == ids).astype(F32)
    side_row = iota((n_z * 8, LANES), 0)
    side = side_row & 7
    to_z = side_row >> 3
    to_span = sp + (to_z - my_z) * SPLIT_CORE
    is_dn = jnp.logical_and((side & 1) == 0, side < 4)
    is_up = jnp.logical_and((side & 1) == 1, side < 4)
    is_rt = jnp.logical_and(side == 4, to_span < n_span - 1)
    is_lt = jnp.logical_and(side == 5, to_span > 0)
    whose = (c * n_span + to_span).astype(F32)
    at_owner, at_x, at_y = aux[0:1, :], aux[1:2, :], aux[2:3, :]
    reach = PATCH - 1
    edge_pick[...] = jnp.where(
        is_dn,
        jnp.logical_and(at_owner == whose + n_span, at_x == 0).astype(F32),
        jnp.where(
            is_up,
            jnp.logical_and(at_owner == whose - n_span, at_x == size_x - 1 - reach).astype(F32),
            jnp.where(
                is_rt,
                jnp.logical_and(at_owner == whose + 1, at_y == 0).astype(F32),
                jnp.where(
                    is_lt,
                    jnp.logical_and(at_owner == whose - 1, at_y == size_y - 1 - reach).astype(F32),
                    0.0,
                ),
            ),
        ),
    )
    aux_t[...] = jnp.transpose(jnp.concatenate([aux, jnp.zeros((LANES - 8, LANES), F32)], axis=0))
    off_x[...] = fiota((LANES, LANES), 1) - aux_t[:, 1:2]
    off_y[...] = fiota((LANES, size_y), 1) - aux_t[:, 2:3]

    taken_t[...] = jnp.transpose(taken[...])
    first_x = jnp.zeros((SLOTS, LANES), F32)
    first_y = jnp.zeros((SLOTS, LANES), F32)
    for a in range(n_block):
        anchor = cells[0:1, a * LANES : (a + 1) * LANES]
        hit = ranks[pl.ds(a * n_z + my_z, 1), :] == slot_ids
        first_x = first_x + jnp.where(hit, (anchor >> shift).astype(F32), 0.0)
        first_y = first_y + jnp.where(hit, (anchor & (size_y - 1)).astype(F32), 0.0)
    first_x = jnp.sum(first_x, axis=1, keepdims=True)
    first_y = jnp.sum(first_y, axis=1, keepdims=True)
    low = iota((8, LANES), 1) < 64
    cell_id = iota((8, LANES), 1) & 63
    slot_x[...] = jnp.where(low, first_x[0:8], first_x[8:16]) + (cell_id >> 3).astype(F32)
    slot_y[...] = jnp.where(low, first_y[0:8], first_y[8:16]) + (cell_id & 7).astype(F32)
    y_ids = fiota((size_y, LANES), 0)
    for t in range(8):
        onehot_y[:, t * LANES : (t + 1) * LANES] = (
            (slot_y[t : t + 1, :] == y_ids).astype(F32).astype(BF16)
        )
    x_ids = fiota((size_x, LANES), 0)

    def table(kind, index):
        out = jnp.full(kind.shape, DT * moduli[0, index], F32)
        for m in range(1, 4):
            out = jnp.where(kind == m, DT * moduli[m, index], out)
        return out

    def coef_layer(z, _):
        kind = mat[z]
        for k in range(10):
            coef[k, z] = table(kind, k)
        return 0

    lax.fori_loop(0, depth, coef_layer, 0)

    def along_x(field, by, edge_row):
        if by > 0:
            return jnp.where(row == 0, edge_row, pltpu.roll(field, 1, 0))
        return jnp.where(row == size_x - 1, edge_row, pltpu.roll(field, size_x - 1, 0))

    def along_y(field, by, edge_col):
        if by > 0:
            moved = pltpu.roll(field, 1, 1)
            head = jnp.where(lane == 0, edge_col, moved[:, :LANES])
            return jnp.concatenate([head, moved[:, LANES:]], axis=1)
        moved = pltpu.roll(field, size_y - 1, 1)
        tail = jnp.where(lane == LANES - 1, edge_col, moved[:, half:])
        return jnp.concatenate([moved[:, :half], tail], axis=1)

    def first_lane(ref, field, z):
        return pltpu.roll(ref[...], lax.rem(2 * LANES - (field * depth + z), LANES), 1)

    def last_lane(ref, field, z):
        return pltpu.roll(ref[...], lax.rem(2 * LANES - 1 - (field * depth + z), LANES), 1)

    bottom, top = 0, depth - 1

    def stress_layer(z, up_ref, dn_ref, lt_ref, rt_ref):
        is_bottom, is_top = isinstance(z, int) and z == bottom, isinstance(z, int) and z == top
        vx, vy, vz = v[0, z], v[1, z], v[2, z]
        zz = vz if is_bottom else vz - v[2, z - 1]
        zy = -vy if is_top else v[1, z + 1] - vy
        zx = -vx if is_top else v[0, z + 1] - vx
        if up_ref is None:
            vx_up = vy_dn = vz_dn = vy_lt = vx_rt = vz_rt = 0.0
        else:
            vx_up = up_ref[pl.ds(z, 1), :]
            vy_dn, vz_dn = dn_ref[pl.ds(depth + z, 1), :], dn_ref[pl.ds(2 * depth + z, 1), :]
            vy_lt = first_lane(lt_ref, 1, z)
            vx_rt, vz_rt = last_lane(rt_ref, 0, z), last_lane(rt_ref, 2, z)
        xx = vx - along_x(vx, 1, vx_up)
        yy = vy - along_y(vy, 1, vy_lt)
        yz = zy + (along_y(vz, -1, vz_rt) - vz)
        xz = zx + (along_x(vz, -1, vz_dn) - vz)
        xy = (along_y(vx, -1, vx_rt) - vx) + (
            along_x(vy, -1, vy_dn) - vy
        )
        s[XX, z] += coef[C11, z] * xx + coef[C12, z] * yy + coef[C13, z] * zz
        s[YY, z] += coef[C12, z] * xx + coef[C22, z] * yy + coef[C23, z] * zz
        s[ZZ, z] += coef[C13, z] * xx + coef[C23, z] * yy + coef[C33, z] * zz
        s[YZ, z] += coef[C44, z] * yz
        s[XZ, z] += coef[C55, z] * xz
        s[XY, z] += coef[C66, z] * xy

    def velocity_layer(z, comps=(0, 1, 2)):
        is_bottom, is_top = isinstance(z, int) and z == bottom, isinstance(z, int) and z == top
        sxx, syy, szz = s[XX, z], s[YY, z], s[ZZ, z]
        syz, sxz, sxy = s[YZ, z], s[XZ, z], s[XY, z]
        b = coef[BUOY, z]
        if 0 in comps:
            v[0, z] += b * (
                (along_x(sxx, -1, halo_row[0, pl.ds(z, 1), :]) - sxx)
                + (sxy - along_y(sxy, 1, first_lane(halo_col.at[1], 0, z)))
                + (sxz if is_bottom else sxz - s[XZ, z - 1])
            )
        if 1 in comps:
            v[1, z] += b * (
                (sxy - along_x(sxy, 1, halo_row[1, pl.ds(z, 1), :]))
                + (along_y(syy, -1, last_lane(halo_col.at[0], 0, z)) - syy)
                + (syz if is_bottom else syz - s[YZ, z - 1])
            )
        if 2 in comps:
            v[2, z] += b * (
                (sxz - along_x(sxz, 1, halo_row[2, pl.ds(z, 1), :]))
                + (syz - along_y(syz, 1, first_lane(halo_col.at[2], 0, z)))
                + (-szz if is_top else s[ZZ, z + 1] - szz)
            )

    wide = (depth, size_y)
    wide_lane = iota(wide, 1)
    wide_z = iota(wide, 0)

    def below_z(f):
        return jnp.where(wide_z == 0, 0.0, pltpu.roll(f, 1, 0))

    def above_z(f):
        return jnp.where(wide_z == depth - 1, 0.0, pltpu.roll(f, depth - 1, 0))

    def lane_below_z(f):
        return jnp.where(lane == 0, 0.0, pltpu.roll(f, 1, 1))

    def lane_above_z(f):
        return jnp.where(lane == depth - 1, 0.0, pltpu.roll(f, LANES - 1, 1))

    def to_lanes(corner, at):
        col = jnp.broadcast_to(corner[:, at : at + 1], (depth, LANES))
        here = iota((depth, LANES), 0) == iota((depth, LANES), 1)
        return jnp.sum(jnp.where(here, col, 0.0), axis=0, keepdims=True)

    def lanes_of(ref, field):
        if field == 0:
            return ref[...]
        return pltpu.roll(ref[...], LANES - field * depth, 1)

    narrow_row = iota((size_x, LANES), 0)

    def halo_stress(up_ref, dn_ref, lt_ref, rt_ref, cup, cdn, my_up, my_dn, my_lt, my_rt):
        def rows(ref, k):
            return ref[k * depth : (k + 1) * depth, :]

        vx, vy, vz = rows(dn_ref, 0), rows(dn_ref, 1), rows(dn_ref, 2)
        corner = jnp.broadcast_to(cdn[:, LANES - 1 : LANES], wide)
        vy_back = jnp.where(wide_lane == 0, corner, pltpu.roll(vy, 1, 1))
        halo_row[0] += (
            hcoef_row[0] * (vx - rows(my_dn, 0))
            + hcoef_row[1] * (vy - vy_back)
            + hcoef_row[2] * (vz - below_z(vz))
        )
        vx, vy, vz = rows(up_ref, 0), rows(up_ref, 1), rows(up_ref, 2)
        corner = jnp.broadcast_to(cup[:, 0:1], wide)
        vx_next = jnp.where(wide_lane == size_y - 1, corner, pltpu.roll(vx, size_y - 1, 1))
        halo_row[1] += hcoef_row[3] * ((vx_next - vx) + (rows(my_up, 1) - vy))
        halo_row[2] += hcoef_row[4] * ((above_z(vx) - vx) + (rows(my_up, 2) - vz))
        vx, vy, vz = lanes_of(rt_ref, 0), lanes_of(rt_ref, 1), lanes_of(rt_ref, 2)
        vx_back = jnp.where(narrow_row == 0, to_lanes(cup, 0), pltpu.roll(vx, 1, 0))
        halo_col[0] += (
            hcoef_col[0] * (vx - vx_back)
            + hcoef_col[1] * (vy - lanes_of(my_rt, 1))
            + hcoef_col[2] * (vz - lane_below_z(vz))
        )
        vx, vy, vz = lanes_of(lt_ref, 0), lanes_of(lt_ref, 1), lanes_of(lt_ref, 2)
        vy_next = jnp.where(
            narrow_row == size_x - 1, to_lanes(cdn, LANES - 1), pltpu.roll(vy, size_x - 1, 0)
        )
        halo_col[1] += hcoef_col[3] * ((lanes_of(my_lt, 0) - vx) + (vy_next - vy))
        halo_col[2] += hcoef_col[4] * ((lane_above_z(vy) - vy) + (lanes_of(my_lt, 2) - vz))

    def stress_inside(z, _):
        stress_layer(z, None, None, None, None)
        return 0

    stress_inside(bottom, 0)
    lax.fori_loop(bottom + 1, top, stress_inside, 0)
    stress_inside(top, 0)

    wait_all(gathered, (n_p - 1) * per, group_recv, 0)
    rows = gathered[...]
    pick = taken[...].astype(BF16)
    routes = sum(dot(pick, part) for part in split(rows))
    early, late = routes[: n_z * 8], routes[n_z * 8 :]
    low_all = iota((n_z * 8, LANES), 1) < 64
    force0 = jnp.where(low_all, early, pltpu.roll(late, 64, 1))
    force1 = jnp.where(low_all, pltpu.roll(early, 64, 1), late)
    for k in range(n_z):
        send2[k, 0:8, :] = force0[k * 8 : (k + 1) * 8]
        send2[k, 8:16, :] = force1[k * 8 : (k + 1) * 8]
    for i in z_order:
        send(send2.at[xor(my_z, i)], routed2.at[my_z], z_partner(i), 1).start()
    routed2[my_z] = send2[my_z]

    at_x0 = aux_t[:, 1:2] == 0.0
    at_y0 = aux_t[:, 2:3] == 0.0
    along_row = jnp.where(at_x0, rows, pltpu.roll(rows, LANES - PATCH * reach, 1))
    along_col = jnp.where(at_y0, rows, pltpu.roll(rows, LANES - reach, 1))
    row_line = jnp.zeros((LANES, size_y), F32)
    col_line = jnp.zeros((LANES, LANES), F32)
    for k in range(PATCH):
        row_line = jnp.where(off_y[...] == k, along_row[:, k : k + 1], row_line)
        col_line = jnp.where(off_x[...] == k, along_col[:, k * PATCH : k * PATCH + 1], col_line)
    lines = jnp.concatenate([row_line, col_line], axis=1)
    pick = edge_pick[...].astype(BF16)
    lines = sum(dot(pick, part) for part in split(lines))
    send3[...] = jnp.where(
        side < 2, lines[:, :LANES], jnp.where(side < 4, lines[:, LANES:size_y], lines[:, size_y:])
    )
    for i in z_order:
        send(block(send3, xor(my_z, i), 8), block(routed3, my_z, 8), z_partner(i), 2).start()
    own = pl.ds(pl.multiple_of(my_z * 8, 8), 8)
    routed3[own, :] = send3[own, :]

    arrive1()
    kind = from_dn[4 * depth : 5 * depth, :]
    inside = has_dn.astype(F32)
    for k, index in enumerate((C11, C12, C13)):
        hcoef_row[k] = table(kind, index) * inside
    kind = from_up[5 * depth : 6 * depth, :]
    inside = has_up.astype(F32)
    for k, index in enumerate((C66, C55)):
        hcoef_row[3 + k] = table(kind, index) * inside
    kind = lanes_of(from_rt, 4)
    inside = has_rt.astype(F32)
    for k, index in enumerate((C12, C22, C23)):
        hcoef_col[k] = table(kind, index) * inside
    kind = lanes_of(from_lt, 5)
    inside = has_lt.astype(F32)
    for k, index in enumerate((C66, C44)):
        hcoef_col[3 + k] = table(kind, index) * inside
    halo_row[0] = from_dn[3 * depth : 4 * depth, :]
    halo_row[1] = from_up[3 * depth : 4 * depth, :]
    halo_row[2] = from_up[4 * depth : 5 * depth, :]
    halo_col[0] = lanes_of(from_rt, 3)
    halo_col[1] = lanes_of(from_lt, 3)
    halo_col[2] = lanes_of(from_lt, 4)

    def velocity_body(z, _):
        velocity_layer(z)
        return 0

    last_x = size_x - 1
    for z in range(depth):
        vx_up = from_up[z : z + 1, :]
        vy_dn, vz_dn = (from_dn[k * depth + z : k * depth + z + 1, :] for k in (1, 2))
        for comp, index in ((XX, C11), (YY, C12), (ZZ, C13)):
            s[comp, z, 0:1, :] -= coef[index, z, 0:1, :] * vx_up
        s[XZ, z, last_x:, :] += coef[C55, z, last_x:, :] * vz_dn
        s[XY, z, last_x:, :] += coef[C66, z, last_x:, :] * vy_dn
        vy_lt = jnp.where(lane == 0, first_lane(from_lt, 1, z), 0.0)
        for comp, index in ((XX, C12), (YY, C22), (ZZ, C23)):
            s[comp, z, :, :LANES] -= coef[index, z, :, :LANES] * vy_lt
        vx_rt, vz_rt = (
            jnp.where(lane == LANES - 1, last_lane(from_rt, k, z), 0.0) for k in (0, 2)
        )
        s[YZ, z, :, half:] += coef[C44, z, :, half:] * vz_rt
        s[XY, z, :, half:] += coef[C66, z, :, half:] * vx_rt
    halo_stress(
        from_up, from_dn, from_lt, from_rt, corner_up, corner_dn, to_up, to_dn, to_lt, to_rt
    )
    velocity_layer(bottom)
    lax.fori_loop(bottom + 1, top, velocity_body, 0)
    velocity_layer(top)

    pack_rows(vto_dn, size_x - 1, v_rows)
    pack_rows(vto_up, 0, v_rows)
    pack_cols(vto_rt, size_y - 1, v_cols)
    pack_cols(vto_lt, 0, v_cols)
    start2()

    def in_slot(t):
        return slot_x[t : t + 1, :] == x_ids

    wait_all(routed2, n_z - 1, group_recv, 1)
    force = routed2[0]
    for k in range(1, n_z):
        force = force + routed2[k]
    wide_force = jnp.concatenate(
        [
            jnp.concatenate(
                [jnp.where(in_slot(t), f[t : t + 1, :], 0.0) for t in range(8)], axis=1
            )
            for f in (force[0:8], force[8:16])
        ],
        axis=0,
    )
    got = dot(jnp.concatenate(split(wide_force), axis=0), onehot_y[...], ((1,), (1,)))
    got = got[: 2 * size_x] + got[2 * size_x :]
    plane[...] = coef[BUOY, top] * got[size_x:]
    top0 = v[2, top] + coef[BUOY, top] * got[:size_x]
    v[2, top] = top0

    def sample(values, step):
        got = dot(jnp.concatenate(split(values), axis=0), onehot_y[...])
        got = got[:size_x] + got[size_x:]
        for t in range(8):
            chosen = jnp.where(in_slot(t), got[:, t * LANES : (t + 1) * LANES], 0.0)
            at = step * 8 + t
            rec_send[at : at + 1, :] = jnp.sum(chosen, axis=0, keepdims=True)

    sample(top0, 0)
    wait_all(routed3, (n_z - 1) * 8, group_recv, 2)
    lines = routed3[0:8, :]
    for k in range(1, n_z):
        lines = lines + routed3[k * 8 : (k + 1) * 8, :]
    top_row = 2 * depth + top
    arrive2()
    leave2()

    def buoyancy(kind):
        return table(kind, BUOY)

    wide_line = jnp.concatenate([lines[0:2], lines[2:4]], axis=1)
    kind = from_dn[4 * depth + top : 4 * depth + top + 1, :]
    vfrom_dn[top_row : top_row + 1, :] += buoyancy(kind) * wide_line[0:1]
    kind = from_up[5 * depth + top : 5 * depth + top + 1, :]
    vfrom_up[top_row : top_row + 1, :] += buoyancy(kind) * wide_line[1:2]
    diagonal = iota((size_x, LANES), 0) == lane

    def upright(line):
        return jnp.sum(jnp.where(diagonal, line, 0.0), axis=1, keepdims=True)

    kind = pltpu.roll(from_rt[...], (top_row - 4 * depth - top) % LANES, 1)
    vfrom_rt[...] += jnp.where(lane == top_row, buoyancy(kind) * upright(lines[4:5]), 0.0)
    kind = pltpu.roll(from_lt[...], (top_row - 5 * depth - top) % LANES, 1)
    vfrom_lt[...] += jnp.where(lane == top_row, buoyancy(kind) * upright(lines[5:6]), 0.0)
    vto_up[top_row : top_row + 1, :] = v[2, top, 0:1, :]
    vto_lt[...] = jnp.where(
        lane == top_row, pltpu.roll(v[2, top, :, :LANES], top_row, 1), vto_lt[...]
    )
    stress_layer(top, vfrom_up, vfrom_dn, vfrom_lt, vfrom_rt)
    halo_stress(
        vfrom_up,
        vfrom_dn,
        vfrom_lt,
        vfrom_rt,
        vcorner_up,
        vcorner_dn,
        vto_up,
        vto_dn,
        vto_lt,
        vto_rt,
    )
    velocity_layer(top, (2,))
    top1 = v[2, top] + plane[...]
    v[2, top] = top1

    sample(top1, 1)
    for i in z_order:
        send(rec_send, rec_rows.at[my_z], z_partner(i), 3).start()
    rec_rows[my_z] = rec_send[...]

    pick = taken_t[...].astype(BF16)
    wait_all(rec_rows, n_z - 1, group_recv, 3)
    early = rec_rows[:, 0:8, :].reshape(n_z * 8, LANES)
    late = rec_rows[:, 8:16, :].reshape(n_z * 8, LANES)
    both = jnp.concatenate(
        [
            jnp.where(low_all, early, pltpu.roll(late, 64, 1)),
            jnp.where(low_all, pltpu.roll(early, 64, 1), late),
        ],
        axis=0,
    )
    back = sum(dot(pick, part) for part in split(both))
    rec_back[...] = back
    for i in p_order:
        send(block(rec_back, xor(my_p, i), per), block(rec_got, my_p, per), p_partner(i), 4).start()
    mine = pl.ds(pl.multiple_of(my_p * per, per), per)
    rec_got[mine, :] = rec_back[mine, :]
    def stress_second(z, _):
        stress_layer(z, vfrom_up, vfrom_dn, vfrom_lt, vfrom_rt)
        return 0

    stress_second(bottom, 0)
    lax.fori_loop(bottom + 1, top, stress_second, 0)
    velocity_layer(bottom)
    lax.fori_loop(bottom + 1, top, velocity_body, 0)
    velocity_layer(top, (0, 1))

    leave1()
    wait_all(gathered, (n_p - 1) * per, group_send, 0)
    wait_all(routed2, n_z - 1, group_send, 1)
    wait_all(routed3, (n_z - 1) * 8, group_send, 2)
    wait_all(rec_rows, n_z - 1, group_send, 3)
    wait_all(rec_got, (n_p - 1) * per, group_recv, 4)
    tile = max(per, 8)
    parts = [rec_got[i * tile : (i + 1) * tile, :] for i in range(n_p * per // tile)]
    while len(parts) > 1:
        parts = [a + b for a, b in zip(parts[::2], parts[1::2])]
    out = parts[0][:per]
    for i in range(1, tile // per):
        out = out + parts[0][i * per : (i + 1) * per]
    rec_out[...] = out

    wait_all(rec_got, (n_p - 1) * per, group_send, 4)


def hand_over(v, s, rec, vel_out, str_out, rec_out, sem):
    pairs = [(v, vel_out), (s, str_out), (rec, rec_out)]
    copies = [pltpu.make_async_copy(a, b, sem.at[i]) for i, (a, b) in enumerate(pairs)]
    for copy in copies:
        copy.start()
    for copy in copies:
        copy.wait()


def solution(mesh):
    n_chord, n_span = mesh.shape["chord"], mesh.shape["span"]

    def local(velocity, stress, material, moduli, drive, owner, cells):
        _, depth, size_x, size_y = velocity.shape
        per = drive.shape[0]

        def mem(*shape):
            return pltpu.VMEM(shape, F32)

        def edges(rows_dn, rows_up):
            return [
                mem(rows_dn * depth, size_y),
                mem(rows_up * depth, size_y),
                mem(size_x, LANES),
                mem(size_x, LANES),
            ]

        layer = (size_x, size_y)
        vmem = pl.BlockSpec(memory_space=pltpu.VMEM)
        slots = SPLIT_Z * SLOTS
        n_p = n_chord * SPLIT_X_HI * SPLIT_CORE
        inputs = (velocity, stress, material, moduli, drive, owner.reshape(-1, LANES), cells.T)
        state = pl.pallas_call(
            functools.partial(kernel, n_chord, n_span),
            out_shape=(
                jax.ShapeDtypeStruct(velocity.shape, F32),
                jax.ShapeDtypeStruct(stress.shape, F32),
                jax.ShapeDtypeStruct(drive.shape, F32),
            ),
            in_specs=[pl.BlockSpec(memory_space=pltpu.HBM)] * 7,
            out_specs=(vmem, vmem, vmem),
            scratch_shapes=[
                pltpu.VMEM((depth, *layer), jnp.int32),
                pltpu.SMEM(moduli.shape, F32),
                mem(*drive.shape),
                pltpu.VMEM((owner.size // LANES, LANES), jnp.int32),
                pltpu.VMEM((8, owner.size), jnp.int32),
                mem(10, depth, *layer),
                pltpu.VMEM((size_y, 8 * LANES), BF16),
                mem(8, LANES),
                mem(8, LANES),
                mem(*layer),
                mem(owner.size // LANES * SPLIT_Z, LANES),
                mem(slots, LANES),
                mem(LANES, slots),
                mem(n_p * per, LANES),
                mem(SPLIT_Z, 16, LANES),
                mem(SPLIT_Z, 16, LANES),
                mem(slots // 2, LANES),
                mem(slots // 2, LANES),
                mem(SLOTS, LANES),
                mem(SPLIT_Z, SLOTS, LANES),
                mem(n_p * per, LANES),
                mem(n_p * per, LANES),
                *edges(6, 5),
                mem(6 * depth, size_y),
                mem(5 * depth, size_y),
                mem(size_x, LANES),
                mem(size_x, LANES),
                mem(depth, LANES),
                mem(depth, LANES),
                *edges(3, 3),
                *edges(3, 3),
                mem(depth, LANES),
                mem(depth, LANES),
                mem(LANES, LANES),
                mem(LANES, size_y),
                mem(LANES, LANES),
                mem(SPLIT_Z * 8, LANES),
                mem(3, depth, size_y),
                mem(3, size_x, LANES),
                mem(5, depth, size_y),
                mem(5, size_x, LANES),
                pltpu.SemaphoreType.DMA((7,)),
                pltpu.SemaphoreType.DMA((5,)),
                pltpu.SemaphoreType.DMA((5,)),
                pltpu.SemaphoreType.DMA((12,)),
                pltpu.SemaphoreType.DMA((12,)),
            ],
            compiler_params=pltpu.CompilerParams(
                collective_id=0, has_side_effects=True, vmem_limit_bytes=48 * 1024 * 1024
            ),
        )(*(pltpu.with_memory_space_constraint(x, pltpu.HBM) for x in inputs))
        hbm = pl.BlockSpec(memory_space=pltpu.HBM)
        return pl.pallas_call(
            hand_over,
            out_shape=tuple(jax.ShapeDtypeStruct(x.shape, x.dtype) for x in state),
            in_specs=[pl.BlockSpec(memory_space=pl.ANY)] * 3,
            out_specs=(hbm, hbm, hbm),
            scratch_shapes=[pltpu.SemaphoreType.DMA((3,))],
        )(*(pltpu.with_memory_space_constraint(x, pltpu.VMEM) for x in state))

    in_specs = (
        P(None, None, "chord", "span"),
        P(None, None, "chord", "span"),
        P(None, "chord", "span"),
        P(),
        P(("chord", "span"), None),
        P(),
        P(),
    )
    out_specs = (
        P(None, None, "chord", "span"),
        P(None, None, "chord", "span"),
        P(("chord", "span"), None),
    )
    return jax.shard_map(local, mesh=mesh, in_specs=in_specs, out_specs=out_specs, check_vma=False)
```

```python
import functools

import jax
import jax.numpy as jnp
from jax import lax
from jax.experimental import pallas as pl
from jax.experimental.pallas import tpu as pltpu
from jax.sharding import PartitionSpec as P

MESH = pl.DeviceIdType.MESH
F32 = jnp.float32
BF16 = jnp.bfloat16
DT = 0.5
SLOTS = 16
PATCH = 8
LANES = 128
SPLIT_X_HI, SPLIT_Z, SPLIT_CORE = 2, 8, 2
C11, C12, C13, C22, C23, C33, C44, C55, C66, BUOY = range(10)
XX, YY, ZZ, YZ, XZ, XY = range(6)


def iota(shape, dim):
    return lax.broadcasted_iota(jnp.int32, shape, dim)


def fiota(shape, dim):
    return iota(shape, dim).astype(F32)


def split(x):
    a = x.astype(BF16)
    return a, (x - a.astype(F32)).astype(BF16)


def dot(a, b, contract=((1,), (0,))):
    return lax.dot_general(a, b, (contract, ((), ())), preferred_element_type=F32)


def kernel(
    n_chord,
    n_span,
    vel_in,
    str_in,
    mat_in,
    moduli_in,
    drive_in,
    owner_in,
    cells_in,
    v,
    s,
    rec_out,
    mat,
    moduli,
    drive,
    owner,
    cells,
    coef,
    onehot_y,
    slot_x,
    slot_y,
    plane,
    ranks,
    taken,
    taken_t,
    gathered,
    send2,
    routed2,
    send3,
    routed3,
    rec_send,
    rec_rows,
    rec_back,
    rec_got,
    to_dn,
    to_up,
    to_rt,
    to_lt,
    from_up,
    from_dn,
    from_lt,
    from_rt,
    corner_up,
    corner_dn,
    vto_dn,
    vto_up,
    vto_rt,
    vto_lt,
    vfrom_up,
    vfrom_dn,
    vfrom_lt,
    vfrom_rt,
    vcorner_up,
    vcorner_dn,
    aux_t,
    off_y,
    off_x,
    edge_pick,
    halo_row,
    halo_col,
    hcoef_row,
    hcoef_col,
    load_sem,
    group_send,
    group_recv,
    edge_send,
    edge_recv,
):
    c = lax.axis_index("chord")
    sp = lax.axis_index("span")
    depth = vel_in.shape[1]
    size_x = vel_in.shape[2]
    size_y = vel_in.shape[3]
    half = size_y - LANES
    n_z = SPLIT_Z
    n_p = n_chord * SPLIT_X_HI * SPLIT_CORE
    my_z = lax.rem(lax.div(sp, SPLIT_CORE), SPLIT_Z)
    x_hi = lax.div(sp, SPLIT_Z * SPLIT_CORE)
    my_p = (c * SPLIT_X_HI + x_hi) * SPLIT_CORE + lax.rem(sp, SPLIT_CORE)
    xor = jnp.bitwise_xor

    def p_partner(i):
        core, high, to_c = i % SPLIT_CORE, i // SPLIT_CORE % SPLIT_X_HI, i // SPLIT_CORE // SPLIT_X_HI
        return xor(c, to_c), xor(sp, high * SPLIT_Z * SPLIT_CORE + core)

    def z_partner(i):
        return c, xor(sp, i * SPLIT_CORE)

    has_up, has_dn = c > 0, c < n_chord - 1
    has_lt, has_rt = sp > 0, sp < n_span - 1
    diag_up = jnp.logical_and(has_up, has_rt)
    diag_dn = jnp.logical_and(has_dn, has_lt)

    pairs = [
        (drive_in, drive),
        (vel_in, v),
        (str_in, s),
        (mat_in, mat),
        (owner_in, owner),
        (cells_in.at[pl.ds(0, 8)], cells),
        (moduli_in, moduli),
    ]
    loads = [pltpu.make_async_copy(a, b, load_sem.at[i]) for i, (a, b) in enumerate(pairs)]
    loads[0].start()

    barrier = pltpu.get_barrier_semaphore()

    def greet(to_c, to_s):
        pl.semaphore_signal(barrier, inc=1, device_id=(to_c, to_s), device_id_type=MESH)

    ring = (0, 1, 2, 1)

    def p_hops(i):
        core, high, to_c = i % SPLIT_CORE, i // SPLIT_CORE % SPLIT_X_HI, i // SPLIT_CORE // SPLIT_X_HI
        return 4 * (ring[2 * high + to_c % 2] + ring[to_c // 2 % 4]) + core

    p_order = sorted(range(1, n_p), key=p_hops, reverse=True)
    z_order = sorted(range(1, n_z), key=lambda i: (0, 1, 2, 3, 4, 3, 2, 3)[i], reverse=True)
    for i in p_order:
        greet(*p_partner(i))
    for i in z_order:
        greet(*z_partner(i))
    sides = [
        (has_up, (c - 1, sp)),
        (has_dn, (c + 1, sp)),
        (has_lt, (c, sp - 1)),
        (has_rt, (c, sp + 1)),
        (diag_up, (c - 1, sp + 1)),
        (diag_dn, (c + 1, sp - 1)),
    ]
    for there, to in sides:
        pl.when(there)(functools.partial(greet, *to))
    for load in loads[1:]:
        load.start()

    @pl.when(jnp.logical_not(has_up))
    def _():
        for ref in (from_up, vfrom_up):
            ref[...] = jnp.zeros_like(ref)

    @pl.when(jnp.logical_not(has_dn))
    def _():
        for ref in (from_dn, vfrom_dn):
            ref[...] = jnp.zeros_like(ref)

    @pl.when(jnp.logical_not(has_lt))
    def _():
        for ref in (from_lt, vfrom_lt):
            ref[...] = jnp.zeros_like(ref)

    @pl.when(jnp.logical_not(has_rt))
    def _():
        for ref in (from_rt, vfrom_rt):
            ref[...] = jnp.zeros_like(ref)

    @pl.when(jnp.logical_not(diag_up))
    def _():
        for ref in (corner_up, vcorner_up):
            ref[...] = jnp.zeros_like(ref)

    @pl.when(jnp.logical_not(diag_dn))
    def _():
        for ref in (corner_dn, vcorner_dn):
            ref[...] = jnp.zeros_like(ref)

    pl.semaphore_wait(
        barrier,
        n_p + n_z - 2 + sum(there.astype(jnp.int32) for there, _ in sides),
    )

    def send(source, target, to, sem):
        return pltpu.make_async_remote_copy(
            src_ref=source,
            dst_ref=target,
            send_sem=group_send.at[sem],
            recv_sem=group_recv.at[sem],
            device_id=to,
            device_id_type=MESH,
        )

    def wait_all(ref, count, sems, sem):
        if count:
            part = ref.at[pl.ds(0, count)]
            pltpu.make_async_copy(part, part, sems.at[sem]).wait()

    def block(ref, index, count):
        return ref.at[pl.ds(pl.multiple_of(index * count, count), count)]

    per = drive.shape[0]
    loads[0].wait()
    for i in p_order:
        send(drive, block(gathered, my_p, per), p_partner(i), 0).start()
    gathered[pl.ds(pl.multiple_of(my_p * per, per), per), :] = drive[...]

    def edge(source, target, to, index):
        return pltpu.make_async_remote_copy(
            src_ref=source,
            dst_ref=target,
            send_sem=edge_send.at[index],
            recv_sem=edge_recv.at[index],
            device_id=to,
            device_id_type=MESH,
        )

    up, dn, lt, rt = (c - 1, sp), (c + 1, sp), (c, sp - 1), (c, sp + 1)

    def exchange(first, up_src, dn_src, lt_src, rt_src, up_dst, dn_dst, lt_dst, rt_dst, corners):
        moves = [
            (has_up, has_dn, edge(up_src, dn_dst, up, first)),
            (has_dn, has_up, edge(dn_src, up_dst, dn, first + 1)),
            (has_lt, has_rt, edge(lt_src, rt_dst, lt, first + 2)),
            (has_rt, has_lt, edge(rt_src, lt_dst, rt, first + 3)),
        ]
        corner_from_dn, corner_from_up = corners
        vy_corner = up_src.at[pl.ds(depth, depth), pl.ds(half, LANES)]
        vx_corner = dn_src.at[pl.ds(0, depth), pl.ds(0, LANES)]
        moves += [
            (diag_up, diag_dn, edge(vy_corner, corner_from_dn, (c - 1, sp + 1), first + 4)),
            (diag_dn, diag_up, edge(vx_corner, corner_from_up, (c + 1, sp - 1), first + 5)),
        ]

        def start():
            for goes, _, copy in moves:
                pl.when(goes)(copy.start)

        def arrive():
            for _, comes, copy in moves:
                pl.when(comes)(copy.wait_recv)

        def leave():
            for goes, _, copy in moves:
                pl.when(goes)(copy.wait_send)

        return start, arrive, leave

    start1, arrive1, leave1 = exchange(
        0, to_up, to_dn, to_lt, to_rt, from_up, from_dn, from_lt, from_rt, (corner_dn, corner_up)
    )
    start2, arrive2, leave2 = exchange(
        6, vto_up, vto_dn, vto_lt, vto_rt, vfrom_up, vfrom_dn, vfrom_lt, vfrom_rt, (vcorner_dn, vcorner_up)
    )

    def pack_rows(ref, row, fields):
        for z in range(depth):
            for k, read in enumerate(fields):
                ref[k * depth + z : k * depth + z + 1, :] = read(z, row)

    lane = iota((size_x, LANES), 1)
    row = iota((size_x, size_y), 0)

    def pack_cols(ref, column, fields):
        base = 0 if column == 0 else half
        at = column - base

        acc = jnp.zeros((size_x, LANES), F32)
        for z in range(depth):
            for k, read in enumerate(fields):
                to = k * depth + z
                by = (to + LANES - at) % LANES
                tile = read(z, base)
                moved = pltpu.roll(tile, by, 1) if by else tile
                acc = jnp.where(lane == to, moved, acc)
        ref[...] = acc

    def row_of(ref, comp):
        return lambda z, r: ref[comp, z, r : r + 1, :]

    def col_of(ref, comp):
        return lambda z, base: ref[comp, z, :, base : base + LANES]

    def mat_row(z, r):
        return mat[z, r : r + 1, :].astype(F32)

    def mat_col(z, base):
        return mat[z, :, base : base + LANES].astype(F32)

    v_rows = [row_of(v, k) for k in range(3)]
    v_cols = [col_of(v, k) for k in range(3)]

    for load in loads[1:]:
        load.wait()
    pack_rows(to_dn, size_x - 1, v_rows + [row_of(s, XY), row_of(s, XZ), mat_row])
    pack_rows(to_up, 0, v_rows + [row_of(s, XX), mat_row])
    pack_cols(to_rt, size_y - 1, v_cols + [col_of(s, XY), col_of(s, YZ), mat_col])
    pack_cols(to_lt, 0, v_cols + [col_of(s, YY), mat_col])
    start1()

    n_block = owner.shape[0]
    earlier = (iota((LANES, LANES), 0) < iota((LANES, LANES), 1)).astype(BF16)
    ones = jnp.ones((LANES, LANES), BF16)
    wanted = c * n_span + sp + (iota((n_z, LANES), 0) - my_z) * SPLIT_CORE
    same = jnp.concatenate(
        [(owner[a : a + 1, :] == wanted).astype(F32) for a in range(n_block)], axis=0
    )
    counts = dot(same.astype(BF16), jnp.concatenate([earlier, ones], axis=1))
    before = jnp.zeros((n_z, LANES), F32)
    chunk = SPLIT_CORE * per
    rank = jnp.full((n_z, LANES), -1.0, F32)
    lane8 = iota((n_z, LANES), 1)
    shift = size_y.bit_length() - 1
    aux = jnp.zeros((8, LANES), F32)
    aux_lane, aux_row = iota((8, LANES), 1), iota((8, LANES), 0)
    for a in range(n_block):
        at = slice(a * n_z, (a + 1) * n_z)
        rank_a = jnp.where(same[at] > 0.5, before + counts[at, :LANES], -1.0)
        before = before + counts[at, LANES:]
        ranks[at, :] = rank_a
        anchor = cells[0:1, a * LANES : (a + 1) * LANES]
        fields = (owner[a : a + 1, :], anchor >> shift, anchor & (size_y - 1))
        aux_a = jnp.zeros((8, LANES), F32)
        for k, field in enumerate(fields):
            aux_a = jnp.where(aux_row == k, field.astype(F32), aux_a)
        for h in range(SPLIT_X_HI):
            to = (a * SPLIT_X_HI + h) * chunk
            by = (to - h * SPLIT_Z * chunk) % LANES + LANES - my_z * chunk
            moved = pltpu.roll(rank_a, lax.rem(by, LANES), 1)
            rank = jnp.where(jnp.logical_and(lane8 >= to, lane8 < to + chunk), moved, rank)
            moved = pltpu.roll(aux_a, lax.rem(by, LANES), 1)
            aux = jnp.where(jnp.logical_and(aux_lane >= to, aux_lane < to + chunk), moved, aux)
    slot_ids = fiota((SLOTS, LANES), 0)
    for h in range(2):
        for k in range(n_z):
            at = (h * n_z + k) * 8
            ids = slot_ids[h * 8 : (h + 1) * 8]
            taken[at : at + 8, :] = (rank[k : k + 1, :] == ids).astype(F32)
    side_row = iota((n_z * 8, LANES), 0)
    side = side_row & 7
    to_z = side_row >> 3
    to_span = sp + (to_z - my_z) * SPLIT_CORE
    is_dn = jnp.logical_and((side & 1) == 0, side < 4)
    is_up = jnp.logical_and((side & 1) == 1, side < 4)
    is_rt = jnp.logical_and(side == 4, to_span < n_span - 1)
    is_lt = jnp.logical_and(side == 5, to_span > 0)
    whose = (c * n_span + to_span).astype(F32)
    at_owner, at_x, at_y = aux[0:1, :], aux[1:2, :], aux[2:3, :]
    reach = PATCH - 1
    edge_pick[...] = jnp.where(
        is_dn,
        jnp.logical_and(at_owner == whose + n_span, at_x == 0).astype(F32),
        jnp.where(
            is_up,
            jnp.logical_and(at_owner == whose - n_span, at_x == size_x - 1 - reach).astype(F32),
            jnp.where(
                is_rt,
                jnp.logical_and(at_owner == whose + 1, at_y == 0).astype(F32),
                jnp.where(
                    is_lt,
                    jnp.logical_and(at_owner == whose - 1, at_y == size_y - 1 - reach).astype(F32),
                    0.0,
                ),
            ),
        ),
    )
    aux_t[...] = jnp.transpose(jnp.concatenate([aux, jnp.zeros((LANES - 8, LANES), F32)], axis=0))
    off_x[...] = iota((LANES, LANES), 1) - aux_t[:, 1:2].astype(jnp.int32)
    off_y[...] = iota((LANES, size_y), 1) - aux_t[:, 2:3].astype(jnp.int32)

    taken_t[...] = jnp.transpose(taken[...])
    first_x = jnp.zeros((SLOTS, LANES), F32)
    first_y = jnp.zeros((SLOTS, LANES), F32)
    for a in range(n_block):
        anchor = cells[0:1, a * LANES : (a + 1) * LANES]
        hit = ranks[pl.ds(a * n_z + my_z, 1), :] == slot_ids
        first_x = first_x + jnp.where(hit, (anchor >> shift).astype(F32), 0.0)
        first_y = first_y + jnp.where(hit, (anchor & (size_y - 1)).astype(F32), 0.0)
    first_x = jnp.sum(first_x, axis=1, keepdims=True)
    first_y = jnp.sum(first_y, axis=1, keepdims=True)
    low = iota((8, LANES), 1) < 64
    cell_id = iota((8, LANES), 1) & 63
    slot_x[...] = jnp.where(low, first_x[0:8], first_x[8:16]) + (cell_id >> 3).astype(F32)
    slot_y[...] = jnp.where(low, first_y[0:8], first_y[8:16]) + (cell_id & 7).astype(F32)
    y_ids = fiota((size_y, LANES), 0)
    for t in range(8):
        onehot_y[:, t * LANES : (t + 1) * LANES] = (
            (slot_y[t : t + 1, :] == y_ids).astype(F32).astype(BF16)
        )
    x_ids = fiota((size_x, LANES), 0)

    def table(kind, index):
        out = jnp.full(kind.shape, DT * moduli[0, index], F32)
        for m in range(1, 4):
            out = jnp.where(kind == m, DT * moduli[m, index], out)
        return out

    def coef_layer(z, _):
        kind = mat[z]
        for k in range(10):
            coef[k, z] = table(kind, k)
        return 0

    lax.fori_loop(0, depth, coef_layer, 0)

    def along_x(field, by, edge_row):
        if by > 0:
            return jnp.where(row == 0, edge_row, pltpu.roll(field, 1, 0))
        return jnp.where(row == size_x - 1, edge_row, pltpu.roll(field, size_x - 1, 0))

    def along_y(field, by, edge_col):
        if by > 0:
            moved = pltpu.roll(field, 1, 1)
            head = jnp.where(lane == 0, edge_col, moved[:, :LANES])
            return jnp.concatenate([head, moved[:, LANES:]], axis=1)
        moved = pltpu.roll(field, size_y - 1, 1)
        tail = jnp.where(lane == LANES - 1, edge_col, moved[:, half:])
        return jnp.concatenate([moved[:, :half], tail], axis=1)

    def first_lane(ref, field, z):
        return pltpu.roll(ref[...], lax.rem(2 * LANES - (field * depth + z), LANES), 1)

    def last_lane(ref, field, z):
        return pltpu.roll(ref[...], lax.rem(2 * LANES - 1 - (field * depth + z), LANES), 1)

    bottom, top = 0, depth - 1

    def stress_layer(z, up_ref, dn_ref, lt_ref, rt_ref):
        is_bottom, is_top = isinstance(z, int) and z == bottom, isinstance(z, int) and z == top
        vx, vy, vz = v[0, z], v[1, z], v[2, z]
        zz = vz if is_bottom else vz - v[2, z - 1]
        zy = -vy if is_top else v[1, z + 1] - vy
        zx = -vx if is_top else v[0, z + 1] - vx
        if up_ref is None:
            vx_up = vy_dn = vz_dn = vy_lt = vx_rt = vz_rt = 0.0
        else:
            vx_up = up_ref[pl.ds(z, 1), :]
            vy_dn, vz_dn = dn_ref[pl.ds(depth + z, 1), :], dn_ref[pl.ds(2 * depth + z, 1), :]
            vy_lt = first_lane(lt_ref, 1, z)
            vx_rt, vz_rt = last_lane(rt_ref, 0, z), last_lane(rt_ref, 2, z)
        xx = vx - along_x(vx, 1, vx_up)
        yy = vy - along_y(vy, 1, vy_lt)
        yz = zy + (along_y(vz, -1, vz_rt) - vz)
        xz = zx + (along_x(vz, -1, vz_dn) - vz)
        xy = (along_y(vx, -1, vx_rt) - vx) + (
            along_x(vy, -1, vy_dn) - vy
        )
        s[XX, z] += coef[C11, z] * xx + coef[C12, z] * yy + coef[C13, z] * zz
        s[YY, z] += coef[C12, z] * xx + coef[C22, z] * yy + coef[C23, z] * zz
        s[ZZ, z] += coef[C13, z] * xx + coef[C23, z] * yy + coef[C33, z] * zz
        s[YZ, z] += coef[C44, z] * yz
        s[XZ, z] += coef[C55, z] * xz
        s[XY, z] += coef[C66, z] * xy

    def velocity_layer(z, comps=(0, 1, 2)):
        is_bottom, is_top = isinstance(z, int) and z == bottom, isinstance(z, int) and z == top
        sxx, syy, szz = s[XX, z], s[YY, z], s[ZZ, z]
        syz, sxz, sxy = s[YZ, z], s[XZ, z], s[XY, z]
        b = coef[BUOY, z]
        if 0 in comps:
            v[0, z] += b * (
                (along_x(sxx, -1, halo_row[0, pl.ds(z, 1), :]) - sxx)
                + (sxy - along_y(sxy, 1, first_lane(halo_col.at[1], 0, z)))
                + (sxz if is_bottom else sxz - s[XZ, z - 1])
            )
        if 1 in comps:
            v[1, z] += b * (
                (sxy - along_x(sxy, 1, halo_row[1, pl.ds(z, 1), :]))
                + (along_y(syy, -1, last_lane(halo_col.at[0], 0, z)) - syy)
                + (syz if is_bottom else syz - s[YZ, z - 1])
            )
        if 2 in comps:
            v[2, z] += b * (
                (sxz - along_x(sxz, 1, halo_row[2, pl.ds(z, 1), :]))
                + (syz - along_y(syz, 1, first_lane(halo_col.at[2], 0, z)))
                + (-szz if is_top else s[ZZ, z + 1] - szz)
            )

    wide = (depth, size_y)
    wide_lane = iota(wide, 1)
    wide_z = iota(wide, 0)

    def below_z(f):
        return jnp.where(wide_z == 0, 0.0, pltpu.roll(f, 1, 0))

    def above_z(f):
        return jnp.where(wide_z == depth - 1, 0.0, pltpu.roll(f, depth - 1, 0))

    def lane_below_z(f):
        return jnp.where(lane == 0, 0.0, pltpu.roll(f, 1, 1))

    def lane_above_z(f):
        return jnp.where(lane == depth - 1, 0.0, pltpu.roll(f, LANES - 1, 1))

    def to_lanes(corner, at):
        col = jnp.broadcast_to(corner[:, at : at + 1], (depth, LANES))
        here = iota((depth, LANES), 0) == iota((depth, LANES), 1)
        return jnp.sum(jnp.where(here, col, 0.0), axis=0, keepdims=True)

    def lanes_of(ref, field):
        if field == 0:
            return ref[...]
        return pltpu.roll(ref[...], LANES - field * depth, 1)

    narrow_row = iota((size_x, LANES), 0)

    def halo_stress(up_ref, dn_ref, lt_ref, rt_ref, cup, cdn, my_up, my_dn, my_lt, my_rt):
        def rows(ref, k):
            return ref[k * depth : (k + 1) * depth, :]

        vx, vy, vz = rows(dn_ref, 0), rows(dn_ref, 1), rows(dn_ref, 2)
        corner = jnp.broadcast_to(cdn[:, LANES - 1 : LANES], wide)
        vy_back = jnp.where(wide_lane == 0, corner, pltpu.roll(vy, 1, 1))
        halo_row[0] += (
            hcoef_row[0] * (vx - rows(my_dn, 0))
            + hcoef_row[1] * (vy - vy_back)
            + hcoef_row[2] * (vz - below_z(vz))
        )
        vx, vy, vz = rows(up_ref, 0), rows(up_ref, 1), rows(up_ref, 2)
        corner = jnp.broadcast_to(cup[:, 0:1], wide)
        vx_next = jnp.where(wide_lane == size_y - 1, corner, pltpu.roll(vx, size_y - 1, 1))
        halo_row[1] += hcoef_row[3] * ((vx_next - vx) + (rows(my_up, 1) - vy))
        halo_row[2] += hcoef_row[4] * ((above_z(vx) - vx) + (rows(my_up, 2) - vz))
        vx, vy, vz = lanes_of(rt_ref, 0), lanes_of(rt_ref, 1), lanes_of(rt_ref, 2)
        vx_back = jnp.where(narrow_row == 0, to_lanes(cup, 0), pltpu.roll(vx, 1, 0))
        halo_col[0] += (
            hcoef_col[0] * (vx - vx_back)
            + hcoef_col[1] * (vy - lanes_of(my_rt, 1))
            + hcoef_col[2] * (vz - lane_below_z(vz))
        )
        vx, vy, vz = lanes_of(lt_ref, 0), lanes_of(lt_ref, 1), lanes_of(lt_ref, 2)
        vy_next = jnp.where(
            narrow_row == size_x - 1, to_lanes(cdn, LANES - 1), pltpu.roll(vy, size_x - 1, 0)
        )
        halo_col[1] += hcoef_col[3] * ((lanes_of(my_lt, 0) - vx) + (vy_next - vy))
        halo_col[2] += hcoef_col[4] * ((lane_above_z(vy) - vy) + (lanes_of(my_lt, 2) - vz))

    def stress_inside(z, _):
        stress_layer(z, None, None, None, None)
        return 0

    stress_inside(bottom, 0)
    lax.fori_loop(bottom + 1, top, stress_inside, 0)
    stress_inside(top, 0)

    wait_all(gathered, (n_p - 1) * per, group_recv, 0)
    rows = gathered[...]
    pick = taken[...].astype(BF16)
    routes = sum(dot(pick, part) for part in split(rows))
    early, late = routes[: n_z * 8], routes[n_z * 8 :]
    low_all = iota((n_z * 8, LANES), 1) < 64
    force0 = jnp.where(low_all, early, pltpu.roll(late, 64, 1))
    force1 = jnp.where(low_all, pltpu.roll(early, 64, 1), late)
    for k in range(n_z):
        send2[k, 0:8, :] = force0[k * 8 : (k + 1) * 8]
        send2[k, 8:16, :] = force1[k * 8 : (k + 1) * 8]
    for i in z_order:
        send(send2.at[xor(my_z, i)], routed2.at[my_z], z_partner(i), 1).start()
    routed2[my_z] = send2[my_z]

    at_x0 = aux_t[:, 1:2] == 0.0
    at_y0 = aux_t[:, 2:3] == 0.0
    along_row = jnp.where(at_x0, rows, pltpu.roll(rows, LANES - PATCH * reach, 1))
    along_col = jnp.where(at_y0, rows, pltpu.roll(rows, LANES - reach, 1))
    in_row = jnp.logical_and(off_y[...] >= 0, off_y[...] < PATCH)
    at = jnp.where(in_row, off_y[...], 0)
    parts = [
        jnp.take_along_axis(along_row, at[:, k : k + LANES], axis=1)
        for k in range(0, size_y, LANES)
    ]
    row_line = jnp.where(in_row, jnp.concatenate(parts, axis=1), 0.0)
    in_col = jnp.logical_and(off_x[...] >= 0, off_x[...] < PATCH)
    at = jnp.where(in_col, off_x[...] * PATCH, 0)
    col_line = jnp.where(in_col, jnp.take_along_axis(along_col, at, axis=1), 0.0)
    lines = jnp.concatenate([row_line, col_line], axis=1)
    pick = edge_pick[...].astype(BF16)
    lines = sum(dot(pick, part) for part in split(lines))
    send3[...] = jnp.where(
        side < 2, lines[:, :LANES], jnp.where(side < 4, lines[:, LANES:size_y], lines[:, size_y:])
    )
    for i in z_order:
        send(block(send3, xor(my_z, i), 8), block(routed3, my_z, 8), z_partner(i), 2).start()
    own = pl.ds(pl.multiple_of(my_z * 8, 8), 8)
    routed3[own, :] = send3[own, :]

    arrive1()
    kind = from_dn[4 * depth : 5 * depth, :]
    inside = has_dn.astype(F32)
    for k, index in enumerate((C11, C12, C13)):
        hcoef_row[k] = table(kind, index) * inside
    kind = from_up[5 * depth : 6 * depth, :]
    inside = has_up.astype(F32)
    for k, index in enumerate((C66, C55)):
        hcoef_row[3 + k] = table(kind, index) * inside
    kind = lanes_of(from_rt, 4)
    inside = has_rt.astype(F32)
    for k, index in enumerate((C12, C22, C23)):
        hcoef_col[k] = table(kind, index) * inside
    kind = lanes_of(from_lt, 5)
    inside = has_lt.astype(F32)
    for k, index in enumerate((C66, C44)):
        hcoef_col[3 + k] = table(kind, index) * inside
    halo_row[0] = from_dn[3 * depth : 4 * depth, :]
    halo_row[1] = from_up[3 * depth : 4 * depth, :]
    halo_row[2] = from_up[4 * depth : 5 * depth, :]
    halo_col[0] = lanes_of(from_rt, 3)
    halo_col[1] = lanes_of(from_lt, 3)
    halo_col[2] = lanes_of(from_lt, 4)

    def velocity_body(z, _):
        velocity_layer(z)
        return 0

    last_x = size_x - 1
    for z in range(depth):
        vx_up = from_up[z : z + 1, :]
        vy_dn, vz_dn = (from_dn[k * depth + z : k * depth + z + 1, :] for k in (1, 2))
        for comp, index in ((XX, C11), (YY, C12), (ZZ, C13)):
            s[comp, z, 0:1, :] -= coef[index, z, 0:1, :] * vx_up
        s[XZ, z, last_x:, :] += coef[C55, z, last_x:, :] * vz_dn
        s[XY, z, last_x:, :] += coef[C66, z, last_x:, :] * vy_dn
        vy_lt = jnp.where(lane == 0, first_lane(from_lt, 1, z), 0.0)
        for comp, index in ((XX, C12), (YY, C22), (ZZ, C23)):
            s[comp, z, :, :LANES] -= coef[index, z, :, :LANES] * vy_lt
        vx_rt, vz_rt = (
            jnp.where(lane == LANES - 1, last_lane(from_rt, k, z), 0.0) for k in (0, 2)
        )
        s[YZ, z, :, half:] += coef[C44, z, :, half:] * vz_rt
        s[XY, z, :, half:] += coef[C66, z, :, half:] * vx_rt
    halo_stress(
        from_up, from_dn, from_lt, from_rt, corner_up, corner_dn, to_up, to_dn, to_lt, to_rt
    )
    velocity_layer(bottom)
    lax.fori_loop(bottom + 1, top, velocity_body, 0)
    velocity_layer(top)

    pack_rows(vto_dn, size_x - 1, v_rows)
    pack_rows(vto_up, 0, v_rows)
    pack_cols(vto_rt, size_y - 1, v_cols)
    pack_cols(vto_lt, 0, v_cols)
    start2()

    def in_slot(t):
        return slot_x[t : t + 1, :] == x_ids

    wait_all(routed2, n_z - 1, group_recv, 1)
    force = routed2[0]
    for k in range(1, n_z):
        force = force + routed2[k]
    wide_force = jnp.concatenate(
        [
            jnp.concatenate(
                [jnp.where(in_slot(t), f[t : t + 1, :], 0.0) for t in range(8)], axis=1
            )
            for f in (force[0:8], force[8:16])
        ],
        axis=0,
    )
    got = dot(jnp.concatenate(split(wide_force), axis=0), onehot_y[...], ((1,), (1,)))
    got = got[: 2 * size_x] + got[2 * size_x :]
    plane[...] = coef[BUOY, top] * got[size_x:]
    top0 = v[2, top] + coef[BUOY, top] * got[:size_x]
    v[2, top] = top0

    def sample(values, step):
        got = dot(jnp.concatenate(split(values), axis=0), onehot_y[...])
        got = got[:size_x] + got[size_x:]
        for t in range(8):
            chosen = jnp.where(in_slot(t), got[:, t * LANES : (t + 1) * LANES], 0.0)
            at = step * 8 + t
            rec_send[at : at + 1, :] = jnp.sum(chosen, axis=0, keepdims=True)

    sample(top0, 0)
    wait_all(routed3, (n_z - 1) * 8, group_recv, 2)
    lines = routed3[0:8, :]
    for k in range(1, n_z):
        lines = lines + routed3[k * 8 : (k + 1) * 8, :]
    top_row = 2 * depth + top
    arrive2()
    leave2()

    def buoyancy(kind):
        return table(kind, BUOY)

    wide_line = jnp.concatenate([lines[0:2], lines[2:4]], axis=1)
    kind = from_dn[4 * depth + top : 4 * depth + top + 1, :]
    vfrom_dn[top_row : top_row + 1, :] += buoyancy(kind) * wide_line[0:1]
    kind = from_up[5 * depth + top : 5 * depth + top + 1, :]
    vfrom_up[top_row : top_row + 1, :] += buoyancy(kind) * wide_line[1:2]
    diagonal = iota((size_x, LANES), 0) == lane

    def upright(line):
        return jnp.sum(jnp.where(diagonal, line, 0.0), axis=1, keepdims=True)

    kind = pltpu.roll(from_rt[...], (top_row - 4 * depth - top) % LANES, 1)
    vfrom_rt[...] += jnp.where(lane == top_row, buoyancy(kind) * upright(lines[4:5]), 0.0)
    kind = pltpu.roll(from_lt[...], (top_row - 5 * depth - top) % LANES, 1)
    vfrom_lt[...] += jnp.where(lane == top_row, buoyancy(kind) * upright(lines[5:6]), 0.0)
    vto_up[top_row : top_row + 1, :] = v[2, top, 0:1, :]
    vto_lt[...] = jnp.where(
        lane == top_row, pltpu.roll(v[2, top, :, :LANES], top_row, 1), vto_lt[...]
    )
    stress_layer(top, vfrom_up, vfrom_dn, vfrom_lt, vfrom_rt)
    halo_stress(
        vfrom_up,
        vfrom_dn,
        vfrom_lt,
        vfrom_rt,
        vcorner_up,
        vcorner_dn,
        vto_up,
        vto_dn,
        vto_lt,
        vto_rt,
    )
    velocity_layer(top, (2,))
    top1 = v[2, top] + plane[...]
    v[2, top] = top1

    sample(top1, 1)
    for i in z_order:
        send(rec_send, rec_rows.at[my_z], z_partner(i), 3).start()
    rec_rows[my_z] = rec_send[...]

    pick = taken_t[...].astype(BF16)
    wait_all(rec_rows, n_z - 1, group_recv, 3)
    early = rec_rows[:, 0:8, :].reshape(n_z * 8, LANES)
    late = rec_rows[:, 8:16, :].reshape(n_z * 8, LANES)
    both = jnp.concatenate(
        [
            jnp.where(low_all, early, pltpu.roll(late, 64, 1)),
            jnp.where(low_all, pltpu.roll(early, 64, 1), late),
        ],
        axis=0,
    )
    back = sum(dot(pick, part) for part in split(both))
    rec_back[...] = back
    for i in p_order:
        send(block(rec_back, xor(my_p, i), per), block(rec_got, my_p, per), p_partner(i), 4).start()
    mine = pl.ds(pl.multiple_of(my_p * per, per), per)
    rec_got[mine, :] = rec_back[mine, :]
    def stress_second(z, _):
        stress_layer(z, vfrom_up, vfrom_dn, vfrom_lt, vfrom_rt)
        return 0

    stress_second(bottom, 0)
    lax.fori_loop(bottom + 1, top, stress_second, 0)
    velocity_layer(bottom)
    lax.fori_loop(bottom + 1, top, velocity_body, 0)
    velocity_layer(top, (0, 1))

    leave1()
    wait_all(gathered, (n_p - 1) * per, group_send, 0)
    wait_all(routed2, n_z - 1, group_send, 1)
    wait_all(routed3, (n_z - 1) * 8, group_send, 2)
    wait_all(rec_rows, n_z - 1, group_send, 3)
    wait_all(rec_got, (n_p - 1) * per, group_recv, 4)
    tile = max(per, 8)
    parts = [rec_got[i * tile : (i + 1) * tile, :] for i in range(n_p * per // tile)]
    while len(parts) > 1:
        parts = [a + b for a, b in zip(parts[::2], parts[1::2])]
    out = parts[0][:per]
    for i in range(1, tile // per):
        out = out + parts[0][i * per : (i + 1) * per]
    rec_out[...] = out

    wait_all(rec_got, (n_p - 1) * per, group_send, 4)


def hand_over(v, s, rec, vel_out, str_out, rec_out, sem):
    pairs = [(v, vel_out), (s, str_out), (rec, rec_out)]
    copies = [pltpu.make_async_copy(a, b, sem.at[i]) for i, (a, b) in enumerate(pairs)]
    for copy in copies:
        copy.start()
    for copy in copies:
        copy.wait()


def solution(mesh):
    n_chord, n_span = mesh.shape["chord"], mesh.shape["span"]

    def local(velocity, stress, material, moduli, drive, owner, cells):
        _, depth, size_x, size_y = velocity.shape
        per = drive.shape[0]

        def mem(*shape):
            return pltpu.VMEM(shape, F32)

        def edges(rows_dn, rows_up):
            return [
                mem(rows_dn * depth, size_y),
                mem(rows_up * depth, size_y),
                mem(size_x, LANES),
                mem(size_x, LANES),
            ]

        layer = (size_x, size_y)
        vmem = pl.BlockSpec(memory_space=pltpu.VMEM)
        slots = SPLIT_Z * SLOTS
        n_p = n_chord * SPLIT_X_HI * SPLIT_CORE
        inputs = (velocity, stress, material, moduli, drive, owner.reshape(-1, LANES), cells.T)
        state = pl.pallas_call(
            functools.partial(kernel, n_chord, n_span),
            out_shape=(
                jax.ShapeDtypeStruct(velocity.shape, F32),
                jax.ShapeDtypeStruct(stress.shape, F32),
                jax.ShapeDtypeStruct(drive.shape, F32),
            ),
            in_specs=[pl.BlockSpec(memory_space=pltpu.HBM)] * 7,
            out_specs=(vmem, vmem, vmem),
            scratch_shapes=[
                pltpu.VMEM((depth, *layer), jnp.int32),
                pltpu.SMEM(moduli.shape, F32),
                mem(*drive.shape),
                pltpu.VMEM((owner.size // LANES, LANES), jnp.int32),
                pltpu.VMEM((8, owner.size), jnp.int32),
                mem(10, depth, *layer),
                pltpu.VMEM((size_y, 8 * LANES), BF16),
                mem(8, LANES),
                mem(8, LANES),
                mem(*layer),
                mem(owner.size // LANES * SPLIT_Z, LANES),
                mem(slots, LANES),
                mem(LANES, slots),
                mem(n_p * per, LANES),
                mem(SPLIT_Z, 16, LANES),
                mem(SPLIT_Z, 16, LANES),
                mem(slots // 2, LANES),
                mem(slots // 2, LANES),
                mem(SLOTS, LANES),
                mem(SPLIT_Z, SLOTS, LANES),
                mem(n_p * per, LANES),
                mem(n_p * per, LANES),
                *edges(6, 5),
                mem(6 * depth, size_y),
                mem(5 * depth, size_y),
                mem(size_x, LANES),
                mem(size_x, LANES),
                mem(depth, LANES),
                mem(depth, LANES),
                *edges(3, 3),
                *edges(3, 3),
                mem(depth, LANES),
                mem(depth, LANES),
                mem(LANES, LANES),
                pltpu.VMEM((LANES, size_y), jnp.int32),
                pltpu.VMEM((LANES, LANES), jnp.int32),
                mem(SPLIT_Z * 8, LANES),
                mem(3, depth, size_y),
                mem(3, size_x, LANES),
                mem(5, depth, size_y),
                mem(5, size_x, LANES),
                pltpu.SemaphoreType.DMA((7,)),
                pltpu.SemaphoreType.DMA((5,)),
                pltpu.SemaphoreType.DMA((5,)),
                pltpu.SemaphoreType.DMA((12,)),
                pltpu.SemaphoreType.DMA((12,)),
            ],
            compiler_params=pltpu.CompilerParams(
                collective_id=0, has_side_effects=True, vmem_limit_bytes=48 * 1024 * 1024
            ),
        )(*(pltpu.with_memory_space_constraint(x, pltpu.HBM) for x in inputs))
        hbm = pl.BlockSpec(memory_space=pltpu.HBM)
        return pl.pallas_call(
            hand_over,
            out_shape=tuple(jax.ShapeDtypeStruct(x.shape, x.dtype) for x in state),
            in_specs=[pl.BlockSpec(memory_space=pl.ANY)] * 3,
            out_specs=(hbm, hbm, hbm),
            scratch_shapes=[pltpu.SemaphoreType.DMA((3,))],
        )(*(pltpu.with_memory_space_constraint(x, pltpu.VMEM) for x in state))

    in_specs = (
        P(None, None, "chord", "span"),
        P(None, None, "chord", "span"),
        P(None, "chord", "span"),
        P(),
        P(("chord", "span"), None),
        P(),
        P(),
    )
    out_specs = (
        P(None, None, "chord", "span"),
        P(None, None, "chord", "span"),
        P(("chord", "span"), None),
    )
    return jax.shard_map(local, mesh=mesh, in_specs=in_specs, out_specs=out_specs, check_vma=False)
```

```python
import functools

import jax
import jax.numpy as jnp
from jax import lax
from jax.experimental import pallas as pl
from jax.experimental.pallas import tpu as pltpu
from jax.sharding import PartitionSpec as P

MESH = pl.DeviceIdType.MESH
F32 = jnp.float32
BF16 = jnp.bfloat16
DT = 0.5
SLOTS = 16
PATCH = 8
LANES = 128
SPLIT_X_HI, SPLIT_Z, SPLIT_CORE = 2, 8, 2
C11, C12, C13, C22, C23, C33, C44, C55, C66, BUOY = range(10)
XX, YY, ZZ, YZ, XZ, XY = range(6)


def iota(shape, dim):
    return lax.broadcasted_iota(jnp.int32, shape, dim)


def fiota(shape, dim):
    return iota(shape, dim).astype(F32)


def split(x):
    a = x.astype(BF16)
    return a, (x - a.astype(F32)).astype(BF16)


def dot(a, b, contract=((1,), (0,))):
    return lax.dot_general(a, b, (contract, ((), ())), preferred_element_type=F32)


def kernel(
    n_chord,
    n_span,
    vel_in,
    str_in,
    mat_in,
    moduli_in,
    drive_in,
    owner_in,
    cells_in,
    v,
    s,
    rec_out,
    mat,
    moduli,
    drive,
    owner,
    cells,
    coef,
    onehot_y,
    slot_x,
    slot_y,
    plane,
    ranks,
    taken,
    pick_out,
    pick_back,
    pick_edge,
    gathered,
    send2,
    routed2,
    send3,
    routed3,
    rec_send,
    rec_rows,
    rec_back,
    rec_got,
    to_dn,
    to_up,
    to_rt,
    to_lt,
    from_up,
    from_dn,
    from_lt,
    from_rt,
    corner_up,
    corner_dn,
    vto_dn,
    vto_up,
    vto_rt,
    vto_lt,
    vfrom_up,
    vfrom_dn,
    vfrom_lt,
    vfrom_rt,
    vcorner_up,
    vcorner_dn,
    aux_t,
    off_y,
    off_x,
    edge_pick,
    halo_row,
    halo_col,
    hcoef_row,
    hcoef_col,
    load_sem,
    group_send,
    group_recv,
    edge_send,
    edge_recv,
):
    c = lax.axis_index("chord")
    sp = lax.axis_index("span")
    depth = vel_in.shape[1]
    size_x = vel_in.shape[2]
    size_y = vel_in.shape[3]
    half = size_y - LANES
    n_z = SPLIT_Z
    n_p = n_chord * SPLIT_X_HI * SPLIT_CORE
    my_z = lax.rem(lax.div(sp, SPLIT_CORE), SPLIT_Z)
    x_hi = lax.div(sp, SPLIT_Z * SPLIT_CORE)
    my_p = (c * SPLIT_X_HI + x_hi) * SPLIT_CORE + lax.rem(sp, SPLIT_CORE)
    xor = jnp.bitwise_xor

    def p_partner(i):
        core, high, to_c = i % SPLIT_CORE, i // SPLIT_CORE % SPLIT_X_HI, i // SPLIT_CORE // SPLIT_X_HI
        return xor(c, to_c), xor(sp, high * SPLIT_Z * SPLIT_CORE + core)

    def z_partner(i):
        return c, xor(sp, i * SPLIT_CORE)

    has_up, has_dn = c > 0, c < n_chord - 1
    has_lt, has_rt = sp > 0, sp < n_span - 1
    diag_up = jnp.logical_and(has_up, has_rt)
    diag_dn = jnp.logical_and(has_dn, has_lt)

    pairs = [
        (drive_in, drive),
        (vel_in, v),
        (str_in, s),
        (mat_in, mat),
        (owner_in, owner),
        (cells_in.at[pl.ds(0, 8)], cells),
        (moduli_in, moduli),
    ]
    loads = [pltpu.make_async_copy(a, b, load_sem.at[i]) for i, (a, b) in enumerate(pairs)]
    loads[0].start()

    barrier = pltpu.get_barrier_semaphore()

    def greet(to_c, to_s):
        pl.semaphore_signal(barrier, inc=1, device_id=(to_c, to_s), device_id_type=MESH)

    ring = (0, 1, 2, 1)

    def p_hops(i):
        core, high, to_c = i % SPLIT_CORE, i // SPLIT_CORE % SPLIT_X_HI, i // SPLIT_CORE // SPLIT_X_HI
        return 4 * (ring[2 * high + to_c % 2] + ring[to_c // 2 % 4]) + core

    p_order = sorted(range(1, n_p), key=p_hops, reverse=True)
    z_order = sorted(range(1, n_z), key=lambda i: (0, 1, 2, 3, 4, 3, 2, 3)[i], reverse=True)
    for i in p_order:
        greet(*p_partner(i))
    for i in z_order:
        greet(*z_partner(i))
    sides = [
        (has_lt, (c, sp - 1)),
        (has_rt, (c, sp + 1)),
        (diag_up, (c - 1, sp + 1)),
        (diag_dn, (c + 1, sp - 1)),
    ]
    for there, to in sides:
        pl.when(there)(functools.partial(greet, *to))
    for load in loads[1:]:
        load.start()

    @pl.when(jnp.logical_not(has_up))
    def _():
        for ref in (from_up, vfrom_up):
            ref[...] = jnp.zeros_like(ref)

    @pl.when(jnp.logical_not(has_dn))
    def _():
        for ref in (from_dn, vfrom_dn):
            ref[...] = jnp.zeros_like(ref)

    @pl.when(jnp.logical_not(has_lt))
    def _():
        for ref in (from_lt, vfrom_lt):
            ref[...] = jnp.zeros_like(ref)

    @pl.when(jnp.logical_not(has_rt))
    def _():
        for ref in (from_rt, vfrom_rt):
            ref[...] = jnp.zeros_like(ref)

    @pl.when(jnp.logical_not(diag_up))
    def _():
        for ref in (corner_up, vcorner_up):
            ref[...] = jnp.zeros_like(ref)

    @pl.when(jnp.logical_not(diag_dn))
    def _():
        for ref in (corner_dn, vcorner_dn):
            ref[...] = jnp.zeros_like(ref)

    pl.semaphore_wait(
        barrier,
        n_p + n_z - 2 + sum(there.astype(jnp.int32) for there, _ in sides),
    )

    def send(source, target, to, sem):
        return pltpu.make_async_remote_copy(
            src_ref=source,
            dst_ref=target,
            send_sem=group_send.at[sem],
            recv_sem=group_recv.at[sem],
            device_id=to,
            device_id_type=MESH,
        )

    def wait_all(ref, count, sems, sem):
        if count:
            part = ref.at[pl.ds(0, count)]
            pltpu.make_async_copy(part, part, sems.at[sem]).wait()

    def block(ref, index, count):
        return ref.at[pl.ds(pl.multiple_of(index * count, count), count)]

    per = drive.shape[0]
    loads[0].wait()
    for i in p_order:
        send(drive, block(gathered, my_p, per), p_partner(i), 0).start()
    gathered[pl.ds(pl.multiple_of(my_p * per, per), per), :] = drive[...]

    def edge(source, target, to, index):
        return pltpu.make_async_remote_copy(
            src_ref=source,
            dst_ref=target,
            send_sem=edge_send.at[index],
            recv_sem=edge_recv.at[index],
            device_id=to,
            device_id_type=MESH,
        )

    up, dn, lt, rt = (c - 1, sp), (c + 1, sp), (c, sp - 1), (c, sp + 1)

    def exchange(first, up_src, dn_src, lt_src, rt_src, up_dst, dn_dst, lt_dst, rt_dst, corners):
        moves = [
            (has_up, has_dn, edge(up_src, dn_dst, up, first)),
            (has_dn, has_up, edge(dn_src, up_dst, dn, first + 1)),
            (has_lt, has_rt, edge(lt_src, rt_dst, lt, first + 2)),
            (has_rt, has_lt, edge(rt_src, lt_dst, rt, first + 3)),
        ]
        corner_from_dn, corner_from_up = corners
        vy_corner = up_src.at[pl.ds(depth, depth), pl.ds(half, LANES)]
        vx_corner = dn_src.at[pl.ds(0, depth), pl.ds(0, LANES)]
        moves += [
            (diag_up, diag_dn, edge(vy_corner, corner_from_dn, (c - 1, sp + 1), first + 4)),
            (diag_dn, diag_up, edge(vx_corner, corner_from_up, (c + 1, sp - 1), first + 5)),
        ]

        def start():
            for goes, _, copy in moves:
                pl.when(goes)(copy.start)

        def arrive():
            for _, comes, copy in moves:
                pl.when(comes)(copy.wait_recv)

        def leave():
            for goes, _, copy in moves:
                pl.when(goes)(copy.wait_send)

        return start, arrive, leave

    start1, arrive1, leave1 = exchange(
        0, to_up, to_dn, to_lt, to_rt, from_up, from_dn, from_lt, from_rt, (corner_dn, corner_up)
    )
    start2, arrive2, leave2 = exchange(
        6, vto_up, vto_dn, vto_lt, vto_rt, vfrom_up, vfrom_dn, vfrom_lt, vfrom_rt, (vcorner_dn, vcorner_up)
    )

    def pack_rows(ref, row, fields):
        for z in range(depth):
            for k, read in enumerate(fields):
                ref[k * depth + z : k * depth + z + 1, :] = read(z, row)

    lane = iota((size_x, LANES), 1)
    row = iota((size_x, size_y), 0)

    def pack_cols(ref, column, fields):
        base = 0 if column == 0 else half
        at = column - base

        acc = jnp.zeros((size_x, LANES), F32)
        for z in range(depth):
            for k, read in enumerate(fields):
                to = k * depth + z
                by = (to + LANES - at) % LANES
                tile = read(z, base)
                moved = pltpu.roll(tile, by, 1) if by else tile
                acc = jnp.where(lane == to, moved, acc)
        ref[...] = acc

    def row_of(ref, comp):
        return lambda z, r: ref[comp, z, r : r + 1, :]

    def col_of(ref, comp):
        return lambda z, base: ref[comp, z, :, base : base + LANES]

    def mat_row(z, r):
        return mat[z, r : r + 1, :].astype(F32)

    def mat_col(z, base):
        return mat[z, :, base : base + LANES].astype(F32)

    v_rows = [row_of(v, k) for k in range(3)]
    v_cols = [col_of(v, k) for k in range(3)]

    for load in loads[1:]:
        load.wait()
    pack_rows(to_dn, size_x - 1, v_rows + [row_of(s, XY), row_of(s, XZ), mat_row])
    pack_rows(to_up, 0, v_rows + [row_of(s, XX), mat_row])
    pack_cols(to_rt, size_y - 1, v_cols + [col_of(s, XY), col_of(s, YZ), mat_col])
    pack_cols(to_lt, 0, v_cols + [col_of(s, YY), mat_col])
    start1()

    n_block = owner.shape[0]
    earlier = (iota((LANES, LANES), 0) < iota((LANES, LANES), 1)).astype(BF16)
    ones = jnp.ones((LANES, LANES), BF16)
    wanted = c * n_span + sp + (iota((n_z, LANES), 0) - my_z) * SPLIT_CORE
    same = jnp.concatenate(
        [(owner[a : a + 1, :] == wanted).astype(F32) for a in range(n_block)], axis=0
    )
    counts = dot(same.astype(BF16), jnp.concatenate([earlier, ones], axis=1))
    before = jnp.zeros((n_z, LANES), F32)
    chunk = SPLIT_CORE * per
    rank = jnp.full((n_z, LANES), -1.0, F32)
    lane8 = iota((n_z, LANES), 1)
    shift = size_y.bit_length() - 1
    aux = jnp.zeros((8, LANES), F32)
    aux_lane, aux_row = iota((8, LANES), 1), iota((8, LANES), 0)
    for a in range(n_block):
        at = slice(a * n_z, (a + 1) * n_z)
        rank_a = jnp.where(same[at] > 0.5, before + counts[at, :LANES], -1.0)
        before = before + counts[at, LANES:]
        ranks[at, :] = rank_a
        anchor = cells[0:1, a * LANES : (a + 1) * LANES]
        fields = (owner[a : a + 1, :], anchor >> shift, anchor & (size_y - 1))
        aux_a = jnp.zeros((8, LANES), F32)
        for k, field in enumerate(fields):
            aux_a = jnp.where(aux_row == k, field.astype(F32), aux_a)
        for h in range(SPLIT_X_HI):
            to = (a * SPLIT_X_HI + h) * chunk
            by = (to - h * SPLIT_Z * chunk) % LANES + LANES - my_z * chunk
            moved = pltpu.roll(rank_a, lax.rem(by, LANES), 1)
            rank = jnp.where(jnp.logical_and(lane8 >= to, lane8 < to + chunk), moved, rank)
            moved = pltpu.roll(aux_a, lax.rem(by, LANES), 1)
            aux = jnp.where(jnp.logical_and(aux_lane >= to, aux_lane < to + chunk), moved, aux)
    slot_ids = fiota((SLOTS, LANES), 0)
    for h in range(2):
        for k in range(n_z):
            at = (h * n_z + k) * 8
            ids = slot_ids[h * 8 : (h + 1) * 8]
            taken[at : at + 8, :] = (rank[k : k + 1, :] == ids).astype(F32)
    side_row = iota((n_z * 8, LANES), 0)
    side = side_row & 7
    to_z = side_row >> 3
    to_span = sp + (to_z - my_z) * SPLIT_CORE
    is_dn = jnp.logical_and((side & 1) == 0, side < 4)
    is_up = jnp.logical_and((side & 1) == 1, side < 4)
    is_rt = jnp.logical_and(side == 4, to_span < n_span - 1)
    is_lt = jnp.logical_and(side == 5, to_span > 0)
    whose = (c * n_span + to_span).astype(F32)
    at_owner, at_x, at_y = aux[0:1, :], aux[1:2, :], aux[2:3, :]
    reach = PATCH - 1
    edge_pick[...] = jnp.where(
        is_dn,
        jnp.logical_and(at_owner == whose + n_span, at_x == 0).astype(F32),
        jnp.where(
            is_up,
            jnp.logical_and(at_owner == whose - n_span, at_x == size_x - 1 - reach).astype(F32),
            jnp.where(
                is_rt,
                jnp.logical_and(at_owner == whose + 1, at_y == 0).astype(F32),
                jnp.where(
                    is_lt,
                    jnp.logical_and(at_owner == whose - 1, at_y == size_y - 1 - reach).astype(F32),
                    0.0,
                ),
            ),
        ),
    )
    aux_t[...] = jnp.transpose(jnp.concatenate([aux, jnp.zeros((LANES - 8, LANES), F32)], axis=0))
    off_x[...] = iota((LANES, LANES), 1) - aux_t[:, 1:2].astype(jnp.int32)
    off_y[...] = iota((LANES, size_y), 1) - aux_t[:, 2:3].astype(jnp.int32)

    pick_out[...] = taken[...].astype(BF16)
    pick_back[...] = jnp.transpose(taken[...]).astype(BF16)
    pick_edge[...] = edge_pick[...].astype(BF16)
    first_x = jnp.zeros((SLOTS, LANES), F32)
    first_y = jnp.zeros((SLOTS, LANES), F32)
    for a in range(n_block):
        anchor = cells[0:1, a * LANES : (a + 1) * LANES]
        hit = ranks[pl.ds(a * n_z + my_z, 1), :] == slot_ids
        first_x = first_x + jnp.where(hit, (anchor >> shift).astype(F32), 0.0)
        first_y = first_y + jnp.where(hit, (anchor & (size_y - 1)).astype(F32), 0.0)
    first_x = jnp.sum(first_x, axis=1, keepdims=True)
    first_y = jnp.sum(first_y, axis=1, keepdims=True)
    low = iota((8, LANES), 1) < 64
    cell_id = iota((8, LANES), 1) & 63
    slot_x[...] = jnp.where(low, first_x[0:8], first_x[8:16]) + (cell_id >> 3).astype(F32)
    slot_y[...] = jnp.where(low, first_y[0:8], first_y[8:16]) + (cell_id & 7).astype(F32)
    y_ids = fiota((size_y, LANES), 0)
    for t in range(8):
        onehot_y[:, t * LANES : (t + 1) * LANES] = (
            (slot_y[t : t + 1, :] == y_ids).astype(F32).astype(BF16)
        )
    x_ids = fiota((size_x, LANES), 0)

    def table(kind, index):
        out = jnp.full(kind.shape, DT * moduli[0, index], F32)
        for m in range(1, 4):
            out = jnp.where(kind == m, DT * moduli[m, index], out)
        return out

    def coef_layer(z, _):
        kind = mat[z]
        for k in range(10):
            coef[k, z] = table(kind, k)
        return 0

    lax.fori_loop(0, depth, coef_layer, 0)

    def along_x(field, by, edge_row):
        if by > 0:
            return jnp.where(row == 0, edge_row, pltpu.roll(field, 1, 0))
        return jnp.where(row == size_x - 1, edge_row, pltpu.roll(field, size_x - 1, 0))

    def along_y(field, by, edge_col):
        if by > 0:
            moved = pltpu.roll(field, 1, 1)
            head = jnp.where(lane == 0, edge_col, moved[:, :LANES])
            return jnp.concatenate([head, moved[:, LANES:]], axis=1)
        moved = pltpu.roll(field, size_y - 1, 1)
        tail = jnp.where(lane == LANES - 1, edge_col, moved[:, half:])
        return jnp.concatenate([moved[:, :half], tail], axis=1)

    def first_lane(ref, field, z):
        return pltpu.roll(ref[...], lax.rem(2 * LANES - (field * depth + z), LANES), 1)

    def last_lane(ref, field, z):
        return pltpu.roll(ref[...], lax.rem(2 * LANES - 1 - (field * depth + z), LANES), 1)

    bottom, top = 0, depth - 1

    def stress_layer(z, up_ref, dn_ref, lt_ref, rt_ref):
        is_bottom, is_top = isinstance(z, int) and z == bottom, isinstance(z, int) and z == top
        vx, vy, vz = v[0, z], v[1, z], v[2, z]
        zz = vz if is_bottom else vz - v[2, z - 1]
        zy = -vy if is_top else v[1, z + 1] - vy
        zx = -vx if is_top else v[0, z + 1] - vx
        if up_ref is None:
            vx_up = vy_dn = vz_dn = vy_lt = vx_rt = vz_rt = 0.0
        else:
            vx_up = up_ref[pl.ds(z, 1), :]
            vy_dn, vz_dn = dn_ref[pl.ds(depth + z, 1), :], dn_ref[pl.ds(2 * depth + z, 1), :]
            vy_lt = first_lane(lt_ref, 1, z)
            vx_rt, vz_rt = last_lane(rt_ref, 0, z), last_lane(rt_ref, 2, z)
        xx = vx - along_x(vx, 1, vx_up)
        yy = vy - along_y(vy, 1, vy_lt)
        yz = zy + (along_y(vz, -1, vz_rt) - vz)
        xz = zx + (along_x(vz, -1, vz_dn) - vz)
        xy = (along_y(vx, -1, vx_rt) - vx) + (
            along_x(vy, -1, vy_dn) - vy
        )
        s[XX, z] += coef[C11, z] * xx + coef[C12, z] * yy + coef[C13, z] * zz
        s[YY, z] += coef[C12, z] * xx + coef[C22, z] * yy + coef[C23, z] * zz
        s[ZZ, z] += coef[C13, z] * xx + coef[C23, z] * yy + coef[C33, z] * zz
        s[YZ, z] += coef[C44, z] * yz
        s[XZ, z] += coef[C55, z] * xz
        s[XY, z] += coef[C66, z] * xy

    def velocity_layer(z, comps=(0, 1, 2)):
        is_bottom, is_top = isinstance(z, int) and z == bottom, isinstance(z, int) and z == top
        sxx, syy, szz = s[XX, z], s[YY, z], s[ZZ, z]
        syz, sxz, sxy = s[YZ, z], s[XZ, z], s[XY, z]
        b = coef[BUOY, z]
        if 0 in comps:
            v[0, z] += b * (
                (along_x(sxx, -1, halo_row[0, pl.ds(z, 1), :]) - sxx)
                + (sxy - along_y(sxy, 1, first_lane(halo_col.at[1], 0, z)))
                + (sxz if is_bottom else sxz - s[XZ, z - 1])
            )
        if 1 in comps:
            v[1, z] += b * (
                (sxy - along_x(sxy, 1, halo_row[1, pl.ds(z, 1), :]))
                + (along_y(syy, -1, last_lane(halo_col.at[0], 0, z)) - syy)
                + (syz if is_bottom else syz - s[YZ, z - 1])
            )
        if 2 in comps:
            v[2, z] += b * (
                (sxz - along_x(sxz, 1, halo_row[2, pl.ds(z, 1), :]))
                + (syz - along_y(syz, 1, first_lane(halo_col.at[2], 0, z)))
                + (-szz if is_top else s[ZZ, z + 1] - szz)
            )

    wide = (depth, size_y)
    wide_lane = iota(wide, 1)
    wide_z = iota(wide, 0)

    def below_z(f):
        return jnp.where(wide_z == 0, 0.0, pltpu.roll(f, 1, 0))

    def above_z(f):
        return jnp.where(wide_z == depth - 1, 0.0, pltpu.roll(f, depth - 1, 0))

    def lane_below_z(f):
        return jnp.where(lane == 0, 0.0, pltpu.roll(f, 1, 1))

    def lane_above_z(f):
        return jnp.where(lane == depth - 1, 0.0, pltpu.roll(f, LANES - 1, 1))

    def to_lanes(corner, at):
        col = jnp.broadcast_to(corner[:, at : at + 1], (depth, LANES))
        here = iota((depth, LANES), 0) == iota((depth, LANES), 1)
        return jnp.sum(jnp.where(here, col, 0.0), axis=0, keepdims=True)

    def lanes_of(ref, field):
        if field == 0:
            return ref[...]
        return pltpu.roll(ref[...], LANES - field * depth, 1)

    narrow_row = iota((size_x, LANES), 0)

    def halo_stress(up_ref, dn_ref, lt_ref, rt_ref, cup, cdn, my_up, my_dn, my_lt, my_rt):
        def rows(ref, k):
            return ref[k * depth : (k + 1) * depth, :]

        vx, vy, vz = rows(dn_ref, 0), rows(dn_ref, 1), rows(dn_ref, 2)
        corner = jnp.broadcast_to(cdn[:, LANES - 1 : LANES], wide)
        vy_back = jnp.where(wide_lane == 0, corner, pltpu.roll(vy, 1, 1))
        halo_row[0] += (
            hcoef_row[0] * (vx - rows(my_dn, 0))
            + hcoef_row[1] * (vy - vy_back)
            + hcoef_row[2] * (vz - below_z(vz))
        )
        vx, vy, vz = rows(up_ref, 0), rows(up_ref, 1), rows(up_ref, 2)
        corner = jnp.broadcast_to(cup[:, 0:1], wide)
        vx_next = jnp.where(wide_lane == size_y - 1, corner, pltpu.roll(vx, size_y - 1, 1))
        halo_row[1] += hcoef_row[3] * ((vx_next - vx) + (rows(my_up, 1) - vy))
        halo_row[2] += hcoef_row[4] * ((above_z(vx) - vx) + (rows(my_up, 2) - vz))
        vx, vy, vz = lanes_of(rt_ref, 0), lanes_of(rt_ref, 1), lanes_of(rt_ref, 2)
        vx_back = jnp.where(narrow_row == 0, to_lanes(cup, 0), pltpu.roll(vx, 1, 0))
        halo_col[0] += (
            hcoef_col[0] * (vx - vx_back)
            + hcoef_col[1] * (vy - lanes_of(my_rt, 1))
            + hcoef_col[2] * (vz - lane_below_z(vz))
        )
        vx, vy, vz = lanes_of(lt_ref, 0), lanes_of(lt_ref, 1), lanes_of(lt_ref, 2)
        vy_next = jnp.where(
            narrow_row == size_x - 1, to_lanes(cdn, LANES - 1), pltpu.roll(vy, size_x - 1, 0)
        )
        halo_col[1] += hcoef_col[3] * ((lanes_of(my_lt, 0) - vx) + (vy_next - vy))
        halo_col[2] += hcoef_col[4] * ((lane_above_z(vy) - vy) + (lanes_of(my_lt, 2) - vz))

    def stress_inside(z, _):
        stress_layer(z, None, None, None, None)
        return 0

    stress_inside(bottom, 0)
    lax.fori_loop(bottom + 1, top, stress_inside, 0)
    stress_inside(top, 0)

    wait_all(gathered, (n_p - 1) * per, group_recv, 0)
    rows = gathered[...]
    pick = pick_out[...]
    routes = sum(dot(pick, part) for part in split(rows))
    early, late = routes[: n_z * 8], routes[n_z * 8 :]
    low_all = iota((n_z * 8, LANES), 1) < 64
    force0 = jnp.where(low_all, early, pltpu.roll(late, 64, 1))
    force1 = jnp.where(low_all, pltpu.roll(early, 64, 1), late)
    for k in range(n_z):
        send2[k, 0:8, :] = force0[k * 8 : (k + 1) * 8]
        send2[k, 8:16, :] = force1[k * 8 : (k + 1) * 8]
    for i in z_order:
        send(send2.at[xor(my_z, i)], routed2.at[my_z], z_partner(i), 1).start()
    routed2[my_z] = send2[my_z]

    at_x0 = aux_t[:, 1:2] == 0.0
    at_y0 = aux_t[:, 2:3] == 0.0
    along_row = jnp.where(at_x0, rows, pltpu.roll(rows, LANES - PATCH * reach, 1))
    along_col = jnp.where(at_y0, rows, pltpu.roll(rows, LANES - reach, 1))
    in_row = jnp.logical_and(off_y[...] >= 0, off_y[...] < PATCH)
    at = jnp.where(in_row, off_y[...], 0)
    parts = [
        jnp.take_along_axis(along_row, at[:, k : k + LANES], axis=1)
        for k in range(0, size_y, LANES)
    ]
    row_line = jnp.where(in_row, jnp.concatenate(parts, axis=1), 0.0)
    in_col = jnp.logical_and(off_x[...] >= 0, off_x[...] < PATCH)
    at = jnp.where(in_col, off_x[...] * PATCH, 0)
    col_line = jnp.where(in_col, jnp.take_along_axis(along_col, at, axis=1), 0.0)
    lines = jnp.concatenate([row_line, col_line], axis=1)
    pick = pick_edge[...]
    lines = sum(dot(pick, part) for part in split(lines))
    send3[...] = jnp.where(
        side < 2, lines[:, :LANES], jnp.where(side < 4, lines[:, LANES:size_y], lines[:, size_y:])
    )
    for i in z_order:
        send(block(send3, xor(my_z, i), 8), block(routed3, my_z, 8), z_partner(i), 2).start()
    own = pl.ds(pl.multiple_of(my_z * 8, 8), 8)
    routed3[own, :] = send3[own, :]

    arrive1()
    kind = from_dn[4 * depth : 5 * depth, :]
    inside = has_dn.astype(F32)
    for k, index in enumerate((C11, C12, C13)):
        hcoef_row[k] = table(kind, index) * inside
    kind = from_up[5 * depth : 6 * depth, :]
    inside = has_up.astype(F32)
    for k, index in enumerate((C66, C55)):
        hcoef_row[3 + k] = table(kind, index) * inside
    kind = lanes_of(from_rt, 4)
    inside = has_rt.astype(F32)
    for k, index in enumerate((C12, C22, C23)):
        hcoef_col[k] = table(kind, index) * inside
    kind = lanes_of(from_lt, 5)
    inside = has_lt.astype(F32)
    for k, index in enumerate((C66, C44)):
        hcoef_col[3 + k] = table(kind, index) * inside
    halo_row[0] = from_dn[3 * depth : 4 * depth, :]
    halo_row[1] = from_up[3 * depth : 4 * depth, :]
    halo_row[2] = from_up[4 * depth : 5 * depth, :]
    halo_col[0] = lanes_of(from_rt, 3)
    halo_col[1] = lanes_of(from_lt, 3)
    halo_col[2] = lanes_of(from_lt, 4)

    def velocity_body(z, _):
        velocity_layer(z)
        return 0

    last_x = size_x - 1
    for z in range(depth):
        vx_up = from_up[z : z + 1, :]
        vy_dn, vz_dn = (from_dn[k * depth + z : k * depth + z + 1, :] for k in (1, 2))
        for comp, index in ((XX, C11), (YY, C12), (ZZ, C13)):
            s[comp, z, 0:1, :] -= coef[index, z, 0:1, :] * vx_up
        s[XZ, z, last_x:, :] += coef[C55, z, last_x:, :] * vz_dn
        s[XY, z, last_x:, :] += coef[C66, z, last_x:, :] * vy_dn
        vy_lt = jnp.where(lane == 0, first_lane(from_lt, 1, z), 0.0)
        for comp, index in ((XX, C12), (YY, C22), (ZZ, C23)):
            s[comp, z, :, :LANES] -= coef[index, z, :, :LANES] * vy_lt
        vx_rt, vz_rt = (
            jnp.where(lane == LANES - 1, last_lane(from_rt, k, z), 0.0) for k in (0, 2)
        )
        s[YZ, z, :, half:] += coef[C44, z, :, half:] * vz_rt
        s[XY, z, :, half:] += coef[C66, z, :, half:] * vx_rt
    halo_stress(
        from_up, from_dn, from_lt, from_rt, corner_up, corner_dn, to_up, to_dn, to_lt, to_rt
    )
    velocity_layer(bottom)
    lax.fori_loop(bottom + 1, top, velocity_body, 0)
    velocity_layer(top)

    pack_rows(vto_dn, size_x - 1, v_rows)
    pack_rows(vto_up, 0, v_rows)
    pack_cols(vto_rt, size_y - 1, v_cols)
    pack_cols(vto_lt, 0, v_cols)
    start2()

    def in_slot(t):
        return slot_x[t : t + 1, :] == x_ids

    wait_all(routed2, n_z - 1, group_recv, 1)
    force = routed2[0]
    for k in range(1, n_z):
        force = force + routed2[k]
    wide_force = jnp.concatenate(
        [
            jnp.concatenate(
                [jnp.where(in_slot(t), f[t : t + 1, :], 0.0) for t in range(8)], axis=1
            )
            for f in (force[0:8], force[8:16])
        ],
        axis=0,
    )
    got = dot(jnp.concatenate(split(wide_force), axis=0), onehot_y[...], ((1,), (1,)))
    got = got[: 2 * size_x] + got[2 * size_x :]
    plane[...] = coef[BUOY, top] * got[size_x:]
    top0 = v[2, top] + coef[BUOY, top] * got[:size_x]
    v[2, top] = top0

    def sample(values, step):
        got = dot(jnp.concatenate(split(values), axis=0), onehot_y[...])
        got = got[:size_x] + got[size_x:]
        for t in range(8):
            chosen = jnp.where(in_slot(t), got[:, t * LANES : (t + 1) * LANES], 0.0)
            at = step * 8 + t
            rec_send[at : at + 1, :] = jnp.sum(chosen, axis=0, keepdims=True)

    sample(top0, 0)
    wait_all(routed3, (n_z - 1) * 8, group_recv, 2)
    lines = routed3[0:8, :]
    for k in range(1, n_z):
        lines = lines + routed3[k * 8 : (k + 1) * 8, :]
    top_row = 2 * depth + top
    arrive2()
    leave2()

    def buoyancy(kind):
        return table(kind, BUOY)

    wide_line = jnp.concatenate([lines[0:2], lines[2:4]], axis=1)
    kind = from_dn[4 * depth + top : 4 * depth + top + 1, :]
    vfrom_dn[top_row : top_row + 1, :] += buoyancy(kind) * wide_line[0:1]
    kind = from_up[5 * depth + top : 5 * depth + top + 1, :]
    vfrom_up[top_row : top_row + 1, :] += buoyancy(kind) * wide_line[1:2]
    diagonal = iota((size_x, LANES), 0) == lane

    def upright(line):
        return jnp.sum(jnp.where(diagonal, line, 0.0), axis=1, keepdims=True)

    kind = pltpu.roll(from_rt[...], (top_row - 4 * depth - top) % LANES, 1)
    vfrom_rt[...] += jnp.where(lane == top_row, buoyancy(kind) * upright(lines[4:5]), 0.0)
    kind = pltpu.roll(from_lt[...], (top_row - 5 * depth - top) % LANES, 1)
    vfrom_lt[...] += jnp.where(lane == top_row, buoyancy(kind) * upright(lines[5:6]), 0.0)
    vto_up[top_row : top_row + 1, :] = v[2, top, 0:1, :]
    vto_lt[...] = jnp.where(
        lane == top_row, pltpu.roll(v[2, top, :, :LANES], top_row, 1), vto_lt[...]
    )
    stress_layer(top, vfrom_up, vfrom_dn, vfrom_lt, vfrom_rt)
    halo_stress(
        vfrom_up,
        vfrom_dn,
        vfrom_lt,
        vfrom_rt,
        vcorner_up,
        vcorner_dn,
        vto_up,
        vto_dn,
        vto_lt,
        vto_rt,
    )
    velocity_layer(top, (2,))
    top1 = v[2, top] + plane[...]
    v[2, top] = top1

    sample(top1, 1)
    for i in z_order:
        send(rec_send, rec_rows.at[my_z], z_partner(i), 3).start()
    rec_rows[my_z] = rec_send[...]

    pick = pick_back[...]
    wait_all(rec_rows, n_z - 1, group_recv, 3)
    early = rec_rows[:, 0:8, :].reshape(n_z * 8, LANES)
    late = rec_rows[:, 8:16, :].reshape(n_z * 8, LANES)
    both = jnp.concatenate(
        [
            jnp.where(low_all, early, pltpu.roll(late, 64, 1)),
            jnp.where(low_all, pltpu.roll(early, 64, 1), late),
        ],
        axis=0,
    )
    back = sum(dot(pick, part) for part in split(both))
    rec_back[...] = back
    for i in p_order:
        send(block(rec_back, xor(my_p, i), per), block(rec_got, my_p, per), p_partner(i), 4).start()
    mine = pl.ds(pl.multiple_of(my_p * per, per), per)
    rec_got[mine, :] = rec_back[mine, :]
    def stress_second(z, _):
        stress_layer(z, vfrom_up, vfrom_dn, vfrom_lt, vfrom_rt)
        return 0

    stress_second(bottom, 0)
    lax.fori_loop(bottom + 1, top, stress_second, 0)
    velocity_layer(bottom)
    lax.fori_loop(bottom + 1, top, velocity_body, 0)
    velocity_layer(top, (0, 1))

    leave1()
    wait_all(gathered, (n_p - 1) * per, group_send, 0)
    wait_all(routed2, n_z - 1, group_send, 1)
    wait_all(routed3, (n_z - 1) * 8, group_send, 2)
    wait_all(rec_rows, n_z - 1, group_send, 3)
    wait_all(rec_got, (n_p - 1) * per, group_recv, 4)
    tile = max(per, 8)
    parts = [rec_got[i * tile : (i + 1) * tile, :] for i in range(n_p * per // tile)]
    while len(parts) > 1:
        parts = [a + b for a, b in zip(parts[::2], parts[1::2])]
    out = parts[0][:per]
    for i in range(1, tile // per):
        out = out + parts[0][i * per : (i + 1) * per]
    rec_out[...] = out

    wait_all(rec_got, (n_p - 1) * per, group_send, 4)


def hand_over(v, s, rec, vel_out, str_out, rec_out, sem):
    pairs = [(v, vel_out), (s, str_out), (rec, rec_out)]
    copies = [pltpu.make_async_copy(a, b, sem.at[i]) for i, (a, b) in enumerate(pairs)]
    for copy in copies:
        copy.start()
    for copy in copies:
        copy.wait()


def solution(mesh):
    n_chord, n_span = mesh.shape["chord"], mesh.shape["span"]

    def local(velocity, stress, material, moduli, drive, owner, cells):
        _, depth, size_x, size_y = velocity.shape
        per = drive.shape[0]

        def mem(*shape):
            return pltpu.VMEM(shape, F32)

        def edges(rows_dn, rows_up):
            return [
                mem(rows_dn * depth, size_y),
                mem(rows_up * depth, size_y),
                mem(size_x, LANES),
                mem(size_x, LANES),
            ]

        layer = (size_x, size_y)
        vmem = pl.BlockSpec(memory_space=pltpu.VMEM)
        slots = SPLIT_Z * SLOTS
        n_p = n_chord * SPLIT_X_HI * SPLIT_CORE
        inputs = (velocity, stress, material, moduli, drive, owner.reshape(-1, LANES), cells.T)
        state = pl.pallas_call(
            functools.partial(kernel, n_chord, n_span),
            out_shape=(
                jax.ShapeDtypeStruct(velocity.shape, F32),
                jax.ShapeDtypeStruct(stress.shape, F32),
                jax.ShapeDtypeStruct(drive.shape, F32),
            ),
            in_specs=[pl.BlockSpec(memory_space=pltpu.HBM)] * 7,
            out_specs=(vmem, vmem, vmem),
            scratch_shapes=[
                pltpu.VMEM((depth, *layer), jnp.int32),
                pltpu.SMEM(moduli.shape, F32),
                mem(*drive.shape),
                pltpu.VMEM((owner.size // LANES, LANES), jnp.int32),
                pltpu.VMEM((8, owner.size), jnp.int32),
                mem(10, depth, *layer),
                pltpu.VMEM((size_y, 8 * LANES), BF16),
                mem(8, LANES),
                mem(8, LANES),
                mem(*layer),
                mem(owner.size // LANES * SPLIT_Z, LANES),
                mem(slots, LANES),
                pltpu.VMEM((slots, LANES), BF16),
                pltpu.VMEM((LANES, slots), BF16),
                pltpu.VMEM((slots // 2, LANES), BF16),
                mem(n_p * per, LANES),
                mem(SPLIT_Z, 16, LANES),
                mem(SPLIT_Z, 16, LANES),
                mem(slots // 2, LANES),
                mem(slots // 2, LANES),
                mem(SLOTS, LANES),
                mem(SPLIT_Z, SLOTS, LANES),
                mem(n_p * per, LANES),
                mem(n_p * per, LANES),
                *edges(6, 5),
                mem(6 * depth, size_y),
                mem(5 * depth, size_y),
                mem(size_x, LANES),
                mem(size_x, LANES),
                mem(depth, LANES),
                mem(depth, LANES),
                *edges(3, 3),
                *edges(3, 3),
                mem(depth, LANES),
                mem(depth, LANES),
                mem(LANES, LANES),
                pltpu.VMEM((LANES, size_y), jnp.int32),
                pltpu.VMEM((LANES, LANES), jnp.int32),
                mem(SPLIT_Z * 8, LANES),
                mem(3, depth, size_y),
                mem(3, size_x, LANES),
                mem(5, depth, size_y),
                mem(5, size_x, LANES),
                pltpu.SemaphoreType.DMA((7,)),
                pltpu.SemaphoreType.DMA((5,)),
                pltpu.SemaphoreType.DMA((5,)),
                pltpu.SemaphoreType.DMA((12,)),
                pltpu.SemaphoreType.DMA((12,)),
            ],
            compiler_params=pltpu.CompilerParams(
                collective_id=0, has_side_effects=True, vmem_limit_bytes=48 * 1024 * 1024
            ),
        )(*(pltpu.with_memory_space_constraint(x, pltpu.HBM) for x in inputs))
        hbm = pl.BlockSpec(memory_space=pltpu.HBM)
        return pl.pallas_call(
            hand_over,
            out_shape=tuple(jax.ShapeDtypeStruct(x.shape, x.dtype) for x in state),
            in_specs=[pl.BlockSpec(memory_space=pl.ANY)] * 3,
            out_specs=(hbm, hbm, hbm),
            scratch_shapes=[pltpu.SemaphoreType.DMA((3,))],
        )(*(pltpu.with_memory_space_constraint(x, pltpu.VMEM) for x in state))

    in_specs = (
        P(None, None, "chord", "span"),
        P(None, None, "chord", "span"),
        P(None, "chord", "span"),
        P(),
        P(("chord", "span"), None),
        P(),
        P(),
    )
    out_specs = (
        P(None, None, "chord", "span"),
        P(None, None, "chord", "span"),
        P(("chord", "span"), None),
    )
    return jax.shard_map(local, mesh=mesh, in_specs=in_specs, out_specs=out_specs, check_vma=False)
```
